256 devices in a mesh: prow: 32 (over y, z), pcol: 8 (over x, core).
Axes of the slice: x: 4, y: 4, z: 8, core: 2. Of those that a mesh axis runs over, the one named last changes fastest.
Arguments:
- matrix: bfloat16 [3, 16384, 2, 4096], P(None, 'prow', None, 'pcol'), may hold values from -6 to 6
- pivots: int32 [2, 512], replicated, may hold values from 0 to 49151, as said below
- lower_inverse: bfloat16 [2, 512, 512], replicated, may hold values from -1 to 1, as said below
- upper_inverse: bfloat16 [2, 512, 512], replicated, may hold values from -1 to 1, as said below
Outputs:
- factored: bfloat16 [3, 16384, 2, 4096], P(None, 'prow', None, 'pcol')
The draws below stay inside these ranges and needn't reach their ends.
Inputs may be any that keep to these rules, and one draw needn't show every extreme that they name: For each panel s, pivots[s, i] is either s * 512 + i or a row of index (s + 1) * 512 or more; the entries of one panel are distinct. Each lower_inverse[s] is unit lower triangular. Each upper_inverse[s] is upper triangular with a positive diagonal.
All inputs are finite; a program needn't handle non-finite values.
Results may differ from the reference program's by a relative error of at most 0.008.
Values may be sent and summed in bfloat16 or wider, within the bound.
No kernel may reach another device: no remote copies, remote signals or barrier semaphores. Data moves between devices by JAX's collectives and lax.ppermute only.
A program may use at most 64 MiB of HBM per device.

```python
import math
import jax
import jax.numpy as jnp

PANEL = 512
ROW_BLOCKS = 3
COL_BLOCKS = 2
ROWS = 49152
COLS = 8192
N_PROW = 32
N_PCOL = 8


def draw_pivots(key, part):
    key = jax.random.fold_in(key, 7)
    offsets = jnp.arange(PANEL, dtype=jnp.int32)
    lists = []
    for panel_index in range(2):
        section_key = jax.random.fold_in(key, panel_index)
        pick_key, keep_key, spot_key = jax.random.split(section_key, 3)
        first_row = (panel_index + 1) * PANEL
        chosen = jax.random.permutation(pick_key, ROWS - 1 - first_row)[:PANEL].astype(jnp.int32) + first_row
        keeping = jax.random.randint(keep_key, (PANEL,), 0, 4) == 0
        if panel_index == 0:
            keeping = keeping | (offsets == 0)
        chosen = jnp.where(keeping, panel_index * PANEL + offsets, chosen)
        if panel_index == 0:
            spot = jax.random.randint(spot_key, (), 1, PANEL)
            chosen = jnp.where(offsets == spot, ROWS - 1, chosen)
        lists.append(chosen)
    return jnp.stack(lists).astype(jnp.int32)


def draw_lower_inverse(key, part):
    key = jax.random.fold_in(key, 23)
    noise = jnp.clip(jax.random.normal(key, (2, PANEL, PANEL), jnp.float32), -4.0, 4.0)
    row_ids = jnp.arange(PANEL)[:, None]
    col_ids = jnp.arange(PANEL)[None, :]
    scaled = noise * (0.5 / math.sqrt(PANEL))
    values = jnp.where(row_ids > col_ids, scaled, jnp.where(row_ids == col_ids, 1.0, 0.0))
    return values.astype(jnp.float32).astype(jnp.bfloat16)


def draw_upper_inverse(key, part):
    key = jax.random.fold_in(key, 31)
    diag_key, noise_key = jax.random.split(key)
    diagonal = jnp.exp(jax.random.uniform(diag_key, (2, PANEL), jnp.float32, math.log(0.5), math.log(2.0)))
    diagonal = diagonal / math.sqrt(PANEL)
    noise = jnp.clip(jax.random.normal(noise_key, (2, PANEL, PANEL), jnp.float32), -4.0, 4.0)
    row_ids = jnp.arange(PANEL)[:, None]
    col_ids = jnp.arange(PANEL)[None, :]
    scaled = noise * (0.7 / PANEL)
    values = jnp.where(row_ids < col_ids, scaled, jnp.where(row_ids == col_ids, diagonal[:, :, None], 0.0))
    return values.astype(jnp.float32).astype(jnp.bfloat16)


def level_of(stream_key, shape, cuts, smallest, high):
    def one(position, shards_of):
        heights = jax.random.uniform(jax.random.fold_in(jax.random.fold_in(stream_key, 6), position), (shards_of,), jnp.float32, smallest / len(cuts), high / len(cuts))
        return jnp.repeat(jnp.exp(heights), shape[position] // shards_of).reshape((-1,) + (1,) * (len(shape) - position - 1))

    factor_of = one(*cuts[0])
    for cut in cuts[1:]:
        factor_of = factor_of * one(*cut)
    return factor_of


def bell_draw(stream_key, extent, deviation, most, cuts=(), held_as=jnp.bfloat16):
    result = deviation * jax.random.normal(stream_key, extent, jnp.float32)
    if cuts:
        result = result * level_of(stream_key, extent, cuts, -0.22, 0.18)
    return jnp.clip(result, -most, most).astype(held_as)


def setup_inputs(seed: int = 0) -> dict:
    splits = jax.random.split(jax.random.key(seed), 5)
    matrix = bell_draw(splits[0], (ROW_BLOCKS, N_PROW * PANEL, COL_BLOCKS, N_PCOL * PANEL), 1.0, 6.0, ((1, 32), (3, 8)))
    pivots = draw_pivots(jax.random.fold_in(splits[4], 71), 0)
    lower_inverse = draw_lower_inverse(jax.random.fold_in(splits[4], 71), 0)
    upper_inverse = draw_upper_inverse(jax.random.fold_in(splits[4], 71), 0)
    return {"matrix": matrix, "pivots": pivots, "lower_inverse": lower_inverse, "upper_inverse": upper_inverse}


def reference(matrix, pivots, lower_inverse, upper_inverse):
    current = matrix.reshape(ROWS, COLS)
    offsets = jnp.arange(PANEL, dtype=jnp.int32)
    for panel_index in range(2):
        begin_at = panel_index * PANEL
        end_at = begin_at + PANEL
        targets = begin_at + offsets
        ordering = jnp.arange(ROWS, dtype=jnp.int32)
        ordering = ordering.at[targets].set(pivots[panel_index].astype(jnp.int32))
        ordering = ordering.at[pivots[panel_index].astype(jnp.int32)].set(targets)
        current = current[ordering]
        factors = jnp.dot(current[end_at:, begin_at:end_at], upper_inverse[panel_index],
                          preferred_element_type=jnp.float32).astype(jnp.bfloat16)
        new_row = jnp.dot(lower_inverse[panel_index], current[begin_at:end_at, end_at:],
                          preferred_element_type=jnp.float32).astype(jnp.bfloat16)
        pieces = []
        for column in range(end_at, COLS, PANEL):
            old_block = current[end_at:, column:column + PANEL].astype(jnp.float32)
            change = jnp.dot(factors, new_row[:, column - end_at:column - end_at + PANEL],
                             preferred_element_type=jnp.float32)
            pieces.append((old_block - change).astype(jnp.bfloat16))
        current = current.at[end_at:, end_at:].set(jnp.concatenate(pieces, axis=1))
        current = current.at[end_at:, begin_at:end_at].set(factors)
        current = current.at[begin_at:end_at, end_at:].set(new_row)
    return current.reshape(matrix.shape)
```

```python
import jax
import jax.numpy as jnp
from jax import lax
from jax.sharding import PartitionSpec as P

NY, NZ, NX, NC = 4, 8, 4, 2
N_HOMES = NY * NZ
PAIR_ROWS = 8
DEST_ROWS = 32
LINE_ROWS = 144
Z_ORDER = (0, 7, 1, 4, 6, 5, 2, 3)
Y_ORDER = (0, 3, 1, 2)


def shift_y(step, rows=range(NY), cols=range(NZ)):
    return [(y * NZ + z, (y + step) % NY * NZ + z) for y in rows for z in cols]


def shift_z(step, cols=range(NZ)):
    return [(y * NZ + z, y * NZ + (z + step) % NZ) for y in range(NY) for z in cols]


def move_x(pairs):
    return [(a * NC + core, b * NC + core) for a, b in pairs for core in range(NC)]


SWAP = [(x * NC + core, x * NC + 1 - core) for x in range(NX) for core in range(NC)]


def broadcast(value, axis, root):
    mine = lax.axis_index(axis) == root
    return lax.psum(jnp.where(mine, value, jnp.zeros_like(value)), axis)


def locate(pivot_list, panel, prow_size, prow_here):
    block_index = pivot_list // panel
    owned_rows = block_index % prow_size == prow_here
    local_row = block_index // prow_size * panel + pivot_list % panel
    return (owned_rows, local_row)


def general_steps(matrix, pivots, lower_inverse, upper_inverse):
    row_blocks = matrix.shape[0]
    panel = matrix.shape[1]
    col_blocks = matrix.shape[2]
    prow_size = lax.axis_size("prow")
    pcol_size = lax.axis_size("pcol")
    prow_here = lax.axis_index("prow")
    pcol_here = lax.axis_index("pcol")
    local_rows = row_blocks * panel
    local_cols = col_blocks * panel
    current = matrix.reshape(local_rows, local_cols)
    row_global = jnp.repeat(jnp.arange(row_blocks, dtype=jnp.int32) * prow_size + prow_here, panel)
    col_global = jnp.repeat(jnp.arange(col_blocks, dtype=jnp.int32) * pcol_size + pcol_here, panel)
    offsets = jnp.arange(panel, dtype=jnp.int32)
    bf_zero = jnp.zeros((), jnp.bfloat16)
    for panel_index in range(2):
        root_row = panel_index % prow_size
        diag_local = panel_index // prow_size * panel
        root_col = panel_index % pcol_size
        panel_local = panel_index // pcol_size * panel
        pivot_list = pivots[panel_index]
        owned_rows, local_row = locate(pivot_list, panel, prow_size, prow_here)
        safe_rows = jnp.where(owned_rows, local_row, 0)
        picked = jnp.where(owned_rows[:, None], current[safe_rows], bf_zero)
        is_root = prow_here == root_row
        previous = current[diag_local : diag_local + panel]
        right_cols = col_global > panel_index
        displaced = broadcast(previous, "prow", root_row)
        gathered = lax.psum(picked, "prow").astype(jnp.float32)
        pivot_block = gathered.astype(jnp.bfloat16)
        product = jnp.dot(
            lower_inverse[panel_index], pivot_block, preferred_element_type=jnp.float32
        ).astype(jnp.bfloat16)
        new_row = jnp.where(right_cols[None, :], product, pivot_block)
        moved_rows = owned_rows & (pivot_list != panel_index * panel + offsets)
        targets = jnp.where(moved_rows, local_row, local_rows)
        current = current.at[targets].set(displaced, mode="drop")
        below_mask = row_global > panel_index
        panel_part = current[:, panel_local : panel_local + panel]
        upper_block = upper_inverse[panel_index]

        def factor(columns):
            result = jnp.dot(columns, upper_block, preferred_element_type=jnp.float32).astype(
                jnp.bfloat16
            )
            return jnp.where(below_mask[:, None], result, jnp.zeros((), jnp.bfloat16))

        def nothing(columns):
            return jnp.zeros((local_rows, panel), jnp.bfloat16)

        factors = lax.cond(pcol_here == root_col, factor, nothing, panel_part)
        factors = broadcast(factors, "pcol", root_col)
        update_rows = jnp.where(right_cols[None, :], new_row, bf_zero)
        correction = jnp.dot(factors, update_rows, preferred_element_type=jnp.float32)
        updated = (current.astype(jnp.float32) - correction).astype(jnp.bfloat16)
        owner_col = pcol_here == root_col
        new_panel = jnp.where(
            owner_col & below_mask[:, None], factors, updated[:, panel_local : panel_local + panel]
        )
        updated = updated.at[:, panel_local : panel_local + panel].set(new_panel)
        row_block = jnp.where(is_root, new_row, updated[diag_local : diag_local + panel])
        current = updated.at[diag_local : diag_local + panel].set(row_block)
    return current.reshape(matrix.shape)


def count(mask, axis):
    return jnp.sum(mask.astype(jnp.int32), axis=axis)


def plan(pivots, panel, y, z, here):
    offsets = jnp.arange(panel, dtype=jnp.int32)
    first, second = pivots[0], pivots[1]
    same = first[:, None] == second[None, :]
    hit_second = jnp.any(same, axis=0)
    hit_first = jnp.any(same, axis=1)
    came_from = jnp.sum(jnp.where(same, offsets[:, None], 0), axis=0)
    source = jnp.stack([first, jnp.where(hit_second, came_from, second)])
    block = source // panel
    owner = block % N_HOMES
    local = block // N_HOMES * panel + source % panel
    equal = owner[:, :, None] == owner[:, None, :]
    before = offsets[:, None] < offsets[None, :]
    lesser = owner[:, :, None] < owner[:, None, :]
    within = count(equal & before, 1)
    rank = count(lesser, 1) + within
    shared = count(owner[0][:, None] == owner[1][None, :], 0)
    skip = jnp.stack([jnp.zeros_like(shared), (shared + N_HOMES - 1) // N_HOMES])
    slot = within // N_HOMES + skip
    home, entry = rank % N_HOMES, rank // N_HOMES
    overflow = jnp.any(slot >= PAIR_ROWS)
    at = jnp.where(owner == here, home * PAIR_ROWS + slot, -1).reshape(-1)
    deal = jnp.sum(
        jnp.where(
            jnp.arange(N_HOMES * PAIR_ROWS)[:, None] == at[None, :], local.reshape(-1)[None, :], 0
        ),
        axis=1,
    )
    per_home = panel // N_HOMES
    kept_at = jnp.where(home == here, entry, -1)
    keep = jnp.sum(
        jnp.where(
            jnp.arange(per_home)[None, :, None] == kept_at[:, None, :],
            (owner * PAIR_ROWS + slot)[:, None, :],
            0,
        ),
        axis=2,
    )
    z_place = jnp.zeros_like(home)
    for place, step in enumerate(Z_ORDER):
        z_place = jnp.where((home % NZ - z) % NZ == step, place, z_place)
    y_place = jnp.zeros_like(home)
    for place, step in enumerate(Y_ORDER):
        y_place = jnp.where((home // NZ - y) % NY == step, place, y_place)
    place = (y_place * NZ + z_place) * per_home + entry
    upper = panel + offsets
    taken = first[:, None] == upper[None, :]
    next_stop = jnp.sum(jnp.where(taken, second[None, :], 0), axis=1)
    inner = (first >= panel) & (first < 2 * panel)
    goal_first = jnp.where(
        inner,
        jnp.where(next_stop == first, -1, next_stop),
        jnp.where((first == offsets) | hit_first, -1, first),
    )
    goal_second = jnp.where(jnp.any(taken, axis=0) | (second == upper), -1, second)
    goal = jnp.stack([goal_first, goal_second])
    goal_block = goal // panel
    dest = jnp.where(goal < 0, -1, goal_block % N_HOMES)
    dest_local = goal_block // N_HOMES * panel + goal % panel
    line = jnp.where(goal < 0, -1, dest // NZ)
    line_rank = count((line[:, :, None] == line[:, None, :]) & before, 1)
    dest_rank = count((dest[:, :, None] == dest[:, None, :]) & before, 1)
    valid = goal >= 0
    overflow |= jnp.any(valid & ((line_rank >= LINE_ROWS) | (dest_rank >= DEST_ROWS)))
    mine = jnp.where(here % 2 == 0, 0, 1)
    line_m, line_rank_m = line[mine], line_rank[mine]
    send_at = jnp.where(line_m < 0, -1, line_m * LINE_ROWS + line_rank_m)
    send = jnp.sum(
        jnp.where(jnp.arange(NY * LINE_ROWS)[:, None] == send_at[None, :], offsets[None, :], 0), axis=1
    )
    dest_m, dest_rank_m = dest[mine], dest_rank[mine]
    pass_at = jnp.where(line_m == y, (dest_m % NZ - z) % NZ * DEST_ROWS + dest_rank_m, -1)
    passing = jnp.sum(
        jnp.where(jnp.arange(NZ * DEST_ROWS)[:, None] == pass_at[None, :], line_rank_m[None, :], 0), axis=1
    )
    land_at = jnp.where(dest == here, dest_rank, -1)
    land = (
        jnp.sum(
            jnp.where(
                jnp.arange(DEST_ROWS)[None, :, None] == land_at[:, None, :],
                dest_local[:, None, :] + 1,
                0,
            ),
            axis=2,
        )
        - 1
    )
    return deal, keep, place, send, passing, land, overflow


def per_device(matrix, pivots, lower_inverse, upper_inverse):
    row_blocks, panel, col_blocks, width = matrix.shape
    local_rows = row_blocks * panel
    bf16 = jnp.bfloat16
    here = lax.axis_index("prow")
    column = lax.axis_index("pcol")
    y, z = here // NZ, here % NZ
    x, core = column // NC, column % NC
    deal, keep, place, send, passing, land, overflow = plan(pivots, panel, y, z, here)
    rows = matrix.reshape(local_rows, col_blocks * width)

    def dot(a, b):
        return jnp.dot(a, b, preferred_element_type=jnp.float32)

    def narrow(value):
        return value.astype(bf16)

    own = [matrix[k, :, 0, :] for k in range(3)]
    got = [lax.ppermute(own[k], "pcol", move_x([(0, k + 1)])) for k in (0, 2, 1)]
    third = jnp.where(x == 1, got[0], jnp.where(x == 3, got[1], got[2]))
    up = lax.ppermute(third, "pcol", move_x([(1, 2), (2, 3)]))
    down = lax.ppermute(third, "pcol", move_x([(2, 1), (3, 2)]))
    across = lax.ppermute(third, "pcol", move_x([(1, 3), (3, 1)]))
    one = jnp.where(x == 0, own[0], jnp.where(x == 1, third, jnp.where(x == 2, up, across)))
    two = jnp.where(x == 0, own[1], jnp.where(x == 2, third, jnp.where(x == 1, down, up)))
    three = jnp.where(x == 0, own[2], jnp.where(x == 3, third, jnp.where(x == 2, down, across)))
    part = jnp.concatenate([one, two, three])
    other = lax.ppermute(part, "pcol", SWAP)
    panel_first = jnp.where(core == 0, part, other)
    panel_second = jnp.where(core == 0, other, part)

    dealt = lax.all_to_all(rows[deal], "prow", 0, 0, tiled=True)
    block = dealt[keep.reshape(-1)]
    from_lo = lax.ppermute(block, "prow", shift_z(1))
    from_hi = lax.ppermute(block, "prow", shift_z(-1))
    opposite = lax.ppermute(block, "prow", shift_z(4))
    two_lo = lax.ppermute(jnp.concatenate([block, from_lo]), "prow", shift_z(2))
    two_hi = lax.ppermute(jnp.concatenate([block, from_hi]), "prow", shift_z(-2))
    z_line = jnp.concatenate([block, from_lo, from_hi, opposite, two_lo, two_hi])
    per_home = panel // N_HOMES
    y_parts = [z_line] + [lax.ppermute(z_line, "prow", shift_y(s)) for s in (1, -1, 2)]

    leaving = rows[:panel][send].reshape(NY, LINE_ROWS, -1)
    arrived = [lax.ppermute(leaving[s], "prow", shift_y(s, [0], [0, 1])) for s in (1, 3, 2)]
    on_line = jnp.where(
        y == 0, leaving[0], jnp.where(y == 1, arrived[0], jnp.where(y == 3, arrived[1], arrived[2]))
    )
    spread = on_line[passing].reshape(NZ, DEST_ROWS, -1)
    landed = [spread[0]] + [
        lax.ppermute(spread[s], "prow", shift_z(s, [0, 1])) for s in range(1, NZ)
    ]
    landed = jnp.stack(landed)
    displaced = jnp.concatenate(
        [
            lax.dynamic_index_in_dim(landed, z, 0, False),
            lax.dynamic_index_in_dim(landed, (z - 1) % NZ, 0, False),
        ]
    )

    halves = z_line.reshape(NZ, 2, per_home, col_blocks * width)
    extra = jnp.where(core == 0, halves[:, 1, :, :width], halves[:, 0, :, :width]).reshape(-1, width)
    extra = jnp.concatenate([extra, displaced[:, :width]])
    sent = [lax.ppermute(extra, "pcol", move_x([(0, k)])) for k in (1, 3, 2)]
    extra = jnp.where(x == 0, extra, jnp.where(x == 1, sent[0], jnp.where(x == 3, sent[1], sent[2])))
    line_rows = NZ * per_home
    cross = extra[:line_rows]
    cross = jnp.concatenate(
        [cross] + [lax.ppermute(cross, "prow", shift_y(s)) for s in (1, -1, 2)] + [extra[line_rows:]]
    )
    cross_other = lax.ppermute(cross, "pcol", SWAP)
    from_first = jnp.where(core == 0, cross, cross_other)
    from_second = jnp.where(core == 0, cross_other, cross)
    lower_left = from_first[:panel]
    upper_right = from_second[:panel]
    displaced_first = from_first[panel:]
    displaced_second = from_second[panel:]

    order = jnp.arange(panel, dtype=jnp.int32)
    select = (place[:, :, None] == order[None, None, :]).astype(bf16)
    low_first = narrow(dot(lower_inverse[0], select[0]))
    low_second = narrow(dot(lower_inverse[1], select[1]))

    hits = jnp.arange(local_rows, dtype=jnp.int32)[:, None] == land.reshape(-1)[None, :]
    hit = jnp.any(hits, axis=1)[:, None]
    hits = hits.astype(bf16)
    current = jnp.where(hit, narrow(dot(hits, displaced)), rows)
    panel_first = jnp.where(hit, narrow(dot(hits, displaced_first)), panel_first)
    panel_second = jnp.where(hit, narrow(dot(hits, displaced_second)), panel_second)

    gathered = jnp.concatenate(y_parts).reshape(N_HOMES, 2, per_home, col_blocks * width)
    pivot_first = gathered[:, 0].reshape(panel, -1)
    pivot_second = gathered[:, 1].reshape(panel, -1)
    row_first = narrow(dot(low_first, pivot_first))
    corner = narrow(dot(low_first, upper_right))
    lower_factor = narrow(dot(lower_left, upper_inverse[0]))
    reduced = narrow(pivot_second.astype(jnp.float32) - dot(lower_factor, row_first))
    row_second = narrow(dot(low_second, reduced))
    factor_first = narrow(dot(panel_first, upper_inverse[0]))
    mid = narrow(panel_second.astype(jnp.float32) - dot(factor_first, corner))
    factor_second = narrow(dot(mid, upper_inverse[1]))
    factors = jnp.concatenate([factor_first, factor_second], axis=1)
    new_rows = jnp.concatenate([row_first, row_second], axis=0)
    updated = narrow(current.astype(jnp.float32) - dot(factors, new_rows))

    raw = jnp.where(
        here == 0, pivot_first[:, :width], jnp.where(column == 0, lower_factor, reduced[:, :width])
    )
    ordered = narrow(dot(jnp.where(here == 0, select[0], select[1]), raw))
    left = jnp.where(
        column == 0, factor_first, jnp.where(column == 1, factor_second, updated[:, :width])
    )
    right = updated[:, width:]
    top_left = jnp.where(
        here == 0,
        jnp.where(column == 0, ordered, row_first[:, :width]),
        jnp.where(
            here == 1, jnp.where(column <= 1, ordered, row_second[:, :width]), left[:panel]
        ),
    )
    top_right = jnp.where(
        here == 0, row_first[:, width:], jnp.where(here == 1, row_second[:, width:], right[:panel])
    )
    left = jnp.concatenate([top_left, left[panel:]])
    right = jnp.concatenate([top_right, right[panel:]])
    result = jnp.stack([left, right], axis=1).reshape(matrix.shape)
    return lax.cond(
        overflow,
        lambda a, *rest: general_steps(*rest),
        lambda a, *rest: a,
        result,
        matrix,
        pivots,
        lower_inverse,
        upper_inverse,
    )


def solution(mesh):
    return jax.shard_map(
        per_device,
        mesh=mesh,
        in_specs=(P(None, "prow", None, "pcol"), P(), P(), P()),
        out_specs=P(None, "prow", None, "pcol"),
        check_vma=False,
    )
```

```python
import functools

import jax
import jax.numpy as jnp
from jax import lax
from jax.experimental import pallas as pl
from jax.experimental.pallas import tpu as pltpu
from jax.sharding import PartitionSpec as P

NY, NZ, NX, NC = 4, 8, 4, 2
N_HOMES = NY * NZ
PAIR_ROWS = 8
DEST_ROWS = 32
LINE_ROWS = 144
Z_ORDER = (0, 7, 1, 4, 6, 5, 2, 3)
Y_ORDER = (0, 3, 1, 2)
MIB = 1 << 20


def shift_y(step, rows=range(NY), cols=range(NZ)):
    return [(y * NZ + z, (y + step) % NY * NZ + z) for y in rows for z in cols]


def shift_z(step, cols=range(NZ)):
    return [(y * NZ + z, y * NZ + (z + step) % NZ) for y in range(NY) for z in cols]


def move_x(pairs):
    return [(a * NC + core, b * NC + core) for a, b in pairs for core in range(NC)]


SWAP = [(x * NC + core, x * NC + 1 - core) for x in range(NX) for core in range(NC)]


def broadcast(value, axis, root):
    mine = lax.axis_index(axis) == root
    return lax.psum(jnp.where(mine, value, jnp.zeros_like(value)), axis)


def locate(pivot_list, panel, prow_size, prow_here):
    block_index = pivot_list // panel
    owned_rows = block_index % prow_size == prow_here
    local_row = block_index // prow_size * panel + pivot_list % panel
    return (owned_rows, local_row)


def general_steps(matrix, pivots, lower_inverse, upper_inverse):
    row_blocks = matrix.shape[0]
    panel = matrix.shape[1]
    col_blocks = matrix.shape[2]
    prow_size = lax.axis_size("prow")
    pcol_size = lax.axis_size("pcol")
    prow_here = lax.axis_index("prow")
    pcol_here = lax.axis_index("pcol")
    local_rows = row_blocks * panel
    local_cols = col_blocks * panel
    current = matrix.reshape(local_rows, local_cols)
    row_global = jnp.repeat(jnp.arange(row_blocks, dtype=jnp.int32) * prow_size + prow_here, panel)
    col_global = jnp.repeat(jnp.arange(col_blocks, dtype=jnp.int32) * pcol_size + pcol_here, panel)
    offsets = jnp.arange(panel, dtype=jnp.int32)
    bf_zero = jnp.zeros((), jnp.bfloat16)
    def one_panel(panel_index, current):
        root_row, root_col = panel_index, panel_index
        diag_local = panel_local = 0
        pivot_list = pivots[panel_index]
        owned_rows, local_row = locate(pivot_list, panel, prow_size, prow_here)
        safe_rows = jnp.where(owned_rows, local_row, 0)
        picked = jnp.where(owned_rows[:, None], current[safe_rows], bf_zero)
        is_root = prow_here == root_row
        previous = current[diag_local : diag_local + panel]
        right_cols = col_global > panel_index
        displaced = broadcast(previous, "prow", root_row)
        gathered = lax.psum(picked, "prow").astype(jnp.float32)
        pivot_block = gathered.astype(jnp.bfloat16)
        product = jnp.dot(
            lower_inverse[panel_index], pivot_block, preferred_element_type=jnp.float32
        ).astype(jnp.bfloat16)
        new_row = jnp.where(right_cols[None, :], product, pivot_block)
        moved_rows = owned_rows & (pivot_list != panel_index * panel + offsets)
        targets = jnp.where(moved_rows, local_row, local_rows)
        current = current.at[targets].set(displaced, mode="drop")
        below_mask = row_global > panel_index
        panel_part = current[:, panel_local : panel_local + panel]
        upper_block = upper_inverse[panel_index]

        def factor(columns):
            result = jnp.dot(columns, upper_block, preferred_element_type=jnp.float32).astype(
                jnp.bfloat16
            )
            return jnp.where(below_mask[:, None], result, jnp.zeros((), jnp.bfloat16))

        def nothing(columns):
            return jnp.zeros((local_rows, panel), jnp.bfloat16)

        factors = lax.cond(pcol_here == root_col, factor, nothing, panel_part)
        factors = broadcast(factors, "pcol", root_col)
        update_rows = jnp.where(right_cols[None, :], new_row, bf_zero)
        correction = jnp.dot(factors, update_rows, preferred_element_type=jnp.float32)
        updated = (current.astype(jnp.float32) - correction).astype(jnp.bfloat16)
        owner_col = pcol_here == root_col
        new_panel = jnp.where(
            owner_col & below_mask[:, None], factors, updated[:, panel_local : panel_local + panel]
        )
        updated = updated.at[:, panel_local : panel_local + panel].set(new_panel)
        row_block = jnp.where(is_root, new_row, updated[diag_local : diag_local + panel])
        return updated.at[diag_local : diag_local + panel].set(row_block)

    current = lax.fori_loop(0, 2, one_panel, current)
    return current.reshape(matrix.shape)


def dot(a, b):
    return jnp.dot(a, b, preferred_element_type=jnp.float32)


def narrow(value):
    return value.astype(jnp.bfloat16)


def iota(shape, axis):
    return lax.broadcasted_iota(jnp.int32, shape, axis)


def total(mask_or_value, axis):
    return jnp.sum(mask_or_value, axis=axis, keepdims=True).astype(jnp.int32)


def pick(mask, value):
    return jnp.where(mask, value, 0).astype(jnp.float32)


def split_rows(row, panel):
    shift = panel.bit_length() - 1
    block = row >> shift
    return block & (N_HOMES - 1), ((block >> 5) << shift) + (row & (panel - 1))


def place_of(step, order):
    result = jnp.zeros_like(step)
    for place, value in enumerate(order):
        result = jnp.where(step == value, place, result)
    return result


def deal_kernel(panel, pos_ref, across_ref, down_ref, rows_ref, picks_ref, keep_ref, place_ref, flag_ref):
    here = pos_ref[0]
    y, z = here >> 3, here & 7
    first_r, second_r = across_ref[0:1, :], across_ref[1:2, :]
    first_c, second_c = down_ref[:, 0:1], down_ref[:, 1:2]
    square = (panel, panel)
    number_c, number_r = iota(square, 0), iota(square, 1)
    came_r = total(pick(first_c == second_r, number_c + 1), 0)
    came_c = total(pick(second_c == first_r, number_r + 1), 1)
    source_r = [first_r, jnp.where(came_r > 0, came_r - 1, second_r)]
    source_c = [first_c, jnp.where(came_c > 0, came_c - 1, second_c)]
    owners_r, locals_r = zip(*[split_rows(s, panel) for s in source_r])
    owners_c = [split_rows(s, panel)[0] for s in source_c]
    before = number_c < number_r
    slots, homes, entries = [], [], []
    for s in range(2):
        counts = total(
            pick((owners_c[s] == owners_r[s]) & before, 1025) + pick(owners_c[s] < owners_r[s], 1), 0
        )
        within, rank = counts >> 10, counts & 1023
        slot = within >> 5
        if s == 1:
            shared = total(pick(owners_c[0] == owners_r[1], 1), 0)
            slot = slot + ((shared + N_HOMES - 1) >> 5)
        slots.append(slot)
        homes.append(rank & (N_HOMES - 1))
        entries.append(rank >> 5)
    flag_ref[...] = jnp.maximum(slots[0], slots[1])
    deal = jnp.zeros((N_HOMES * PAIR_ROWS, 1), jnp.int32)
    position = iota((N_HOMES * PAIR_ROWS, panel), 0)
    per_home = panel // N_HOMES
    for s in range(2):
        at = jnp.where(owners_r[s] == here, homes[s] * PAIR_ROWS + slots[s], -1)
        deal = deal + total(pick(position == at, locals_r[s]), 1)
        kept_at = jnp.where(homes[s] == here, entries[s], -1)
        keep_ref[s * per_home : (s + 1) * per_home, :] = total(
            pick(iota((per_home, panel), 0) == kept_at, owners_r[s] * PAIR_ROWS + slots[s]), 1
        )
        z_place = place_of((homes[s] - z) & (NZ - 1), Z_ORDER)
        y_place = place_of(((homes[s] >> 3) - y) & (NY - 1), Y_ORDER)
        place_ref[s : s + 1, :] = (y_place * NZ + z_place) * per_home + entries[s]
    n_rows = rows_ref.shape[0]
    choose = jnp.where(iota((N_HOMES * PAIR_ROWS, n_rows), 1) == deal, 1.0, 0.0)
    picks_ref[...] = narrow(dot(narrow(choose), rows_ref[...]))


def leave_kernel(
    panel, pos_ref, across_ref, down_ref, rows_ref, place_ref, lower_ref, leaving_ref, passing_ref, land_ref, flag_ref, low_ref
):
    here = pos_ref[0]
    y, z = here >> 3, here & 7
    odd = (here & 1) == 1
    first_r, second_r = across_ref[0:1, :], across_ref[1:2, :]
    first_c, second_c = down_ref[:, 0:1], down_ref[:, 1:2]
    square = (panel, panel)
    number_c, number_r = iota(square, 0), iota(square, 1)
    big = 1 << 20
    seen_r = total(pick(second_c == first_r, big) + pick(number_c + panel == first_r, second_c), 0)
    seen_c = total(pick(first_c == second_r, big) + pick(first_c == number_r + panel, second_r), 1)
    used_r = total(pick(first_c == number_r + panel, 1), 0)
    used_c = total(pick(number_c + panel == first_r, 1), 1)

    def goals(first, second, seen, used, number):
        inner = (first >= panel) & (first < 2 * panel)
        stop = seen & (big - 1)
        goal_first = jnp.where(
            inner,
            jnp.where(stop == first, -1, stop),
            jnp.where((first == number) | (seen >= big), -1, first),
        )
        goal_second = jnp.where((used > 0) | (second == number + panel), -1, second)
        return goal_first, goal_second

    goal_r = goals(first_r, second_r, seen_r, used_r, number_r[0:1, :])
    goal_c = goals(first_c, second_c, seen_c, used_c, number_c[:, 0:1])
    before = number_c < number_r
    lines, line_ranks, dests, dest_ranks = [], [], [], []
    worst = jnp.zeros((1, panel), jnp.int32)
    for s in range(2):
        dest_r, local_r = split_rows(goal_r[s], panel)
        dest_r = jnp.where(goal_r[s] < 0, -1, dest_r)
        dest_c = jnp.where(goal_c[s] < 0, -1, split_rows(goal_c[s], panel)[0])
        line_r, line_c = dest_r >> 3, dest_c >> 3
        counts = total(
            pick((dest_c == dest_r) & before, 1024) + pick((line_c == line_r) & before, 1), 0
        )
        line_rank, dest_rank = counts & 1023, counts >> 10
        worst = jnp.maximum(
            worst,
            jnp.where(
                (dest_r >= 0) & ((line_rank >= LINE_ROWS) | (dest_rank >= DEST_ROWS)), 1, 0
            ),
        )
        land_at = jnp.where(dest_r == here, dest_rank, -1)
        land_ref[s * DEST_ROWS : (s + 1) * DEST_ROWS, :] = (
            total(pick(iota((DEST_ROWS, panel), 0) == land_at, local_r + 1), 1) - 1
        )
        lines.append(line_r)
        line_ranks.append(line_rank)
        dests.append(dest_r)
        dest_ranks.append(dest_rank)
    flag_ref[...] = worst
    line = jnp.where(odd, lines[1], lines[0])
    line_rank = jnp.where(odd, line_ranks[1], line_ranks[0])
    dest = jnp.where(odd, dests[1], dests[0])
    dest_rank = jnp.where(odd, dest_ranks[1], dest_ranks[0])
    send_at = jnp.where(line < 0, -1, line * LINE_ROWS + line_rank)
    choose = jnp.where(iota((NY * LINE_ROWS, panel), 0) == send_at, 1.0, 0.0)
    leaving_ref[...] = narrow(dot(narrow(choose), rows_ref[...]))
    pass_at = jnp.where(line == y, ((dest - z) & (NZ - 1)) * DEST_ROWS + dest_rank, -1)
    passing_ref[...] = total(
        pick(iota((NZ * DEST_ROWS, panel), 0) == pass_at, line_rank), 1
    )
    for s in range(2):
        order = narrow(jnp.where(number_c == place_ref[s : s + 1, :], 1.0, 0.0))
        low_ref[s] = narrow(
            lax.dot_general(
                lower_ref[s], order, (((1,), (1,)), ((), ())), preferred_element_type=jnp.float32
            )
        )


def finish_kernel(
    panel,
    pos_ref,
    rows_ref,
    part_ref,
    other_ref,
    land_ref,
    gone_ref,
    cross_ref,
    cross_other_ref,
    y0_ref,
    y1_ref,
    y2_ref,
    y3_ref,
    low_ref,
    upper_ref,
    place_ref,
    out_ref,
    new_ref,
    corner_ref,
    gone_first_ref,
    gone_second_ref,
    top_ref,
):
    step = pl.program_id(0)
    here, column = pos_ref[0], pos_ref[1]
    even = (column & 1) == 0
    width = panel
    bf16 = jnp.bfloat16

    @pl.when(step == 0)
    def _():
        mine, others = cross_ref[...], cross_other_ref[...]
        from_first = jnp.where(even, mine, others)
        from_second = jnp.where(even, others, mine)
        gone_first_ref[...] = from_first[panel:]
        gone_second_ref[...] = from_second[panel:]
        quarter = panel // NY
        y_refs = (y0_ref, y1_ref, y2_ref, y3_ref)
        pivot_first = jnp.concatenate([r[:quarter, :] for r in y_refs])
        pivot_second = jnp.concatenate([r[quarter:, :] for r in y_refs])
        row_first = narrow(dot(low_ref[0], pivot_first))
        corner_ref[...] = narrow(dot(low_ref[0], from_second[:panel]))
        lower_factor = narrow(dot(from_first[:panel], upper_ref[0]))
        reduced = narrow(pivot_second.astype(jnp.float32) - dot(lower_factor, row_first))
        row_second = narrow(dot(low_ref[1], reduced))
        new_ref[:panel, :] = row_first
        new_ref[panel:, :] = row_second

        @pl.when(here <= 1)
        def _():
            top_ref[...] = jnp.where(here == 0, row_first, row_second)

        @pl.when((here <= 1) & (column <= 1) & (here >= column))
        def _():
            raw = jnp.where(
                here == 0,
                pivot_first[:, :width],
                jnp.where(column == 0, lower_factor, reduced[:, :width]),
            )
            place = jnp.where(here == 0, place_ref[0:1, :], place_ref[1:2, :])
            order = narrow(jnp.where(iota((panel, panel), 0) == place, 1.0, 0.0))
            top_ref[:, :width] = narrow(
                lax.dot_general(
                    order, raw, (((0,), (0,)), ((), ())), preferred_element_type=jnp.float32
                )
            )

    @pl.when(step > 0)
    def _():
        n = rows_ref.shape[0]
        begin = (step - 1) * n
        hits = (iota((n, 2 * DEST_ROWS), 0) + begin) == land_ref[...]
        marks = jnp.where(hits, 1.0, 0.0)
        hit = jnp.sum(marks, axis=1, keepdims=True) > 0.5
        marks = narrow(marks)

        def settle(value, gone):
            return jnp.where(hit, dot(marks, gone), value.astype(jnp.float32))

        mine, others = part_ref[...], other_ref[...]
        panel_first = settle(jnp.where(even, mine, others), gone_first_ref[...])
        panel_second = settle(jnp.where(even, others, mine), gone_second_ref[...])
        factor_first = narrow(dot(narrow(panel_first), upper_ref[0]))
        mid = narrow(panel_second - dot(factor_first, corner_ref[...]))
        factor_second = narrow(dot(mid, upper_ref[1]))
        current = settle(rows_ref[...], gone_ref[...])
        updated = narrow(
            current
            - dot(factor_first, new_ref[:panel, :])
            - dot(factor_second, new_ref[panel:, :])
        )
        out_ref[...] = updated

        @pl.when(column <= 1)
        def _():
            out_ref[:, :width] = jnp.where(column == 0, factor_first, factor_second)

        @pl.when((here <= 1) & (begin < panel))
        def _():
            out_ref[...] = top_ref[pl.ds(pl.multiple_of(begin, n), n), :]


def whole(shape):
    return pl.BlockSpec(shape, lambda *_: (0,) * len(shape))


def smem():
    return pl.BlockSpec(memory_space=pltpu.SMEM)


def shape(dims, dtype=jnp.bfloat16):
    return jax.ShapeDtypeStruct(dims, dtype)


def per_device(matrix, pivots, lower_inverse, upper_inverse):
    row_blocks, panel, col_blocks, width = matrix.shape
    local_rows, local_cols = row_blocks * panel, col_blocks * width
    here = lax.axis_index("prow")
    column = lax.axis_index("pcol")
    y, z = here // NZ, here % NZ
    x, core = column // NC, column % NC
    position = jnp.stack([here, column]).astype(jnp.int32)
    rows = matrix.reshape(local_rows, local_cols)
    down_pivots = pivots.T
    per_home = panel // N_HOMES
    params = pltpu.CompilerParams(vmem_limit_bytes=40 * MIB)

    picks, keep, place, flag_deal = pl.pallas_call(
        functools.partial(deal_kernel, panel),
        grid=(1,),
        in_specs=[smem(), whole((2, panel)), whole((panel, 2)), whole((local_rows, local_cols))],
        out_specs=[
            whole((N_HOMES * PAIR_ROWS, local_cols)),
            whole((2 * per_home, 1)),
            whole((2, panel)),
            whole((1, panel)),
        ],
        out_shape=[
            shape((N_HOMES * PAIR_ROWS, local_cols)),
            shape((2 * per_home, 1), jnp.int32),
            shape((2, panel), jnp.int32),
            shape((1, panel), jnp.int32),
        ],
        compiler_params=params,
        name="deal",
    )(position, pivots, down_pivots, rows)

    dealt = lax.all_to_all(picks, "prow", 0, 0, tiled=True)

    matrix_later, keep_later = lax.optimization_barrier((matrix, keep))
    own = [matrix_later[k, :, 0, :] for k in range(3)]
    got = [lax.ppermute(own[k], "pcol", move_x([(0, k + 1)])) for k in (0, 2, 1)]
    third = jnp.where(x == 1, got[0], jnp.where(x == 3, got[1], got[2]))
    up = lax.ppermute(third, "pcol", move_x([(1, 2), (2, 3)]))
    down = lax.ppermute(third, "pcol", move_x([(2, 1), (3, 2)]))
    across = lax.ppermute(third, "pcol", move_x([(1, 3), (3, 1)]))
    one = jnp.where(x == 0, own[0], jnp.where(x == 1, third, jnp.where(x == 2, up, across)))
    two = jnp.where(x == 0, own[1], jnp.where(x == 2, third, jnp.where(x == 1, down, up)))
    three = jnp.where(x == 0, own[2], jnp.where(x == 3, third, jnp.where(x == 2, down, across)))
    part = jnp.concatenate([one, two, three])
    other = lax.ppermute(part, "pcol", SWAP)

    leaving, passing, land, flag_leave, low = pl.pallas_call(
        functools.partial(leave_kernel, panel),
        grid=(1,),
        in_specs=[
            smem(),
            whole((2, panel)),
            whole((panel, 2)),
            whole((panel, local_cols)),
            whole((2, panel)),
            whole((2, panel, panel)),
        ],
        out_specs=[
            whole((NY * LINE_ROWS, local_cols)),
            whole((NZ * DEST_ROWS, 1)),
            whole((2 * DEST_ROWS, 1)),
            whole((1, panel)),
            whole((2, panel, panel)),
        ],
        out_shape=[
            shape((NY * LINE_ROWS, local_cols)),
            shape((NZ * DEST_ROWS, 1), jnp.int32),
            shape((2 * DEST_ROWS, 1), jnp.int32),
            shape((1, panel), jnp.int32),
            shape((2, panel, panel)),
        ],
        compiler_params=params,
        name="leave",
    )(position, pivots, down_pivots, rows, place, lower_inverse)
    leaving = leaving.reshape(NY, LINE_ROWS, local_cols)
    arrived = [lax.ppermute(leaving[s], "prow", shift_y(s, [0], [0, 1])) for s in (1, 3, 2)]

    choose = narrow((keep_later == jnp.arange(N_HOMES * PAIR_ROWS)[None, :]).astype(jnp.float32))
    block = narrow(dot(choose, dealt))
    from_lo = lax.ppermute(block, "prow", shift_z(1))
    from_hi = lax.ppermute(block, "prow", shift_z(-1))
    opposite = lax.ppermute(block, "prow", shift_z(4))
    two_lo = lax.ppermute(jnp.concatenate([block, from_lo]), "prow", shift_z(2))
    two_hi = lax.ppermute(jnp.concatenate([block, from_hi]), "prow", shift_z(-2))

    on_line = jnp.where(
        y == 0, leaving[0], jnp.where(y == 1, arrived[0], jnp.where(y == 3, arrived[1], arrived[2]))
    )
    on_line, from_lo, from_hi = lax.optimization_barrier((on_line, from_lo, from_hi))
    choose = narrow((passing == jnp.arange(LINE_ROWS)[None, :]).astype(jnp.float32))
    spread = narrow(dot(choose, on_line)).reshape(NZ, DEST_ROWS, local_cols)
    landed = [spread[0]] + [
        lax.ppermute(spread[s], "prow", shift_z(s, [0, 1])) for s in range(1, NZ)
    ]

    blocks = [block, from_lo, from_hi, opposite, two_lo[: 2 * per_home], two_lo[2 * per_home :]]
    blocks += [two_hi[: 2 * per_home], two_hi[2 * per_home :]]
    z_line = jnp.concatenate([b[:per_home] for b in blocks] + [b[per_home:] for b in blocks])
    y_parts = [z_line] + [lax.ppermute(z_line, "prow", shift_y(s)) for s in (1, -1, 2)]

    landed = jnp.stack(landed)
    gone = jnp.concatenate(
        [
            lax.dynamic_index_in_dim(landed, z, 0, False),
            lax.dynamic_index_in_dim(landed, (z - 1) % NZ, 0, False),
        ]
    )

    half = panel // NY
    extra = jnp.where(core == 0, z_line[half:, :width], z_line[:half, :width])
    extra = jnp.concatenate([extra, gone[:, :width]])
    sent = [lax.ppermute(extra, "pcol", move_x([(0, k)])) for k in (1, 3, 2)]
    extra = jnp.where(x == 0, extra, jnp.where(x == 1, sent[0], jnp.where(x == 3, sent[1], sent[2])))
    cross = extra[:half]
    cross = jnp.concatenate(
        [cross] + [lax.ppermute(cross, "prow", shift_y(s)) for s in (1, -1, 2)] + [extra[half:]]
    )
    cross_other = lax.ppermute(cross, "pcol", SWAP)

    n_block = panel // 2
    steps = local_rows // n_block

    def row_block(cols):
        return pl.BlockSpec((n_block, cols), lambda i: (jnp.maximum(i - 1, 0), 0))

    result = pl.pallas_call(
        functools.partial(finish_kernel, panel),
        grid=(steps + 1,),
        in_specs=[
            smem(),
            row_block(local_cols),
            row_block(width),
            row_block(width),
            whole((1, 2 * DEST_ROWS)),
            whole((2 * DEST_ROWS, local_cols)),
            whole((panel + 2 * DEST_ROWS, width)),
            whole((panel + 2 * DEST_ROWS, width)),
            whole((2 * half, local_cols)),
            whole((2 * half, local_cols)),
            whole((2 * half, local_cols)),
            whole((2 * half, local_cols)),
            whole((2, panel, panel)),
            whole((2, panel, panel)),
            whole((2, panel)),
        ],
        out_specs=row_block(local_cols),
        out_shape=shape((local_rows, local_cols)),
        scratch_shapes=[
            pltpu.VMEM((2 * panel, local_cols), jnp.bfloat16),
            pltpu.VMEM((panel, width), jnp.bfloat16),
            pltpu.VMEM((2 * DEST_ROWS, width), jnp.bfloat16),
            pltpu.VMEM((2 * DEST_ROWS, width), jnp.bfloat16),
            pltpu.VMEM((panel, local_cols), jnp.bfloat16),
        ],
        compiler_params=params,
        name="finish",
    )(position, rows, part, other, land.reshape(1, -1), gone, cross, cross_other, *y_parts, low, upper_inverse, place)
    result = result.reshape(matrix.shape)
    overflow = (jnp.max(flag_deal) >= PAIR_ROWS) | (jnp.max(flag_leave) > 0)
    return lax.cond(
        overflow,
        lambda a, *rest: general_steps(*rest),
        lambda a, *rest: a,
        result,
        matrix,
        pivots,
        lower_inverse,
        upper_inverse,
    )


def solution(mesh):
    return jax.shard_map(
        per_device,
        mesh=mesh,
        in_specs=(P(None, "prow", None, "pcol"), P(), P(), P()),
        out_specs=P(None, "prow", None, "pcol"),
        check_vma=False,
    )
```

```python
import functools

import jax
import jax.numpy as jnp
from jax import lax
from jax.experimental import pallas as pl
from jax.experimental.pallas import tpu as pltpu
from jax.sharding import PartitionSpec as P

NY, NZ, NX, NC = 4, 8, 4, 2
N_HOMES = NY * NZ
PAIR_ROWS = 8
DEST_ROWS = 32
LINE_ROWS = 144
Z_ORDER = (0, 7, 1, 4, 6, 5, 2, 3)
Y_ORDER = (0, 3, 1, 2)
MIB = 1 << 20


def shift_y(step, rows=range(NY), cols=range(NZ)):
    return [(y * NZ + z, (y + step) % NY * NZ + z) for y in rows for z in cols]


def shift_z(step, cols=range(NZ)):
    return [(y * NZ + z, y * NZ + (z + step) % NZ) for y in range(NY) for z in cols]


def move_x(pairs):
    return [(a * NC + core, b * NC + core) for a, b in pairs for core in range(NC)]


SWAP = [(x * NC + core, x * NC + 1 - core) for x in range(NX) for core in range(NC)]


def broadcast(value, axis, root):
    mine = lax.axis_index(axis) == root
    return lax.psum(jnp.where(mine, value, jnp.zeros_like(value)), axis)


def locate(pivot_list, panel, prow_size, prow_here):
    block_index = pivot_list // panel
    owned_rows = block_index % prow_size == prow_here
    local_row = block_index // prow_size * panel + pivot_list % panel
    return (owned_rows, local_row)


def general_steps(matrix, pivots, lower_inverse, upper_inverse):
    row_blocks = matrix.shape[0]
    panel = matrix.shape[1]
    col_blocks = matrix.shape[2]
    prow_size = lax.axis_size("prow")
    pcol_size = lax.axis_size("pcol")
    prow_here = lax.axis_index("prow")
    pcol_here = lax.axis_index("pcol")
    local_rows = row_blocks * panel
    local_cols = col_blocks * panel
    current = matrix.reshape(local_rows, local_cols)
    row_global = jnp.repeat(jnp.arange(row_blocks, dtype=jnp.int32) * prow_size + prow_here, panel)
    col_global = jnp.repeat(jnp.arange(col_blocks, dtype=jnp.int32) * pcol_size + pcol_here, panel)
    offsets = jnp.arange(panel, dtype=jnp.int32)
    bf_zero = jnp.zeros((), jnp.bfloat16)
    def one_panel(panel_index, current):
        root_row, root_col = panel_index, panel_index
        diag_local = panel_local = 0
        pivot_list = pivots[panel_index]
        owned_rows, local_row = locate(pivot_list, panel, prow_size, prow_here)
        safe_rows = jnp.where(owned_rows, local_row, 0)
        picked = jnp.where(owned_rows[:, None], current[safe_rows], bf_zero)
        is_root = prow_here == root_row
        previous = current[diag_local : diag_local + panel]
        right_cols = col_global > panel_index
        displaced = broadcast(previous, "prow", root_row)
        gathered = lax.psum(picked, "prow").astype(jnp.float32)
        pivot_block = gathered.astype(jnp.bfloat16)
        product = jnp.dot(
            lower_inverse[panel_index], pivot_block, preferred_element_type=jnp.float32
        ).astype(jnp.bfloat16)
        new_row = jnp.where(right_cols[None, :], product, pivot_block)
        moved_rows = owned_rows & (pivot_list != panel_index * panel + offsets)
        targets = jnp.where(moved_rows, local_row, local_rows)
        current = current.at[targets].set(displaced, mode="drop")
        below_mask = row_global > panel_index
        panel_part = current[:, panel_local : panel_local + panel]
        upper_block = upper_inverse[panel_index]

        def factor(columns):
            result = jnp.dot(columns, upper_block, preferred_element_type=jnp.float32).astype(
                jnp.bfloat16
            )
            return jnp.where(below_mask[:, None], result, jnp.zeros((), jnp.bfloat16))

        def nothing(columns):
            return jnp.zeros((local_rows, panel), jnp.bfloat16)

        factors = lax.cond(pcol_here == root_col, factor, nothing, panel_part)
        factors = broadcast(factors, "pcol", root_col)
        update_rows = jnp.where(right_cols[None, :], new_row, bf_zero)
        correction = jnp.dot(factors, update_rows, preferred_element_type=jnp.float32)
        updated = (current.astype(jnp.float32) - correction).astype(jnp.bfloat16)
        owner_col = pcol_here == root_col
        new_panel = jnp.where(
            owner_col & below_mask[:, None], factors, updated[:, panel_local : panel_local + panel]
        )
        updated = updated.at[:, panel_local : panel_local + panel].set(new_panel)
        row_block = jnp.where(is_root, new_row, updated[diag_local : diag_local + panel])
        return updated.at[diag_local : diag_local + panel].set(row_block)

    current = lax.fori_loop(0, 2, one_panel, current)
    return current.reshape(matrix.shape)


def dot(a, b):
    return jnp.dot(a, b, preferred_element_type=jnp.float32)


def narrow(value):
    return value.astype(jnp.bfloat16)


def iota(shape, axis):
    return lax.broadcasted_iota(jnp.int32, shape, axis)


def total(mask_or_value, axis):
    return jnp.sum(mask_or_value, axis=axis, keepdims=True).astype(jnp.int32)


def pick(mask, value):
    return jnp.where(mask, value, 0).astype(jnp.float32)


def split_rows(row, panel):
    shift = panel.bit_length() - 1
    block = row >> shift
    return block & (N_HOMES - 1), ((block >> 5) << shift) + (row & (panel - 1))


def upright(row):
    tall = jnp.transpose(jnp.broadcast_to(row.astype(jnp.float32), (8, row.shape[1])))
    return tall[:, 0:1].astype(jnp.int32)


def place_of(step, order):
    result = jnp.zeros_like(step)
    for place, value in enumerate(order):
        result = jnp.where(step == value, place, result)
    return result


def deal_kernel(panel, pos_ref, across_ref, rows_ref, picks_ref, keep_ref, place_ref, flag_ref):
    here = pos_ref[0]
    y, z = here >> 3, here & 7
    first_r, second_r = across_ref[0:1, :], across_ref[1:2, :]
    first_c, second_c = upright(first_r), upright(second_r)
    square = (panel, panel)
    number_c, number_r = iota(square, 0), iota(square, 1)
    came_r = total(pick(first_c == second_r, number_c + 1), 0)
    came_c = total(pick(second_c == first_r, number_r + 1), 1)
    source_r = [first_r, jnp.where(came_r > 0, came_r - 1, second_r)]
    source_c = [first_c, jnp.where(came_c > 0, came_c - 1, second_c)]
    owners_r, locals_r = zip(*[split_rows(s, panel) for s in source_r])
    owners_c = [split_rows(s, panel)[0] for s in source_c]
    before = number_c < number_r
    slots, homes, entries = [], [], []
    for s in range(2):
        counts = total(
            pick((owners_c[s] == owners_r[s]) & before, 1025) + pick(owners_c[s] < owners_r[s], 1), 0
        )
        within, rank = counts >> 10, counts & 1023
        slot = within >> 5
        if s == 1:
            shared = total(pick(owners_c[0] == owners_r[1], 1), 0)
            slot = slot + ((shared + N_HOMES - 1) >> 5)
        slots.append(slot)
        homes.append(rank & (N_HOMES - 1))
        entries.append(rank >> 5)
    flag_ref[...] = jnp.maximum(slots[0], slots[1])
    deal = jnp.zeros((N_HOMES * PAIR_ROWS, 1), jnp.int32)
    position = iota((N_HOMES * PAIR_ROWS, panel), 0)
    per_home = panel // N_HOMES
    for s in range(2):
        at = jnp.where(owners_r[s] == here, homes[s] * PAIR_ROWS + slots[s], -1)
        deal = deal + total(pick(position == at, locals_r[s]), 1)
        kept_at = jnp.where(homes[s] == here, entries[s], -1)
        keep_ref[s * per_home : (s + 1) * per_home, :] = total(
            pick(iota((per_home, panel), 0) == kept_at, owners_r[s] * PAIR_ROWS + slots[s]), 1
        )
        z_place = place_of((homes[s] - z) & (NZ - 1), Z_ORDER)
        y_place = place_of(((homes[s] >> 3) - y) & (NY - 1), Y_ORDER)
        place_ref[s : s + 1, :] = (y_place * NZ + z_place) * per_home + entries[s]
    n_rows = rows_ref.shape[0]
    choose = jnp.where(iota((N_HOMES * PAIR_ROWS, n_rows), 1) == deal, 1.0, 0.0)
    picks_ref[...] = narrow(dot(narrow(choose), rows_ref[...]))


def leave_kernel(
    panel,
    pos_ref,
    across_ref,
    rows_ref,
    place_ref,
    lower_ref,
    slots_ref,
    leave0_ref,
    leave1_ref,
    leave2_ref,
    leave3_ref,
    passing_ref,
    land_ref,
    flag_ref,
    low_ref,
):
    here = pos_ref[0]
    y, z = here >> 3, here & 7
    odd = (here & 1) == 1
    first_r, second_r = across_ref[0:1, :], across_ref[1:2, :]
    first_c, second_c = upright(first_r), upright(second_r)
    square = (panel, panel)
    number_c, number_r = iota(square, 0), iota(square, 1)
    big = 1 << 20
    seen_r = total(pick(second_c == first_r, big) + pick(number_c + panel == first_r, second_c), 0)
    seen_c = total(pick(first_c == second_r, big) + pick(first_c == number_r + panel, second_r), 1)
    used_r = total(pick(first_c == number_r + panel, 1), 0)
    used_c = total(pick(number_c + panel == first_r, 1), 1)

    def goals(first, second, seen, used, number):
        inner = (first >= panel) & (first < 2 * panel)
        stop = seen & (big - 1)
        goal_first = jnp.where(
            inner,
            jnp.where(stop == first, -1, stop),
            jnp.where((first == number) | (seen >= big), -1, first),
        )
        goal_second = jnp.where((used > 0) | (second == number + panel), -1, second)
        return goal_first, goal_second

    goal_r = goals(first_r, second_r, seen_r, used_r, number_r[0:1, :])
    goal_c = goals(first_c, second_c, seen_c, used_c, number_c[:, 0:1])
    before = number_c < number_r
    lines, line_ranks, dests, dest_ranks, landing = [], [], [], [], []
    worst = jnp.zeros((1, panel), jnp.int32)
    for s in range(2):
        dest_r, local_r = split_rows(goal_r[s], panel)
        dest_r = jnp.where(goal_r[s] < 0, -1, dest_r)
        dest_c = jnp.where(goal_c[s] < 0, -1, split_rows(goal_c[s], panel)[0])
        line_r, line_c = dest_r >> 3, dest_c >> 3
        counts = total(
            pick((dest_c == dest_r) & before, 1024) + pick((line_c == line_r) & before, 1), 0
        )
        line_rank, dest_rank = counts & 1023, counts >> 10
        worst = jnp.maximum(
            worst,
            jnp.where(
                (dest_r >= 0) & ((line_rank >= LINE_ROWS) | (dest_rank >= DEST_ROWS)), 1, 0
            ),
        )
        land_at = jnp.where(dest_r == here, dest_rank, -1)
        landing.append(total(pick(iota((DEST_ROWS, panel), 0) == land_at, local_r + 1), 1) - 1)
        lines.append(line_r)
        line_ranks.append(line_rank)
        dests.append(dest_r)
        dest_ranks.append(dest_rank)
    worst = jnp.maximum(worst, jnp.where(slots_ref[...] >= PAIR_ROWS, 1, 0))
    flag_ref[0] = jnp.max(worst.astype(jnp.float32)).astype(jnp.int32)
    landing = jnp.concatenate(landing).astype(jnp.float32)
    landing = jnp.transpose(jnp.broadcast_to(landing, (2 * DEST_ROWS, 128)))
    land_ref[...] = landing[0:1, :].astype(jnp.int32)
    line = jnp.where(odd, lines[1], lines[0])
    line_rank = jnp.where(odd, line_ranks[1], line_ranks[0])
    dest = jnp.where(odd, dests[1], dests[0])
    dest_rank = jnp.where(odd, dest_ranks[1], dest_ranks[0])
    send_at = jnp.where(line < 0, -1, line * LINE_ROWS + line_rank)
    choose = jnp.where(iota((NY * LINE_ROWS, panel), 0) == send_at, 1.0, 0.0)
    leaving = narrow(dot(narrow(choose), rows_ref[:panel, :]))
    for k, ref in enumerate((leave0_ref, leave1_ref, leave2_ref, leave3_ref)):
        ref[...] = leaving[k * LINE_ROWS : (k + 1) * LINE_ROWS]
    pass_at = jnp.where(line == y, ((dest - z) & (NZ - 1)) * DEST_ROWS + dest_rank, -1)
    passing_ref[...] = total(
        pick(iota((NZ * DEST_ROWS, panel), 0) == pass_at, line_rank), 1
    )
    for s in range(2):
        order = narrow(jnp.where(number_c == place_ref[s : s + 1, :], 1.0, 0.0))
        low_ref[s] = narrow(
            lax.dot_general(
                lower_ref[s], order, (((1,), (1,)), ((), ())), preferred_element_type=jnp.float32
            )
        )


def block_kernel(keep_ref, dealt_ref, block_ref):
    n = dealt_ref.shape[0]
    choose = jnp.where(keep_ref[...] == iota((keep_ref.shape[0], n), 1), 1.0, 0.0)
    block_ref[...] = narrow(dot(narrow(choose), dealt_ref[...]))


def pair_kernel(block_ref, lo_ref, hi_ref, pair_lo_ref, pair_hi_ref):
    n = block_ref.shape[0]
    pair_lo_ref[:n, :] = block_ref[...]
    pair_lo_ref[n:, :] = lo_ref[...]
    pair_hi_ref[:n, :] = block_ref[...]
    pair_hi_ref[n:, :] = hi_ref[...]


def line_kernel(
    pos_ref, block_ref, lo_ref, hi_ref, opposite_ref, two_lo_ref, two_hi_ref, line_ref, extra_ref
):
    n = block_ref.shape[0]
    half = n // 2
    blocks = [block_ref[...], lo_ref[...], hi_ref[...], opposite_ref[...]]
    blocks += [two_lo_ref[:n, :], two_lo_ref[n:, :], two_hi_ref[:n, :], two_hi_ref[n:, :]]
    for k, value in enumerate(blocks):
        line_ref[k * half : (k + 1) * half, :] = value[:half]
        line_ref[(NZ + k) * half : (NZ + k + 1) * half, :] = value[half:]
    even = (pos_ref[1] & 1) == 0
    n, width = extra_ref.shape
    extra_ref[...] = jnp.where(even, line_ref[n:, :width], line_ref[:n, :width])


def by_x(x, at_0, at_1, at_2, at_3):
    return jnp.where(x <= 1, jnp.where(x == 0, at_0, at_1), jnp.where(x == 2, at_2, at_3))


def third_kernel(pos_ref, one_ref, two_ref, three_ref, third_ref):
    x = pos_ref[1] >> 1

    @pl.when(x <= 1)
    def _():
        third_ref[...] = one_ref[...]

    @pl.when(x == 2)
    def _():
        third_ref[...] = two_ref[...]

    @pl.when(x == 3)
    def _():
        third_ref[...] = three_ref[...]


def part_kernel(pos_ref, own_ref, third_ref, up_ref, down_ref, across_ref, part_ref):
    x = pos_ref[1] >> 1
    n = third_ref.shape[0]
    width = third_ref.shape[1]
    own = [own_ref.at[pl.ds(k * n, n), pl.ds(0, width)] for k in range(3)]
    by_place = (
        own,
        (third_ref, down_ref, across_ref),
        (up_ref, third_ref, down_ref),
        (across_ref, up_ref, third_ref),
    )
    for place, refs in enumerate(by_place):

        @pl.when(x == place)
        def _(refs=refs):
            for k, ref in enumerate(refs):
                part_ref[k * n : (k + 1) * n, :] = ref[...]


def spread_kernel(pos_ref, passing_ref, own_ref, one_ref, two_ref, three_ref, keep_ref, send_ref):
    y = pos_ref[0] >> 3
    on_line = by_x(y, own_ref[...], one_ref[...], two_ref[...], three_ref[...])
    n_rows = passing_ref.shape[0]
    choose = jnp.where(passing_ref[...] == iota((n_rows, LINE_ROWS), 1), 1.0, 0.0)
    spread = narrow(dot(narrow(choose), on_line))
    keep_ref[...] = spread[: n_rows // 2]
    send_ref[...] = spread[n_rows // 2 :]


def fold_kernel(bit, pos_ref, kept_ref, came_ref, keep_ref, send_ref):
    n = keep_ref.shape[0]

    @pl.when((pos_ref[0] & bit) == 0)
    def _():
        keep_ref[...] = kept_ref[:n, :]
        send_ref[...] = kept_ref[n:, :]

    @pl.when((pos_ref[0] & bit) != 0)
    def _():
        keep_ref[...] = came_ref[:n, :]
        send_ref[...] = came_ref[n:, :]


def gone_kernel(pos_ref, kept_ref, came_ref, gone_ref, gone_panel_ref):
    n, width = kept_ref.shape[0], gone_panel_ref.shape[1]
    even = (pos_ref[0] & 1) == 0
    kept, came = kept_ref[...], came_ref[...]
    gone_ref[:n, :] = jnp.where(even, kept, came)
    gone_ref[n:, :] = jnp.where(even, came, kept)
    gone_panel_ref[...] = gone_ref[:, :width]


def extra_kernel(pos_ref, own_ref, one_ref, two_ref, three_ref, cross_ref):
    x = pos_ref[1] >> 1
    cross_ref[...] = by_x(x, own_ref[...], one_ref[...], two_ref[...], three_ref[...])


def cross_kernel(pos_ref, c0_ref, c1_ref, c2_ref, c3_ref, own_ref, one_ref, two_ref, three_ref, cross_ref):
    n = c0_ref.shape[0]
    for k, ref in enumerate((c0_ref, c1_ref, c2_ref, c3_ref)):
        cross_ref[k * n : (k + 1) * n, :] = ref[...]
    x = pos_ref[1] >> 1
    cross_ref[NY * n :, :] = by_x(x, own_ref[...], one_ref[...], two_ref[...], three_ref[...])


def finish_kernel(
    panel,
    pos_ref,
    rows_ref,
    part_ref,
    other_ref,
    land_ref,
    gone_ref,
    cross_ref,
    cross_other_ref,
    y0_ref,
    y1_ref,
    y2_ref,
    far_first_ref,
    far_second_ref,
    low_ref,
    upper_ref,
    place_ref,
    out_ref,
    new_ref,
    corner_ref,
    gone_first_ref,
    gone_second_ref,
    top_ref,
):
    step = pl.program_id(0)
    here, column = pos_ref[0], pos_ref[1]
    even = (column & 1) == 0
    width = panel
    bf16 = jnp.bfloat16

    @pl.when(step == 0)
    def _():
        mine, others = cross_ref[...], cross_other_ref[...]
        from_first = jnp.where(even, mine, others)
        from_second = jnp.where(even, others, mine)
        gone_first_ref[...] = from_first[panel:]
        gone_second_ref[...] = from_second[panel:]
        quarter = panel // NY
        y_refs = (y0_ref, y1_ref, y2_ref)
        pivot_first = jnp.concatenate([r[:quarter, :] for r in y_refs] + [far_first_ref[...]])
        pivot_second = jnp.concatenate([r[quarter:, :] for r in y_refs] + [far_second_ref[...]])
        row_first = narrow(dot(low_ref[0], pivot_first))
        corner_ref[...] = narrow(dot(low_ref[0], from_second[:panel]))
        lower_factor = narrow(dot(from_first[:panel], upper_ref[0]))
        reduced = narrow(pivot_second.astype(jnp.float32) - dot(lower_factor, row_first))
        row_second = narrow(dot(low_ref[1], reduced))
        new_ref[:panel, :] = row_first
        new_ref[panel:, :] = row_second

        @pl.when(here <= 1)
        def _():
            top_ref[...] = jnp.where(here == 0, row_first, row_second)

        @pl.when((here <= 1) & (column <= 1) & (here >= column))
        def _():
            raw = jnp.where(
                here == 0,
                pivot_first[:, :width],
                jnp.where(column == 0, lower_factor, reduced[:, :width]),
            )
            place = jnp.where(here == 0, place_ref[0:1, :], place_ref[1:2, :])
            order = narrow(jnp.where(iota((panel, panel), 0) == place, 1.0, 0.0))
            top_ref[:, :width] = narrow(
                lax.dot_general(
                    order, raw, (((0,), (0,)), ((), ())), preferred_element_type=jnp.float32
                )
            )

    @pl.when(step > 0)
    def _():
        n = rows_ref.shape[0]
        begin = (step - 1) * n
        hits = (iota((n, 2 * DEST_ROWS), 0) + begin) == land_ref[...]
        marks = jnp.where(hits, 1.0, 0.0)
        hit = jnp.sum(marks, axis=1, keepdims=True) > 0.5
        marks = narrow(marks)

        def settle(value, gone):
            return jnp.where(hit, dot(marks, gone), value.astype(jnp.float32))

        mine, others = part_ref[...], other_ref[...]
        panel_first = settle(jnp.where(even, mine, others), gone_first_ref[...])
        panel_second = settle(jnp.where(even, others, mine), gone_second_ref[...])
        factor_first = narrow(dot(narrow(panel_first), upper_ref[0]))
        mid = narrow(panel_second - dot(factor_first, corner_ref[...]))
        factor_second = narrow(dot(mid, upper_ref[1]))
        current = settle(rows_ref[...], gone_ref[...])
        updated = narrow(
            current
            - dot(factor_first, new_ref[:panel, :])
            - dot(factor_second, new_ref[panel:, :])
        )
        out_ref[...] = updated

        @pl.when(column <= 1)
        def _():
            out_ref[:, :width] = jnp.where(column == 0, factor_first, factor_second)

        @pl.when((here <= 1) & (begin < panel))
        def _():
            out_ref[...] = top_ref[pl.ds(pl.multiple_of(begin, n), n), :]


def whole(shape):
    return pl.BlockSpec(shape, lambda *_: (0,) * len(shape))


def smem():
    return pl.BlockSpec(memory_space=pltpu.SMEM)


def shape(dims, dtype=jnp.bfloat16):
    return jax.ShapeDtypeStruct(dims, dtype)


def local_kernel(body, name, outs, scalars, *arrays):
    return pl.pallas_call(
        body,
        grid=(1,),
        in_specs=[smem() for _ in scalars] + [whole(v.shape) for v in arrays],
        out_specs=[smem() if o.shape == (1,) else whole(o.shape) for o in outs],
        out_shape=outs,
        compiler_params=pltpu.CompilerParams(vmem_limit_bytes=40 * MIB),
        cost_estimate=pl.CostEstimate(flops=0, bytes_accessed=0, transcendentals=0),
        name=name,
    )(*scalars, *arrays)


def after(values, *others):
    return lax.optimization_barrier((values, others))[0]


def per_device(matrix, pivots, lower_inverse, upper_inverse):
    row_blocks, panel, col_blocks, width = matrix.shape
    local_rows, local_cols = row_blocks * panel, col_blocks * width
    here = lax.axis_index("prow")
    column = lax.axis_index("pcol")
    position = jnp.stack([here, column]).astype(jnp.int32)
    rows = matrix.reshape(local_rows, local_cols)
    per_home = panel // N_HOMES
    i32 = jnp.int32

    picks, keep, place, slots = local_kernel(
        functools.partial(deal_kernel, panel),
        "deal",
        [
            shape((N_HOMES * PAIR_ROWS, local_cols)),
            shape((2 * per_home, 1), i32),
            shape((2, panel), i32),
            shape((1, panel), i32),
        ],
        [position],
        pivots,
        rows,
    )
    dealt = lax.all_to_all(picks, "prow", 0, 0, tiled=True)

    own = [rows[k * panel : (k + 1) * panel, :width] for k in range(3)]
    got = [lax.ppermute(own[k], "pcol", move_x([(0, k + 1)])) for k in range(3)]

    line_shape = shape((LINE_ROWS, local_cols))
    *leaving, passing, land, flag, low = local_kernel(
        functools.partial(leave_kernel, panel),
        "leave",
        [line_shape] * NY
        + [
            shape((NZ * DEST_ROWS, 1), i32),
            shape((1, 2 * DEST_ROWS), i32),
            shape((1,), i32),
            shape((2, panel, panel)),
        ],
        [position],
        pivots,
        rows,
        place,
        lower_inverse,
        slots,
    )
    arrived = [lax.ppermute(leaving[s], "prow", shift_y(s, [0], [0, 1])) for s in (1, 2, 3)]

    dealt = after(dealt, got[0], got[2])
    (block,) = local_kernel(
        block_kernel, "block", [shape((2 * per_home, local_cols))], [], keep, dealt
    )
    from_lo = lax.ppermute(block, "prow", shift_z(1))
    from_hi = lax.ppermute(block, "prow", shift_z(-1))
    opposite = lax.ppermute(block, "prow", shift_z(4))
    quarter_shape = shape((NZ // 2 * DEST_ROWS, local_cols))
    kept, send = local_kernel(
        spread_kernel, "spread", [quarter_shape] * 2, [position], passing, leaving[0], *arrived
    )
    came = lax.ppermute(send, "prow", shift_z(4, [0, 1]))

    from_lo, from_hi = after((from_lo, from_hi), got[1], came)
    pair_shape = shape((4 * per_home, local_cols))
    pair_lo, pair_hi = local_kernel(
        pair_kernel, "pair", [pair_shape] * 2, [], block, from_lo, from_hi
    )
    two_lo = lax.ppermute(pair_lo, "prow", shift_z(2))
    two_hi = lax.ppermute(pair_hi, "prow", shift_z(-2))
    eighth_shape = shape((NZ // 4 * DEST_ROWS, local_cols))
    kept, send = local_kernel(
        functools.partial(fold_kernel, 4), "fold4", [eighth_shape] * 2, [position], kept, came
    )
    came = lax.ppermute(send, "prow", shift_z(2, [0, 1, 4, 5]))
    third_shape = shape((panel, width))
    (third,) = local_kernel(third_kernel, "third", [third_shape], [position], *after(got, from_lo))
    up = lax.ppermute(third, "pcol", move_x([(1, 2), (2, 3)]))
    down = lax.ppermute(third, "pcol", move_x([(2, 1), (3, 2)]))

    two_lo, two_hi = after((two_lo, two_hi), up, down, came)
    half = panel // NY
    z_line, extra = local_kernel(
        line_kernel,
        "line",
        [shape((2 * half, local_cols)), shape((half, width))],
        [position],
        block,
        from_lo,
        from_hi,
        opposite,
        two_lo,
        two_hi,
    )
    y_lo = lax.ppermute(z_line, "prow", shift_y(1))
    y_hi = lax.ppermute(z_line, "prow", shift_y(-1))
    across = lax.ppermute(after(third, extra), "pcol", move_x([(1, 3), (3, 1)]))
    sent = [lax.ppermute(extra, "pcol", move_x([(0, k)])) for k in (1, 2, 3)]
    one_shape = shape((DEST_ROWS, local_cols))
    kept, send = local_kernel(
        functools.partial(fold_kernel, 2), "fold2", [one_shape] * 2, [position], kept, came
    )
    came = lax.ppermute(send, "prow", shift_z(1))

    y_lo, y_hi = after((y_lo, y_hi), across, sent, came)
    far_first = lax.ppermute(y_lo[:half], "prow", shift_y(1))
    far_second = lax.ppermute(y_hi[half:], "prow", shift_y(-1))
    (cross,) = local_kernel(
        extra_kernel, "extra", [shape((half, width))], [position], extra, *sent
    )
    crossed = [lax.ppermute(cross, "prow", shift_y(s)) for s in (1, -1, 2)]
    n_gone = 2 * DEST_ROWS
    gone, gone_panel = local_kernel(
        gone_kernel,
        "gone",
        [shape((n_gone, local_cols)), shape((n_gone, width))],
        [position],
        kept,
        came,
    )
    gone_sent = [lax.ppermute(gone_panel, "pcol", move_x([(0, k)])) for k in (1, 2, 3)]
    (part,) = local_kernel(
        part_kernel,
        "part",
        [shape((local_rows, width))],
        [position],
        rows,
        third,
        up,
        down,
        across,
    )
    other = lax.ppermute(part, "pcol", SWAP)

    crossed = after(crossed, far_first, far_second, other)
    (cross,) = local_kernel(
        cross_kernel,
        "cross",
        [shape((panel + n_gone, width))],
        [position],
        cross,
        *crossed,
        gone_panel,
        *gone_sent,
    )
    cross_other = lax.ppermute(cross, "pcol", SWAP)
    y_parts = [z_line, y_lo, y_hi, far_first, far_second]

    n_block = panel // 2
    steps = local_rows // n_block

    def row_block(cols):
        return pl.BlockSpec((n_block, cols), lambda i: (jnp.maximum(i - 1, 0), 0))

    result = pl.pallas_call(
        functools.partial(finish_kernel, panel),
        grid=(steps + 1,),
        in_specs=[
            smem(),
            row_block(local_cols),
            row_block(width),
            row_block(width),
            whole((1, 2 * DEST_ROWS)),
            whole((2 * DEST_ROWS, local_cols)),
            whole((panel + 2 * DEST_ROWS, width)),
            whole((panel + 2 * DEST_ROWS, width)),
            whole((2 * half, local_cols)),
            whole((2 * half, local_cols)),
            whole((2 * half, local_cols)),
            whole((half, local_cols)),
            whole((half, local_cols)),
            whole((2, panel, panel)),
            whole((2, panel, panel)),
            whole((2, panel)),
        ],
        out_specs=row_block(local_cols),
        out_shape=shape((local_rows, local_cols)),
        scratch_shapes=[
            pltpu.VMEM((2 * panel, local_cols), jnp.bfloat16),
            pltpu.VMEM((panel, width), jnp.bfloat16),
            pltpu.VMEM((2 * DEST_ROWS, width), jnp.bfloat16),
            pltpu.VMEM((2 * DEST_ROWS, width), jnp.bfloat16),
            pltpu.VMEM((panel, local_cols), jnp.bfloat16),
        ],
        compiler_params=pltpu.CompilerParams(vmem_limit_bytes=40 * MIB),
        name="finish",
    )(position, rows, part, other, land, gone, cross, cross_other, *y_parts, low, upper_inverse, place)
    result = result.reshape(matrix.shape)
    return lax.cond(
        flag[0] > 0,
        lambda a, *rest: general_steps(*rest),
        lambda a, *rest: a,
        result,
        matrix,
        pivots,
        lower_inverse,
        upper_inverse,
    )


def solution(mesh):
    return jax.shard_map(
        per_device,
        mesh=mesh,
        in_specs=(P(None, "prow", None, "pcol"), P(), P(), P()),
        out_specs=P(None, "prow", None, "pcol"),
        check_vma=False,
    )
```

```python
import functools

import jax
import jax.numpy as jnp
from jax import lax
from jax.experimental import pallas as pl
from jax.experimental.pallas import tpu as pltpu
from jax.sharding import PartitionSpec as P

NY, NZ, NX, NC = 4, 8, 4, 2
N_HOMES = NY * NZ
PAIR_ROWS = 8
DEST_ROWS = 32
LINE_ROWS = 144
Z_ORDER = (0, 7, 1, 4, 6, 5, 2, 3)
Y_ORDER = (0, 3, 1, 2)
MIB = 1 << 20
GROUP = 16


def shift_y(step, rows=range(NY), cols=range(NZ)):
    return [(y * NZ + z, (y + step) % NY * NZ + z) for y in rows for z in cols]


def shift_z(step, cols=range(NZ)):
    return [(y * NZ + z, y * NZ + (z + step) % NZ) for y in range(NY) for z in cols]


def move_x(pairs):
    return [(a * NC + core, b * NC + core) for a, b in pairs for core in range(NC)]


SWAP = [(x * NC + core, x * NC + 1 - core) for x in range(NX) for core in range(NC)]


def broadcast(value, axis, root):
    mine = lax.axis_index(axis) == root
    return lax.psum(jnp.where(mine, value, jnp.zeros_like(value)), axis)


def locate(pivot_list, panel, prow_size, prow_here):
    block_index = pivot_list // panel
    owned_rows = block_index % prow_size == prow_here
    local_row = block_index // prow_size * panel + pivot_list % panel
    return (owned_rows, local_row)


def general_steps(matrix, pivots, lower_inverse, upper_inverse):
    row_blocks = matrix.shape[0]
    panel = matrix.shape[1]
    col_blocks = matrix.shape[2]
    prow_size = lax.axis_size("prow")
    pcol_size = lax.axis_size("pcol")
    prow_here = lax.axis_index("prow")
    pcol_here = lax.axis_index("pcol")
    local_rows = row_blocks * panel
    local_cols = col_blocks * panel
    current = matrix.reshape(local_rows, local_cols)
    row_global = jnp.repeat(jnp.arange(row_blocks, dtype=jnp.int32) * prow_size + prow_here, panel)
    col_global = jnp.repeat(jnp.arange(col_blocks, dtype=jnp.int32) * pcol_size + pcol_here, panel)
    offsets = jnp.arange(panel, dtype=jnp.int32)
    bf_zero = jnp.zeros((), jnp.bfloat16)
    def one_panel(panel_index, current):
        root_row, root_col = panel_index, panel_index
        diag_local = panel_local = 0
        pivot_list = pivots[panel_index]
        owned_rows, local_row = locate(pivot_list, panel, prow_size, prow_here)
        safe_rows = jnp.where(owned_rows, local_row, 0)
        picked = jnp.where(owned_rows[:, None], current[safe_rows], bf_zero)
        is_root = prow_here == root_row
        previous = current[diag_local : diag_local + panel]
        right_cols = col_global > panel_index
        displaced = broadcast(previous, "prow", root_row)
        gathered = lax.psum(picked, "prow").astype(jnp.float32)
        pivot_block = gathered.astype(jnp.bfloat16)
        product = jnp.dot(
            lower_inverse[panel_index], pivot_block, preferred_element_type=jnp.float32
        ).astype(jnp.bfloat16)
        new_row = jnp.where(right_cols[None, :], product, pivot_block)
        moved_rows = owned_rows & (pivot_list != panel_index * panel + offsets)
        targets = jnp.where(moved_rows, local_row, local_rows)
        current = current.at[targets].set(displaced, mode="drop")
        below_mask = row_global > panel_index
        panel_part = current[:, panel_local : panel_local + panel]
        upper_block = upper_inverse[panel_index]

        def factor(columns):
            result = jnp.dot(columns, upper_block, preferred_element_type=jnp.float32).astype(
                jnp.bfloat16
            )
            return jnp.where(below_mask[:, None], result, jnp.zeros((), jnp.bfloat16))

        def nothing(columns):
            return jnp.zeros((local_rows, panel), jnp.bfloat16)

        factors = lax.cond(pcol_here == root_col, factor, nothing, panel_part)
        factors = broadcast(factors, "pcol", root_col)
        update_rows = jnp.where(right_cols[None, :], new_row, bf_zero)
        correction = jnp.dot(factors, update_rows, preferred_element_type=jnp.float32)
        updated = (current.astype(jnp.float32) - correction).astype(jnp.bfloat16)
        owner_col = pcol_here == root_col
        new_panel = jnp.where(
            owner_col & below_mask[:, None], factors, updated[:, panel_local : panel_local + panel]
        )
        updated = updated.at[:, panel_local : panel_local + panel].set(new_panel)
        row_block = jnp.where(is_root, new_row, updated[diag_local : diag_local + panel])
        return updated.at[diag_local : diag_local + panel].set(row_block)

    current = lax.fori_loop(0, 2, one_panel, current)
    return current.reshape(matrix.shape)


def dot(a, b):
    return jnp.dot(a, b, preferred_element_type=jnp.float32)


def narrow(value):
    return value.astype(jnp.bfloat16)


def iota(shape, axis):
    return lax.broadcasted_iota(jnp.int32, shape, axis)


def total(mask_or_value, axis):
    return jnp.sum(mask_or_value, axis=axis, keepdims=True).astype(jnp.int32)


def pick(mask, value):
    return jnp.where(mask, value, 0).astype(jnp.float32)


def split_rows(row, panel):
    shift = panel.bit_length() - 1
    block = row >> shift
    return block & (N_HOMES - 1), ((block >> 5) << shift) + (row & (panel - 1))


def upright(row):
    tall = jnp.transpose(jnp.broadcast_to(row.astype(jnp.float32), (8, row.shape[1])))
    return tall[:, 0:1].astype(jnp.int32)


def place_of(step, order):
    result = jnp.zeros_like(step)
    for place, value in enumerate(order):
        result = jnp.where(step == value, place, result)
    return result


def deal_kernel(panel, pos_ref, across_ref, rows_ref, picks_ref, keep_ref, place_ref, flag_ref):
    here = pos_ref[0]
    y, z = here >> 3, here & 7
    first_r, second_r = across_ref[0:1, :], across_ref[1:2, :]
    first_c, second_c = upright(first_r), upright(second_r)
    square = (panel, panel)
    number_c, number_r = iota(square, 0), iota(square, 1)
    came_r = total(pick(first_c == second_r, number_c + 1), 0)
    came_c = total(pick(second_c == first_r, number_r + 1), 1)
    source_r = [first_r, jnp.where(came_r > 0, came_r - 1, second_r)]
    source_c = [first_c, jnp.where(came_c > 0, came_c - 1, second_c)]
    owners_r, locals_r = zip(*[split_rows(s, panel) for s in source_r])
    owners_c = [split_rows(s, panel)[0] for s in source_c]
    before = number_c < number_r
    slots, homes, entries = [], [], []
    for s in range(2):
        counts = total(
            pick((owners_c[s] == owners_r[s]) & before, 1025) + pick(owners_c[s] < owners_r[s], 1), 0
        )
        within, rank = counts >> 10, counts & 1023
        slot = within >> 5
        if s == 1:
            shared = total(pick(owners_c[0] == owners_r[1], 1), 0)
            slot = slot + ((shared + N_HOMES - 1) >> 5)
        slots.append(slot)
        homes.append(rank & (N_HOMES - 1))
        entries.append(rank >> 5)
    flag_ref[...] = jnp.maximum(slots[0], slots[1])
    deal = jnp.zeros((N_HOMES * PAIR_ROWS, 1), jnp.int32)
    position = iota((N_HOMES * PAIR_ROWS, panel), 0)
    per_home = panel // N_HOMES
    for s in range(2):
        at = jnp.where(owners_r[s] == here, homes[s] * PAIR_ROWS + slots[s], -1)
        deal = deal + total(pick(position == at, locals_r[s]), 1)
        kept_at = jnp.where(homes[s] == here, entries[s], -1)
        keep_ref[s * per_home : (s + 1) * per_home, :] = total(
            pick(iota((per_home, panel), 0) == kept_at, owners_r[s] * PAIR_ROWS + slots[s]), 1
        )
        z_place = place_of((homes[s] - z) & (NZ - 1), Z_ORDER)
        y_place = place_of(((homes[s] >> 3) - y) & (NY - 1), Y_ORDER)
        place_ref[s : s + 1, :] = (y_place * NZ + z_place) * per_home + entries[s]
    n_rows = rows_ref.shape[0]
    choose = jnp.where(iota((N_HOMES * PAIR_ROWS, n_rows), 1) == deal, 1.0, 0.0)
    picks_ref[...] = narrow(dot(narrow(choose), rows_ref[...]))


def leave_kernel(
    panel,
    pos_ref,
    across_ref,
    rows_ref,
    place_ref,
    lower_ref,
    slots_ref,
    leave0_ref,
    leave1_ref,
    leave2_ref,
    leave3_ref,
    passing_ref,
    land_ref,
    flag_ref,
    low_ref,
):
    here = pos_ref[0]
    y, z = here >> 3, here & 7
    odd = (here & 1) == 1
    first_r, second_r = across_ref[0:1, :], across_ref[1:2, :]
    first_c, second_c = upright(first_r), upright(second_r)
    square = (panel, panel)
    number_c, number_r = iota(square, 0), iota(square, 1)
    big = 1 << 20
    seen_r = total(pick(second_c == first_r, big) + pick(number_c + panel == first_r, second_c), 0)
    seen_c = total(pick(first_c == second_r, big) + pick(first_c == number_r + panel, second_r), 1)
    used_r = total(pick(first_c == number_r + panel, 1), 0)
    used_c = total(pick(number_c + panel == first_r, 1), 1)

    def goals(first, second, seen, used, number):
        inner = (first >= panel) & (first < 2 * panel)
        stop = seen & (big - 1)
        goal_first = jnp.where(
            inner,
            jnp.where(stop == first, -1, stop),
            jnp.where((first == number) | (seen >= big), -1, first),
        )
        goal_second = jnp.where((used > 0) | (second == number + panel), -1, second)
        return goal_first, goal_second

    goal_r = goals(first_r, second_r, seen_r, used_r, number_r[0:1, :])
    goal_c = goals(first_c, second_c, seen_c, used_c, number_c[:, 0:1])
    before = number_c < number_r
    lines, line_ranks, dests, dest_ranks, landing = [], [], [], [], []
    worst = jnp.zeros((1, panel), jnp.int32)
    for s in range(2):
        dest_r, local_r = split_rows(goal_r[s], panel)
        dest_r = jnp.where(goal_r[s] < 0, -1, dest_r)
        dest_c = jnp.where(goal_c[s] < 0, -1, split_rows(goal_c[s], panel)[0])
        line_r, line_c = dest_r >> 3, dest_c >> 3
        counts = total(
            pick((dest_c == dest_r) & before, 1024) + pick((line_c == line_r) & before, 1), 0
        )
        line_rank, dest_rank = counts & 1023, counts >> 10
        worst = jnp.maximum(
            worst,
            jnp.where(
                (dest_r >= 0) & ((line_rank >= LINE_ROWS) | (dest_rank >= DEST_ROWS)), 1, 0
            ),
        )
        land_at = jnp.where(dest_r == here, dest_rank, -1)
        landing.append(total(pick(iota((DEST_ROWS, panel), 0) == land_at, local_r + 1), 1) - 1)
        lines.append(line_r)
        line_ranks.append(line_rank)
        dests.append(dest_r)
        dest_ranks.append(dest_rank)
    worst = jnp.maximum(worst, jnp.where(slots_ref[...] >= PAIR_ROWS, 1, 0))
    flag_ref[0] = jnp.max(worst.astype(jnp.float32)).astype(jnp.int32)
    landing = jnp.concatenate(landing).astype(jnp.float32)
    landing = jnp.transpose(jnp.broadcast_to(landing, (2 * DEST_ROWS, 128)))
    land_ref[...] = landing[0:1, :].astype(jnp.int32)
    line = jnp.where(odd, lines[1], lines[0])
    line_rank = jnp.where(odd, line_ranks[1], line_ranks[0])
    dest = jnp.where(odd, dests[1], dests[0])
    dest_rank = jnp.where(odd, dest_ranks[1], dest_ranks[0])
    send_at = jnp.where(line < 0, -1, line * LINE_ROWS + line_rank)
    choose = jnp.where(iota((NY * LINE_ROWS, panel), 0) == send_at, 1.0, 0.0)
    leaving = narrow(dot(narrow(choose), rows_ref[:panel, :]))
    for k, ref in enumerate((leave0_ref, leave1_ref, leave2_ref, leave3_ref)):
        ref[...] = leaving[k * LINE_ROWS : (k + 1) * LINE_ROWS]
    pass_at = jnp.where(line == y, ((dest - z) & (NZ - 1)) * DEST_ROWS + dest_rank, -1)
    passing_ref[...] = total(
        pick(iota((NZ * DEST_ROWS, panel), 0) == pass_at, line_rank), 1
    )
    for s in range(2):
        order = narrow(jnp.where(number_c == place_ref[s : s + 1, :], 1.0, 0.0))
        low_ref[s] = narrow(
            lax.dot_general(
                lower_ref[s], order, (((1,), (1,)), ((), ())), preferred_element_type=jnp.float32
            )
        )


def block_kernel(keep_ref, dealt_ref, block_ref):
    n = dealt_ref.shape[0]
    choose = jnp.where(keep_ref[...] == iota((keep_ref.shape[0], n), 1), 1.0, 0.0)
    block_ref[...] = narrow(dot(narrow(choose), dealt_ref[...]))


def pair_kernel(block_ref, lo_ref, hi_ref, pair_lo_ref, pair_hi_ref):
    n = block_ref.shape[0]
    pair_lo_ref[:n, :] = block_ref[...]
    pair_lo_ref[n:, :] = lo_ref[...]
    pair_hi_ref[:n, :] = block_ref[...]
    pair_hi_ref[n:, :] = hi_ref[...]


def line_kernel(
    pos_ref, block_ref, lo_ref, hi_ref, opposite_ref, two_lo_ref, two_hi_ref, line_ref, extra_ref
):
    n = block_ref.shape[0]
    half = n // 2
    blocks = [block_ref[...], lo_ref[...], hi_ref[...], opposite_ref[...]]
    blocks += [two_lo_ref[:n, :], two_lo_ref[n:, :], two_hi_ref[:n, :], two_hi_ref[n:, :]]
    for k, value in enumerate(blocks):
        line_ref[k * half : (k + 1) * half, :] = value[:half]
        line_ref[(NZ + k) * half : (NZ + k + 1) * half, :] = value[half:]
    even = (pos_ref[1] & 1) == 0
    n, width = extra_ref.shape
    extra_ref[...] = jnp.where(even, line_ref[n:, :width], line_ref[:n, :width])


def by_x(x, at_0, at_1, at_2, at_3):
    return jnp.where(x <= 1, jnp.where(x == 0, at_0, at_1), jnp.where(x == 2, at_2, at_3))


def turn_kernel(pos_ref, *refs):
    own, got, outs, sems = refs[:4], refs[4:8], refs[8:12], refs[12]
    x = pos_ref[1] >> 1

    def pass_on(sources, first):
        copies = [
            pltpu.make_async_copy(source, outs[first + k], sems.at[first + k])
            for k, source in enumerate(sources)
        ]
        for copy in copies:
            copy.start()
        for copy in copies:
            copy.wait()

    @pl.when(x == 0)
    def _():
        pass_on((*own[2:], *own[:2]), 0)

    @pl.when(x == 1)
    def _():
        pass_on(got[:2], 0)

    @pl.when(x == 3)
    def _():
        pass_on(got[2:], 2)


def part_kernel(pos_ref, own_ref, *refs):
    got, up, down, part_ref = refs[:4], refs[4:6], refs[6:8], refs[8]
    x = pos_ref[1] >> 1
    n = got[0].shape[0]

    @pl.when(x == 0)
    def _():
        part_ref[...] = own_ref[:, : part_ref.shape[1]]

    for place, sources in ((1, (*got[:2], *up)), (2, (*up, *down)), (3, (*down, *got[2:]))):

        @pl.when(x == place)
        def _(sources=sources):
            for k, source in enumerate(sources):
                part_ref[k * n : (k + 1) * n, :] = source[...]


def spread_kernel(pos_ref, passing_ref, own_ref, one_ref, two_ref, three_ref, keep_ref, send_ref):
    y = pos_ref[0] >> 3
    on_line = by_x(y, own_ref[...], one_ref[...], two_ref[...], three_ref[...])
    n_rows = passing_ref.shape[0]
    choose = jnp.where(passing_ref[...] == iota((n_rows, LINE_ROWS), 1), 1.0, 0.0)
    spread = narrow(dot(narrow(choose), on_line))
    keep_ref[...] = spread[: n_rows // 2]
    send_ref[...] = spread[n_rows // 2 :]


def fold_kernel(bit, pos_ref, kept_ref, came_ref, keep_ref, send_ref):
    n = keep_ref.shape[0]

    @pl.when((pos_ref[0] & bit) == 0)
    def _():
        keep_ref[...] = kept_ref[:n, :]
        send_ref[...] = kept_ref[n:, :]

    @pl.when((pos_ref[0] & bit) != 0)
    def _():
        keep_ref[...] = came_ref[:n, :]
        send_ref[...] = came_ref[n:, :]


def gone_kernel(pos_ref, kept_ref, came_ref, gone_ref, gone_panel_ref):
    n, width = kept_ref.shape[0], gone_panel_ref.shape[1]
    even = (pos_ref[0] & 1) == 0
    kept, came = kept_ref[...], came_ref[...]
    gone_ref[:n, :] = jnp.where(even, kept, came)
    gone_ref[n:, :] = jnp.where(even, came, kept)
    gone_panel_ref[...] = gone_ref[:, :width]


def extra_kernel(pos_ref, own_ref, one_ref, two_ref, three_ref, cross_ref):
    x = pos_ref[1] >> 1
    cross_ref[...] = by_x(x, own_ref[...], one_ref[...], two_ref[...], three_ref[...])


def cross_kernel(pos_ref, c0_ref, c1_ref, c2_ref, c3_ref, own_ref, one_ref, two_ref, three_ref, cross_ref):
    n = c0_ref.shape[0]
    for k, ref in enumerate((c0_ref, c1_ref, c2_ref, c3_ref)):
        cross_ref[k * n : (k + 1) * n, :] = ref[...]
    x = pos_ref[1] >> 1
    cross_ref[NY * n :, :] = by_x(x, own_ref[...], one_ref[...], two_ref[...], three_ref[...])


def first_kernel(
    low_ref, y0_ref, y1_ref, y2_ref, far_first_ref, far_second_ref, row_ref, second_ref, a00_ref
):
    quarter = far_first_ref.shape[0]
    y_refs = (y0_ref, y1_ref, y2_ref)
    pivot_first = jnp.concatenate([r[:quarter, :] for r in y_refs] + [far_first_ref[...]])
    row_ref[...] = narrow(dot(low_ref[0], pivot_first))
    a00_ref[...] = pivot_first[:, : a00_ref.shape[1]]
    for k, ref in enumerate(y_refs):
        second_ref[k * quarter : (k + 1) * quarter, :] = ref[quarter:, :]
    second_ref[3 * quarter :, :] = far_second_ref[...]


def finish_kernel(
    panel,
    pos_ref,
    rows_ref,
    part_ref,
    other_ref,
    land_ref,
    gone_ref,
    cross_ref,
    cross_other_ref,
    row_first_ref,
    second_ref,
    a00_ref,
    low_ref,
    upper_ref,
    place_ref,
    out_ref,
    new_ref,
    corner_ref,
    gone_first_ref,
    gone_second_ref,
    top_ref,
):
    step = pl.program_id(0)
    here, column = pos_ref[0], pos_ref[1]
    even = (column & 1) == 0
    width = panel
    bf16 = jnp.bfloat16

    @pl.when(step == 0)
    def _():
        mine, others = cross_ref[...], cross_other_ref[...]
        from_first = jnp.where(even, mine, others)
        from_second = jnp.where(even, others, mine)
        gone_first_ref[...] = from_first[panel:]
        gone_second_ref[...] = from_second[panel:]
        row_first = row_first_ref[...]
        pivot_second = second_ref[...]
        corner_ref[...] = narrow(dot(low_ref[0], from_second[:panel]))
        lower_factor = narrow(dot(from_first[:panel], upper_ref[0]))
        reduced = narrow(pivot_second.astype(jnp.float32) - dot(lower_factor, row_first))
        row_second = narrow(dot(low_ref[1], reduced))
        new_ref[:panel, :] = row_first
        new_ref[panel:, :] = row_second

        @pl.when(here <= 1)
        def _():
            top_ref[...] = jnp.where(here == 0, row_first, row_second)

        @pl.when((here <= 1) & (column <= 1) & (here >= column))
        def _():
            raw = jnp.where(
                here == 0,
                a00_ref[...],
                jnp.where(column == 0, lower_factor, reduced[:, :width]),
            )
            place = jnp.where(here == 0, place_ref[0:1, :], place_ref[1:2, :])
            order = narrow(jnp.where(iota((panel, panel), 0) == place, 1.0, 0.0))
            top_ref[:, :width] = narrow(
                lax.dot_general(
                    order, raw, (((0,), (0,)), ((), ())), preferred_element_type=jnp.float32
                )
            )

    @pl.when(step > 0)
    def _():
        n = rows_ref.shape[0]
        begin = (step - 1) * n
        hits = (iota((n, 2 * DEST_ROWS), 0) + begin) == land_ref[...]
        marks = jnp.where(hits, 1.0, 0.0)
        hit = jnp.sum(marks, axis=1, keepdims=True) > 0.5
        marks = narrow(marks)

        def settle(value, gone):
            return jnp.where(hit, dot(marks, gone), value.astype(jnp.float32))

        mine, others = part_ref[...], other_ref[...]
        panel_first = settle(jnp.where(even, mine, others), gone_first_ref[...])
        panel_second = settle(jnp.where(even, others, mine), gone_second_ref[...])
        factor_first = narrow(dot(narrow(panel_first), upper_ref[0]))
        mid = narrow(panel_second - dot(factor_first, corner_ref[...]))
        factor_second = narrow(dot(mid, upper_ref[1]))
        current = settle(rows_ref[...], gone_ref[...])
        updated = narrow(
            current
            - dot(factor_first, new_ref[:panel, :])
            - dot(factor_second, new_ref[panel:, :])
        )

        def put(half, value):
            out_ref[:, half] = value.reshape(n // GROUP, GROUP, width)

        put(0, updated[:, :width])
        put(1, updated[:, width:])

        @pl.when(column <= 1)
        def _():
            put(0, jnp.where(column == 0, factor_first, factor_second))

        @pl.when((here <= 1) & (begin < panel))
        def _():
            top = top_ref[pl.ds(pl.multiple_of(begin, n), n), :]
            put(0, top[:, :width])
            put(1, top[:, width:])


def whole(shape):
    return pl.BlockSpec(shape, lambda *_: (0,) * len(shape))


def smem():
    return pl.BlockSpec(memory_space=pltpu.SMEM)


def shape(dims, dtype=jnp.bfloat16):
    return jax.ShapeDtypeStruct(dims, dtype)


def local_kernel(body, name, outs, scalars, *arrays):
    return pl.pallas_call(
        body,
        grid=(1,),
        in_specs=[smem() for _ in scalars] + [whole(v.shape) for v in arrays],
        out_specs=[smem() if o.shape == (1,) else whole(o.shape) for o in outs],
        out_shape=outs,
        compiler_params=pltpu.CompilerParams(vmem_limit_bytes=40 * MIB),
        cost_estimate=pl.CostEstimate(flops=0, bytes_accessed=0, transcendentals=0),
        name=name,
    )(*scalars, *arrays)


def after(values, *others):
    return lax.optimization_barrier((values, others))[0]


def per_device(matrix, pivots, lower_inverse, upper_inverse):
    row_blocks, panel, col_blocks, width = matrix.shape
    local_rows, local_cols = row_blocks * panel, col_blocks * width
    here = lax.axis_index("prow")
    column = lax.axis_index("pcol")
    position = jnp.stack([here, column]).astype(jnp.int32)
    rows = matrix.reshape(local_rows, local_cols)
    per_home = panel // N_HOMES
    i32 = jnp.int32

    picks, keep, place, slots = local_kernel(
        functools.partial(deal_kernel, panel),
        "deal",
        [
            shape((N_HOMES * PAIR_ROWS, local_cols)),
            shape((2 * per_home, 1), i32),
            shape((2, panel), i32),
            shape((1, panel), i32),
        ],
        [position],
        pivots,
        rows,
    )
    dealt = lax.all_to_all(picks, "prow", 0, 0, tiled=True)

    piece = local_rows // 4
    pieces = [rows[k * piece : (k + 1) * piece, :width] for k in range(4)]
    got = [
        lax.ppermute(pieces[k], "pcol", move_x([(0, 1) if k < 2 else (0, 3)])) for k in (0, 2)
    ]

    line_shape = shape((LINE_ROWS, local_cols))
    *leaving, passing, land, flag, low = local_kernel(
        functools.partial(leave_kernel, panel),
        "leave",
        [line_shape] * NY
        + [
            shape((NZ * DEST_ROWS, 1), i32),
            shape((1, 2 * DEST_ROWS), i32),
            shape((1,), i32),
            shape((2, panel, panel)),
        ],
        [position],
        pivots,
        rows,
        place,
        lower_inverse,
        slots,
    )
    arrived = [lax.ppermute(leaving[s], "prow", shift_y(s, [0], [0, 1])) for s in (1, 2, 3)]

    dealt = after(dealt, got, passing)
    (block,) = local_kernel(
        block_kernel, "block", [shape((2 * per_home, local_cols))], [], keep, dealt
    )
    from_lo = lax.ppermute(block, "prow", shift_z(1))
    from_hi = lax.ppermute(block, "prow", shift_z(-1))
    opposite = lax.ppermute(block, "prow", shift_z(4))
    quarter_shape = shape((NZ // 2 * DEST_ROWS, local_cols))
    kept, send = local_kernel(
        spread_kernel, "spread", [quarter_shape] * 2, [position], passing, leaving[0], *arrived
    )
    came = lax.ppermute(send, "prow", shift_z(4, [0, 1]))

    late_pieces = after((pieces[1], pieces[3]), block)
    got += [
        lax.ppermute(late_pieces[0], "pcol", move_x([(0, 1)])),
        lax.ppermute(late_pieces[1], "pcol", move_x([(0, 3)])),
    ]

    from_lo, from_hi = after((from_lo, from_hi), got, kept)
    pair_shape = shape((4 * per_home, local_cols))
    pair_lo, pair_hi = local_kernel(
        pair_kernel, "pair", [pair_shape] * 2, [], block, from_lo, from_hi
    )
    two_lo = lax.ppermute(pair_lo, "prow", shift_z(2))
    two_hi = lax.ppermute(pair_hi, "prow", shift_z(-2))

    got = after(got, pair_lo)
    ups_downs = pl.pallas_call(
        turn_kernel,
        in_specs=[smem()] + [pl.BlockSpec(memory_space=pl.ANY)] * 8,
        out_specs=[pl.BlockSpec(memory_space=pl.ANY)] * 4,
        out_shape=[shape((piece, width))] * 4,
        scratch_shapes=[pltpu.SemaphoreType.DMA((4,))],
        cost_estimate=pl.CostEstimate(flops=0, bytes_accessed=0, transcendentals=0),
        name="turn",
    )(position, *pieces, got[0], got[2], got[1], got[3])
    go_up, go_down = move_x([(0, 1), (1, 2)]), move_x([(0, 3), (3, 2)])
    up = [lax.ppermute(ups_downs[0], "pcol", go_up)]
    down = [lax.ppermute(ups_downs[2], "pcol", go_down)]

    two_lo, two_hi = after((two_lo, two_hi), up, down, came)
    half = panel // NY
    z_line, extra = local_kernel(
        line_kernel,
        "line",
        [shape((2 * half, local_cols)), shape((half, width))],
        [position],
        block,
        from_lo,
        from_hi,
        opposite,
        two_lo,
        two_hi,
    )
    y_lo = lax.ppermute(z_line, "prow", shift_y(1))
    y_hi = lax.ppermute(z_line, "prow", shift_y(-1))
    sent = [lax.ppermute(extra, "pcol", move_x([(0, k)])) for k in (1, 2, 3)]
    late_up, late_down = after((ups_downs[1], ups_downs[3]), extra)
    up.append(lax.ppermute(late_up, "pcol", go_up))
    down.append(lax.ppermute(late_down, "pcol", go_down))
    eighth_shape = shape((NZ // 4 * DEST_ROWS, local_cols))
    kept, send = local_kernel(
        functools.partial(fold_kernel, 4),
        "fold4",
        [eighth_shape] * 2,
        [position],
        kept,
        after(came, extra),
    )
    came = lax.ppermute(send, "prow", shift_z(2, [0, 1, 4, 5]))
    one_shape = shape((DEST_ROWS, local_cols))
    kept, send = local_kernel(
        functools.partial(fold_kernel, 2), "fold2", [one_shape] * 2, [position], kept, came
    )
    came = lax.ppermute(send, "prow", shift_z(1))

    y_lo, y_hi = after((y_lo, y_hi), sent, up, down, came)
    far_first = lax.ppermute(y_lo[:half], "prow", shift_y(1))
    far_second = lax.ppermute(y_hi[half:], "prow", shift_y(-1))
    (cross,) = local_kernel(
        extra_kernel, "extra", [shape((half, width))], [position], extra, *sent
    )
    crossed = [lax.ppermute(cross, "prow", shift_y(s)) for s in (1, -1, 2)]
    n_gone = 2 * DEST_ROWS
    gone, gone_panel = local_kernel(
        gone_kernel,
        "gone",
        [shape((n_gone, local_cols)), shape((n_gone, width))],
        [position],
        kept,
        came,
    )
    gone_sent = [lax.ppermute(gone_panel, "pcol", move_x([(0, k)])) for k in (1, 2, 3)]
    (part,) = local_kernel(
        part_kernel,
        "part",
        [shape((local_rows, width))],
        [position],
        rows,
        *after((got[0], got[2], got[1], got[3]), y_lo),
        *up,
        *down,
    )
    other = lax.ppermute(part, "pcol", SWAP)

    crossed = after(crossed, far_first, far_second, other)
    (cross,) = local_kernel(
        cross_kernel,
        "cross",
        [shape((panel + n_gone, width))],
        [position],
        cross,
        *crossed,
        gone_panel,
        *gone_sent,
    )
    cross_other = lax.ppermute(cross, "pcol", SWAP)
    row_first, second, a00 = pl.pallas_call(
        first_kernel,
        grid=(1,),
        in_specs=[whole((2, panel, panel))]
        + [whole((2 * half, local_cols))] * 3
        + [whole((half, local_cols))] * 2,
        out_specs=[whole((panel, local_cols))] * 2 + [whole((panel, width))],
        out_shape=[shape((panel, local_cols))] * 2 + [shape((panel, width))],
        compiler_params=pltpu.CompilerParams(vmem_limit_bytes=40 * MIB),
        cost_estimate=pl.CostEstimate(
            flops=2 * panel * panel * local_cols, bytes_accessed=8 * MIB, transcendentals=0
        ),
        name="first",
    )(low, z_line, y_lo, y_hi, far_first, far_second)

    n_block = panel // 2
    steps = local_rows // n_block

    def row_block(cols):
        return pl.BlockSpec((n_block, cols), lambda i: (jnp.maximum(i - 1, 0), 0))

    result = pl.pallas_call(
        functools.partial(finish_kernel, panel),
        grid=(steps + 1,),
        in_specs=[
            smem(),
            row_block(local_cols),
            row_block(width),
            row_block(width),
            whole((1, 2 * DEST_ROWS)),
            whole((2 * DEST_ROWS, local_cols)),
            whole((panel + 2 * DEST_ROWS, width)),
            whole((panel + 2 * DEST_ROWS, width)),
            whole((panel, local_cols)),
            whole((panel, local_cols)),
            whole((panel, width)),
            whole((2, panel, panel)),
            whole((2, panel, panel)),
            whole((2, panel)),
        ],
        out_specs=pl.BlockSpec(
            (n_block // GROUP, 2, GROUP, width), lambda i: (jnp.maximum(i - 1, 0), 0, 0, 0)
        ),
        out_shape=shape((local_rows // GROUP, 2, GROUP, width)),
        scratch_shapes=[
            pltpu.VMEM((2 * panel, local_cols), jnp.bfloat16),
            pltpu.VMEM((panel, width), jnp.bfloat16),
            pltpu.VMEM((2 * DEST_ROWS, width), jnp.bfloat16),
            pltpu.VMEM((2 * DEST_ROWS, width), jnp.bfloat16),
            pltpu.VMEM((panel, local_cols), jnp.bfloat16),
        ],
        compiler_params=pltpu.CompilerParams(vmem_limit_bytes=40 * MIB),
        name="finish",
    )(position, rows, part, other, land, gone, cross, cross_other, row_first, second, a00, low, upper_inverse, place)
    result = result.transpose(0, 2, 1, 3).reshape(matrix.shape)
    return lax.cond(
        flag[0] > 0,
        lambda a, *rest: general_steps(*rest),
        lambda a, *rest: a,
        result,
        matrix,
        pivots,
        lower_inverse,
        upper_inverse,
    )


def solution(mesh):
    return jax.shard_map(
        per_device,
        mesh=mesh,
        in_specs=(P(None, "prow", None, "pcol"), P(), P(), P()),
        out_specs=P(None, "prow", None, "pcol"),
        check_vma=False,
    )
```

```python
import functools

import jax
import jax.numpy as jnp
from jax import lax
from jax.experimental import pallas as pl
from jax.experimental.pallas import tpu as pltpu
from jax.sharding import PartitionSpec as P

NY, NZ, NX, NC = 4, 8, 4, 2
N_HOMES = NY * NZ
PAIR_ROWS = 8
DEST_ROWS = 32
LINE_ROWS = 144
Z_ORDER = (0, 7, 1, 4, 6, 5, 2, 3)
Y_ORDER = (0, 3, 1, 2)
MIB = 1 << 20


def shift_y(step, rows=range(NY), cols=range(NZ)):
    return [(y * NZ + z, (y + step) % NY * NZ + z) for y in rows for z in cols]


def shift_z(step, cols=range(NZ)):
    return [(y * NZ + z, y * NZ + (z + step) % NZ) for y in range(NY) for z in cols]


def move_x(pairs):
    return [(a * NC + core, b * NC + core) for a, b in pairs for core in range(NC)]


SWAP = [(x * NC + core, x * NC + 1 - core) for x in range(NX) for core in range(NC)]


def broadcast(value, axis, root):
    mine = lax.axis_index(axis) == root
    return lax.psum(jnp.where(mine, value, jnp.zeros_like(value)), axis)


def locate(pivot_list, panel, prow_size, prow_here):
    block_index = pivot_list // panel
    owned_rows = block_index % prow_size == prow_here
    local_row = block_index // prow_size * panel + pivot_list % panel
    return (owned_rows, local_row)


def general_steps(matrix, pivots, lower_inverse, upper_inverse):
    row_blocks = matrix.shape[0]
    panel = matrix.shape[1]
    col_blocks = matrix.shape[2]
    prow_size = lax.axis_size("prow")
    pcol_size = lax.axis_size("pcol")
    prow_here = lax.axis_index("prow")
    pcol_here = lax.axis_index("pcol")
    local_rows = row_blocks * panel
    local_cols = col_blocks * panel
    current = matrix.reshape(local_rows, local_cols)
    row_global = jnp.repeat(jnp.arange(row_blocks, dtype=jnp.int32) * prow_size + prow_here, panel)
    col_global = jnp.repeat(jnp.arange(col_blocks, dtype=jnp.int32) * pcol_size + pcol_here, panel)
    offsets = jnp.arange(panel, dtype=jnp.int32)
    bf_zero = jnp.zeros((), jnp.bfloat16)
    def one_panel(panel_index, current):
        root_row, root_col = panel_index, panel_index
        diag_local = panel_local = 0
        pivot_list = pivots[panel_index]
        owned_rows, local_row = locate(pivot_list, panel, prow_size, prow_here)
        safe_rows = jnp.where(owned_rows, local_row, 0)
        picked = jnp.where(owned_rows[:, None], current[safe_rows], bf_zero)
        is_root = prow_here == root_row
        previous = current[diag_local : diag_local + panel]
        right_cols = col_global > panel_index
        displaced = broadcast(previous, "prow", root_row)
        gathered = lax.psum(picked, "prow").astype(jnp.float32)
        pivot_block = gathered.astype(jnp.bfloat16)
        product = jnp.dot(
            lower_inverse[panel_index], pivot_block, preferred_element_type=jnp.float32
        ).astype(jnp.bfloat16)
        new_row = jnp.where(right_cols[None, :], product, pivot_block)
        moved_rows = owned_rows & (pivot_list != panel_index * panel + offsets)
        targets = jnp.where(moved_rows, local_row, local_rows)
        current = current.at[targets].set(displaced, mode="drop")
        below_mask = row_global > panel_index
        panel_part = current[:, panel_local : panel_local + panel]
        upper_block = upper_inverse[panel_index]

        def factor(columns):
            result = jnp.dot(columns, upper_block, preferred_element_type=jnp.float32).astype(
                jnp.bfloat16
            )
            return jnp.where(below_mask[:, None], result, jnp.zeros((), jnp.bfloat16))

        def nothing(columns):
            return jnp.zeros((local_rows, panel), jnp.bfloat16)

        factors = lax.cond(pcol_here == root_col, factor, nothing, panel_part)
        factors = broadcast(factors, "pcol", root_col)
        update_rows = jnp.where(right_cols[None, :], new_row, bf_zero)
        correction = jnp.dot(factors, update_rows, preferred_element_type=jnp.float32)
        updated = (current.astype(jnp.float32) - correction).astype(jnp.bfloat16)
        owner_col = pcol_here == root_col
        new_panel = jnp.where(
            owner_col & below_mask[:, None], factors, updated[:, panel_local : panel_local + panel]
        )
        updated = updated.at[:, panel_local : panel_local + panel].set(new_panel)
        row_block = jnp.where(is_root, new_row, updated[diag_local : diag_local + panel])
        return updated.at[diag_local : diag_local + panel].set(row_block)

    current = lax.fori_loop(0, 2, one_panel, current)
    return current.reshape(matrix.shape)


def dot(a, b):
    return jnp.dot(a, b, preferred_element_type=jnp.float32)


def narrow(value):
    return value.astype(jnp.bfloat16)


def iota(shape, axis):
    return lax.broadcasted_iota(jnp.int32, shape, axis)


def total(mask_or_value, axis):
    return jnp.sum(mask_or_value, axis=axis, keepdims=True).astype(jnp.int32)


def pick(mask, value):
    return jnp.where(mask, value, 0).astype(jnp.float32)


def split_rows(row, panel):
    shift = panel.bit_length() - 1
    block = row >> shift
    return block & (N_HOMES - 1), ((block >> 5) << shift) + (row & (panel - 1))


def upright(row):
    tall = jnp.transpose(jnp.broadcast_to(row.astype(jnp.float32), (8, row.shape[1])))
    return tall[:, 0:1].astype(jnp.int32)


def place_of(step, order):
    result = jnp.zeros_like(step)
    for place, value in enumerate(order):
        result = jnp.where(step == value, place, result)
    return result


def deal_kernel(panel, pos_ref, across_ref, rows_ref, picks_ref, keep_ref, place_ref, flag_ref):
    here = pos_ref[0]
    y, z = here >> 3, here & 7
    first_r, second_r = across_ref[0:1, :], across_ref[1:2, :]
    first_c, second_c = upright(first_r), upright(second_r)
    square = (panel, panel)
    number_c, number_r = iota(square, 0), iota(square, 1)
    came_r = total(pick(first_c == second_r, number_c + 1), 0)
    came_c = total(pick(second_c == first_r, number_r + 1), 1)
    source_r = [first_r, jnp.where(came_r > 0, came_r - 1, second_r)]
    source_c = [first_c, jnp.where(came_c > 0, came_c - 1, second_c)]
    owners_r, locals_r = zip(*[split_rows(s, panel) for s in source_r])
    owners_c = [split_rows(s, panel)[0] for s in source_c]
    before = number_c < number_r
    slots, homes, entries = [], [], []
    for s in range(2):
        counts = total(
            pick((owners_c[s] == owners_r[s]) & before, 1025) + pick(owners_c[s] < owners_r[s], 1), 0
        )
        within, rank = counts >> 10, counts & 1023
        slot = within >> 5
        if s == 1:
            shared = total(pick(owners_c[0] == owners_r[1], 1), 0)
            slot = slot + ((shared + N_HOMES - 1) >> 5)
        slots.append(slot)
        homes.append(rank & (N_HOMES - 1))
        entries.append(rank >> 5)
    flag_ref[...] = jnp.maximum(slots[0], slots[1])
    deal = jnp.zeros((N_HOMES * PAIR_ROWS, 1), jnp.int32)
    position = iota((N_HOMES * PAIR_ROWS, panel), 0)
    per_home = panel // N_HOMES
    for s in range(2):
        at = jnp.where(owners_r[s] == here, homes[s] * PAIR_ROWS + slots[s], -1)
        deal = deal + total(pick(position == at, locals_r[s]), 1)
        kept_at = jnp.where(homes[s] == here, entries[s], -1)
        keep_ref[s * per_home : (s + 1) * per_home, :] = total(
            pick(iota((per_home, panel), 0) == kept_at, owners_r[s] * PAIR_ROWS + slots[s]), 1
        )
        z_place = place_of((homes[s] - z) & (NZ - 1), Z_ORDER)
        y_place = place_of(((homes[s] >> 3) - y) & (NY - 1), Y_ORDER)
        place_ref[s : s + 1, :] = (y_place * NZ + z_place) * per_home + entries[s]
    n_rows = rows_ref.shape[0]
    choose = jnp.where(iota((N_HOMES * PAIR_ROWS, n_rows), 1) == deal, 1.0, 0.0)
    picks_ref[...] = narrow(dot(narrow(choose), rows_ref[...]))


def leave_kernel(
    panel,
    pos_ref,
    across_ref,
    rows_ref,
    place_ref,
    lower_ref,
    slots_ref,
    leave0_ref,
    leave1_ref,
    leave2_ref,
    leave3_ref,
    passing_ref,
    land_ref,
    flag_ref,
    low_ref,
):
    here = pos_ref[0]
    y, z = here >> 3, here & 7
    odd = (here & 1) == 1
    first_r, second_r = across_ref[0:1, :], across_ref[1:2, :]
    first_c, second_c = upright(first_r), upright(second_r)
    square = (panel, panel)
    number_c, number_r = iota(square, 0), iota(square, 1)
    big = 1 << 20
    seen_r = total(pick(second_c == first_r, big) + pick(number_c + panel == first_r, second_c), 0)
    seen_c = total(pick(first_c == second_r, big) + pick(first_c == number_r + panel, second_r), 1)
    used_r = total(pick(first_c == number_r + panel, 1), 0)
    used_c = total(pick(number_c + panel == first_r, 1), 1)

    def goals(first, second, seen, used, number):
        inner = (first >= panel) & (first < 2 * panel)
        stop = seen & (big - 1)
        goal_first = jnp.where(
            inner,
            jnp.where(stop == first, -1, stop),
            jnp.where((first == number) | (seen >= big), -1, first),
        )
        goal_second = jnp.where((used > 0) | (second == number + panel), -1, second)
        return goal_first, goal_second

    goal_r = goals(first_r, second_r, seen_r, used_r, number_r[0:1, :])
    goal_c = goals(first_c, second_c, seen_c, used_c, number_c[:, 0:1])
    before = number_c < number_r
    lines, line_ranks, dests, dest_ranks, landing = [], [], [], [], []
    worst = jnp.zeros((1, panel), jnp.int32)
    for s in range(2):
        dest_r, local_r = split_rows(goal_r[s], panel)
        dest_r = jnp.where(goal_r[s] < 0, -1, dest_r)
        dest_c = jnp.where(goal_c[s] < 0, -1, split_rows(goal_c[s], panel)[0])
        line_r, line_c = dest_r >> 3, dest_c >> 3
        counts = total(
            pick((dest_c == dest_r) & before, 1024) + pick((line_c == line_r) & before, 1), 0
        )
        line_rank, dest_rank = counts & 1023, counts >> 10
        worst = jnp.maximum(
            worst,
            jnp.where(
                (dest_r >= 0) & ((line_rank >= LINE_ROWS) | (dest_rank >= DEST_ROWS)), 1, 0
            ),
        )
        land_at = jnp.where(dest_r == here, dest_rank, -1)
        landing.append(total(pick(iota((DEST_ROWS, panel), 0) == land_at, local_r + 1), 1) - 1)
        lines.append(line_r)
        line_ranks.append(line_rank)
        dests.append(dest_r)
        dest_ranks.append(dest_rank)
    worst = jnp.maximum(worst, jnp.where(slots_ref[...] >= PAIR_ROWS, 1, 0))
    flag_ref[0] = jnp.max(worst.astype(jnp.float32)).astype(jnp.int32)
    landing = jnp.concatenate(landing).astype(jnp.float32)
    landing = jnp.transpose(jnp.broadcast_to(landing, (2 * DEST_ROWS, 128)))
    land_ref[...] = landing[0:1, :].astype(jnp.int32)
    line = jnp.where(odd, lines[1], lines[0])
    line_rank = jnp.where(odd, line_ranks[1], line_ranks[0])
    dest = jnp.where(odd, dests[1], dests[0])
    dest_rank = jnp.where(odd, dest_ranks[1], dest_ranks[0])
    send_at = jnp.where(line < 0, -1, line * LINE_ROWS + line_rank)
    choose = jnp.where(iota((NY * LINE_ROWS, panel), 0) == send_at, 1.0, 0.0)
    leaving = narrow(dot(narrow(choose), rows_ref[:panel, :]))
    for k, ref in enumerate((leave0_ref, leave1_ref, leave2_ref, leave3_ref)):
        ref[...] = leaving[k * LINE_ROWS : (k + 1) * LINE_ROWS]
    pass_at = jnp.where(line == y, ((dest - z) & (NZ - 1)) * DEST_ROWS + dest_rank, -1)
    passing_ref[...] = total(
        pick(iota((NZ * DEST_ROWS, panel), 0) == pass_at, line_rank), 1
    )
    for s in range(2):
        order = narrow(jnp.where(number_c == place_ref[s : s + 1, :], 1.0, 0.0))
        low_ref[s] = narrow(
            lax.dot_general(
                lower_ref[s], order, (((1,), (1,)), ((), ())), preferred_element_type=jnp.float32
            )
        )


def block_kernel(keep_ref, dealt_ref, block_ref):
    n = dealt_ref.shape[0]
    choose = jnp.where(keep_ref[...] == iota((keep_ref.shape[0], n), 1), 1.0, 0.0)
    block_ref[...] = narrow(dot(narrow(choose), dealt_ref[...]))


def pair_kernel(block_ref, lo_ref, hi_ref, pair_lo_ref, pair_hi_ref):
    n = block_ref.shape[0]
    pair_lo_ref[:n, :] = block_ref[...]
    pair_lo_ref[n:, :] = lo_ref[...]
    pair_hi_ref[:n, :] = block_ref[...]
    pair_hi_ref[n:, :] = hi_ref[...]


def line_kernel(block_ref, lo_ref, hi_ref, opposite_ref, two_lo_ref, two_hi_ref, line_ref):
    n = block_ref.shape[0]
    half = n // 2
    blocks = [block_ref[...], lo_ref[...], hi_ref[...], opposite_ref[...]]
    blocks += [two_lo_ref[:n, :], two_lo_ref[n:, :], two_hi_ref[:n, :], two_hi_ref[n:, :]]
    for k, value in enumerate(blocks):
        line_ref[k * half : (k + 1) * half, :] = value[:half]
        line_ref[(NZ + k) * half : (NZ + k + 1) * half, :] = value[half:]


def by_x(x, at_0, at_1, at_2, at_3):
    return jnp.where(x <= 1, jnp.where(x == 0, at_0, at_1), jnp.where(x == 2, at_2, at_3))


def choose_kernel(pos_ref, own_ref, one_ref, two_ref, three_ref, out_ref):
    x = pos_ref[1] >> 1
    for place, ref in enumerate((own_ref, one_ref, two_ref, three_ref)):

        @pl.when(x == place)
        def _(ref=ref):
            out_ref[...] = ref[...]


def spread_kernel(pos_ref, passing_ref, own_ref, one_ref, two_ref, three_ref, keep_ref, send_ref):
    y = pos_ref[0] >> 3
    on_line = by_x(y, own_ref[...], one_ref[...], two_ref[...], three_ref[...])
    n_rows = passing_ref.shape[0]
    choose = jnp.where(passing_ref[...] == iota((n_rows, LINE_ROWS), 1), 1.0, 0.0)
    spread = narrow(dot(narrow(choose), on_line))
    keep_ref[...] = spread[: n_rows // 2]
    send_ref[...] = spread[n_rows // 2 :]


def fold_kernel(pos_ref, kept_ref, came_ref, *out_refs):
    for bit, source in ((0, kept_ref), (4, came_ref)):

        @pl.when((pos_ref[0] & 4) == bit)
        def _(source=source):
            for k, ref in enumerate(out_refs):
                ref[...] = source[k * DEST_ROWS : (k + 1) * DEST_ROWS, :]


def gone_kernel(pos_ref, line_ref, *refs):
    landed, gone_ref, extra_ref = refs[:4], refs[4], refs[5]
    width = extra_ref.shape[1]
    half = line_ref.shape[0] // 2
    for s in range(2):
        for k in range(4):

            @pl.when(((pos_ref[0] - s) & 3) == k)
            def _(k=k, s=s):
                gone_ref[s * DEST_ROWS : (s + 1) * DEST_ROWS, :] = landed[k][...]

    even = (pos_ref[1] & 1) == 0
    extra_ref[:half, :] = jnp.where(even, line_ref[half:, :width], line_ref[:half, :width])
    extra_ref[half:, :] = gone_ref[:, :width]


def extra_kernel(pos_ref, own_ref, one_ref, two_ref, three_ref, cross_ref, gone_ref):
    x = pos_ref[1] >> 1
    value = by_x(x, own_ref[...], one_ref[...], two_ref[...], three_ref[...])
    n = cross_ref.shape[0]
    cross_ref[...] = value[:n]
    gone_ref[...] = value[n:]


def part_kernel(pos_ref, mine_ref, before_ref, after_ref, across_ref, part_ref):
    x = pos_ref[1] >> 1
    n = mine_ref.shape[0]
    for step, ref in ((0, mine_ref), (-1, before_ref), (1, after_ref), (2, across_ref)):
        begin = ((x + step) & (NX - 1)) * n
        part_ref[pl.ds(pl.multiple_of(begin, n), n), :] = ref[...]


def cross_kernel(*refs):
    begin = 0
    for ref in refs[:-1]:
        n = ref.shape[0]
        refs[-1][begin : begin + n, :] = ref[...]
        begin += n


def first_kernel(
    low_ref, y0_ref, y1_ref, y2_ref, far_first_ref, far_second_ref, row_ref, second_ref, a00_ref
):
    quarter = far_first_ref.shape[0]
    y_refs = (y0_ref, y1_ref, y2_ref)
    pivot_first = jnp.concatenate([r[:quarter, :] for r in y_refs] + [far_first_ref[...]])
    row_ref[...] = narrow(dot(low_ref[0], pivot_first))
    a00_ref[...] = pivot_first[:, : a00_ref.shape[1]]
    for k, ref in enumerate(y_refs):
        second_ref[k * quarter : (k + 1) * quarter, :] = ref[quarter:, :]
    second_ref[3 * quarter :, :] = far_second_ref[...]


def finish_kernel(
    panel,
    pos_ref,
    rows_ref,
    part_ref,
    other_ref,
    land_ref,
    gone_ref,
    cross_ref,
    cross_other_ref,
    row_first_ref,
    second_ref,
    a00_ref,
    low_ref,
    upper_ref,
    place_ref,
    out_ref,
    new_ref,
    corner_ref,
    gone_first_ref,
    gone_second_ref,
    top_ref,
):
    step = pl.program_id(0)
    here, column = pos_ref[0], pos_ref[1]
    even = (column & 1) == 0
    width = panel
    bf16 = jnp.bfloat16

    @pl.when(step == 0)
    def _():
        mine, others = cross_ref[...], cross_other_ref[...]
        from_first = jnp.where(even, mine, others)
        from_second = jnp.where(even, others, mine)
        gone_first_ref[...] = from_first[panel:]
        gone_second_ref[...] = from_second[panel:]
        row_first = row_first_ref[...]
        pivot_second = second_ref[...]
        corner_ref[...] = narrow(dot(low_ref[0], from_second[:panel]))
        lower_factor = narrow(dot(from_first[:panel], upper_ref[0]))
        reduced = narrow(pivot_second.astype(jnp.float32) - dot(lower_factor, row_first))
        row_second = narrow(dot(low_ref[1], reduced))
        new_ref[:panel, :] = row_first
        new_ref[panel:, :] = row_second

        @pl.when(here <= 1)
        def _():
            top_ref[...] = jnp.where(here == 0, row_first, row_second)

        @pl.when((here <= 1) & (column <= 1) & (here >= column))
        def _():
            raw = jnp.where(
                here == 0,
                a00_ref[...],
                jnp.where(column == 0, lower_factor, reduced[:, :width]),
            )
            place = jnp.where(here == 0, place_ref[0:1, :], place_ref[1:2, :])
            order = narrow(jnp.where(iota((panel, panel), 0) == place, 1.0, 0.0))
            top_ref[:, :width] = narrow(
                lax.dot_general(
                    order, raw, (((0,), (0,)), ((), ())), preferred_element_type=jnp.float32
                )
            )

    @pl.when(step > 0)
    def _():
        n = rows_ref.shape[0]
        begin = (step - 1) * n
        hits = (iota((n, 2 * DEST_ROWS), 0) + begin) == land_ref[...]
        marks = jnp.where(hits, 1.0, 0.0)
        hit = jnp.sum(marks, axis=1, keepdims=True) > 0.5
        marks = narrow(marks)

        def settle(value, gone):
            return jnp.where(hit, dot(marks, gone), value.astype(jnp.float32))

        mine, others = part_ref[...], other_ref[...]
        panel_first = settle(jnp.where(even, mine, others), gone_first_ref[...])
        panel_second = settle(jnp.where(even, others, mine), gone_second_ref[...])
        factor_first = narrow(dot(narrow(panel_first), upper_ref[0]))
        mid = narrow(panel_second - dot(factor_first, corner_ref[...]))
        factor_second = narrow(dot(mid, upper_ref[1]))
        current = settle(rows_ref[...], gone_ref[...])
        updated = narrow(
            current
            - dot(factor_first, new_ref[:panel, :])
            - dot(factor_second, new_ref[panel:, :])
        )
        out_ref[...] = updated

        @pl.when(column <= 1)
        def _():
            out_ref[:, :width] = jnp.where(column == 0, factor_first, factor_second)

        @pl.when((here <= 1) & (begin < panel))
        def _():
            out_ref[...] = top_ref[pl.ds(pl.multiple_of(begin, n), n), :]


def whole(shape):
    return pl.BlockSpec(shape, lambda *_: (0,) * len(shape))


def smem():
    return pl.BlockSpec(memory_space=pltpu.SMEM)


def shape(dims, dtype=jnp.bfloat16):
    return jax.ShapeDtypeStruct(dims, dtype)


def local_kernel(body, name, outs, scalars, *arrays, limit=12):
    return pl.pallas_call(
        body,
        grid=(1,),
        in_specs=[smem() for _ in scalars] + [whole(v.shape) for v in arrays],
        out_specs=[smem() if o.shape == (1,) else whole(o.shape) for o in outs],
        out_shape=outs,
        compiler_params=pltpu.CompilerParams(vmem_limit_bytes=limit * MIB),
        cost_estimate=pl.CostEstimate(flops=0, bytes_accessed=0, transcendentals=0),
        name=name,
    )(*scalars, *arrays)


def after(values, *others):
    return lax.optimization_barrier((values, others))[0]


def per_device(matrix, pivots, lower_inverse, upper_inverse):
    row_blocks, panel, col_blocks, width = matrix.shape
    local_rows, local_cols = row_blocks * panel, col_blocks * width
    here = lax.axis_index("prow")
    column = lax.axis_index("pcol")
    position = jnp.stack([here, column]).astype(jnp.int32)
    rows = matrix.reshape(local_rows, local_cols)
    per_home = panel // N_HOMES
    i32 = jnp.int32

    picks, keep, place, slots = local_kernel(
        functools.partial(deal_kernel, panel),
        "deal",
        [
            shape((N_HOMES * PAIR_ROWS, local_cols)),
            shape((2 * per_home, 1), i32),
            shape((2, panel), i32),
            shape((1, panel), i32),
        ],
        [position],
        pivots,
        rows,
        limit=32,
    )
    dealt = lax.all_to_all(picks, "prow", 0, 0, tiled=True)

    quarter = local_rows // NX
    own = [rows[k * quarter : (k + 1) * quarter, :width] for k in range(NX)]
    got = [lax.ppermute(own[k], "pcol", move_x([(0, k)])) for k in range(1, NX)]
    (mine,) = local_kernel(
        choose_kernel, "choose", [shape((quarter, width))], [position], own[0], *got
    )

    line_shape = shape((LINE_ROWS, local_cols))
    *leaving, passing, land, flag, low = local_kernel(
        functools.partial(leave_kernel, panel),
        "leave",
        [line_shape]
        + [pltpu.HBM(line_shape.shape, line_shape.dtype)] * (NY - 1)
        + [
            shape((NZ * DEST_ROWS, 1), i32),
            shape((1, 2 * DEST_ROWS), i32),
            shape((1,), i32),
            shape((2, panel, panel)),
        ],
        [position],
        pivots,
        rows,
        place,
        lower_inverse,
        slots,
        limit=32,
    )
    arrived = [lax.ppermute(leaving[s], "prow", shift_y(s, [0], [0, 1])) for s in (1, 2, 3)]

    (block,) = local_kernel(
        block_kernel, "block", [shape((2 * per_home, local_cols))], [], keep, dealt
    )
    from_lo = lax.ppermute(block, "prow", shift_z(1))
    from_hi = lax.ppermute(block, "prow", shift_z(-1))
    opposite = lax.ppermute(block, "prow", shift_z(4))
    quarter_shape = shape((NZ // 2 * DEST_ROWS, local_cols))
    kept, send = local_kernel(
        spread_kernel, "spread", [quarter_shape] * 2, [position], passing, leaving[0], *arrived
    )
    came = lax.ppermute(send, "prow", shift_z(4, [0, 1]))

    from_lo, from_hi = after((from_lo, from_hi), came, mine)
    pair_shape = shape((4 * per_home, local_cols))
    pair_lo, pair_hi = local_kernel(
        pair_kernel, "pair", [pair_shape] * 2, [], block, from_lo, from_hi
    )
    two_lo = lax.ppermute(pair_lo, "prow", shift_z(2))
    two_hi = lax.ppermute(pair_hi, "prow", shift_z(-2))
    one_shape = shape((DEST_ROWS, local_cols))
    spread = local_kernel(
        fold_kernel, "fold", [one_shape] * 4, [position], kept, after(came, pair_lo)
    )
    landed = [spread[0]] + [
        lax.ppermute(spread[k], "prow", shift_z(k, [0, 1, 4, 5])) for k in (1, 2, 3)
    ]
    quarter_out = after(mine, pair_lo)
    ring = [(x, (x + 1) % NX) for x in range(NX)]
    before = lax.ppermute(quarter_out, "pcol", move_x(ring))
    behind = lax.ppermute(quarter_out, "pcol", move_x([(b, a) for a, b in ring]))

    two_lo, two_hi, opposite = after((two_lo, two_hi, opposite), before, behind, landed)
    half = panel // NY
    n_gone = 2 * DEST_ROWS
    (z_line,) = local_kernel(
        line_kernel,
        "line",
        [shape((2 * half, local_cols))],
        [],
        block,
        from_lo,
        from_hi,
        opposite,
        two_lo,
        two_hi,
    )
    y_lo = lax.ppermute(z_line, "prow", shift_y(1))
    y_hi = lax.ppermute(z_line, "prow", shift_y(-1))
    gone, extra = local_kernel(
        gone_kernel,
        "gone",
        [shape((n_gone, local_cols)), shape((half + n_gone, width))],
        [position],
        z_line,
        *landed,
    )
    sent = [lax.ppermute(extra, "pcol", move_x([(0, k)])) for k in (1, 2, 3)]
    across = lax.ppermute(
        after(mine, z_line), "pcol", move_x([(x, (x + 2) % NX) for x in range(NX)])
    )

    y_lo, y_hi = after((y_lo, y_hi), sent, across)
    far_first = lax.ppermute(y_lo[:half], "prow", shift_y(1))
    far_second = lax.ppermute(y_hi[half:], "prow", shift_y(-1))
    cross, gone_panel = local_kernel(
        extra_kernel,
        "extra",
        [shape((half, width)), shape((n_gone, width))],
        [position],
        extra,
        *sent,
    )
    crossed = [lax.ppermute(cross, "prow", shift_y(s)) for s in (1, -1, 2)]
    (part,) = local_kernel(
        part_kernel,
        "part",
        [shape((local_rows, width))],
        [position],
        mine,
        before,
        behind,
        after(across, y_lo),
    )
    other = lax.ppermute(part, "pcol", SWAP)

    crossed = after(crossed, far_first, far_second, other)
    (cross,) = local_kernel(
        cross_kernel,
        "cross",
        [shape((panel + n_gone, width))],
        [],
        cross,
        *crossed,
        gone_panel,
    )
    cross_other = lax.ppermute(cross, "pcol", SWAP)
    row_first, second, a00 = pl.pallas_call(
        first_kernel,
        grid=(1,),
        in_specs=[whole((2, panel, panel))]
        + [whole((2 * half, local_cols))] * 3
        + [whole((half, local_cols))] * 2,
        out_specs=[whole((panel, local_cols))] * 2 + [whole((panel, width))],
        out_shape=[shape((panel, local_cols))] * 2 + [shape((panel, width))],
        compiler_params=pltpu.CompilerParams(vmem_limit_bytes=40 * MIB),
        cost_estimate=pl.CostEstimate(
            flops=2 * panel * panel * local_cols, bytes_accessed=8 * MIB, transcendentals=0
        ),
        name="first",
    )(low, z_line, y_lo, y_hi, far_first, far_second)

    n_block = panel // 2
    steps = local_rows // n_block

    def row_block(cols):
        return pl.BlockSpec((n_block, cols), lambda i: (jnp.maximum(i - 1, 0), 0))

    result = pl.pallas_call(
        functools.partial(finish_kernel, panel),
        grid=(steps + 1,),
        in_specs=[
            smem(),
            row_block(local_cols),
            row_block(width),
            row_block(width),
            whole((1, 2 * DEST_ROWS)),
            whole((2 * DEST_ROWS, local_cols)),
            whole((panel + 2 * DEST_ROWS, width)),
            whole((panel + 2 * DEST_ROWS, width)),
            whole((panel, local_cols)),
            whole((panel, local_cols)),
            whole((panel, width)),
            whole((2, panel, panel)),
            whole((2, panel, panel)),
            whole((2, panel)),
        ],
        out_specs=row_block(local_cols),
        out_shape=shape((local_rows, local_cols)),
        scratch_shapes=[
            pltpu.VMEM((2 * panel, local_cols), jnp.bfloat16),
            pltpu.VMEM((panel, width), jnp.bfloat16),
            pltpu.VMEM((2 * DEST_ROWS, width), jnp.bfloat16),
            pltpu.VMEM((2 * DEST_ROWS, width), jnp.bfloat16),
            pltpu.VMEM((panel, local_cols), jnp.bfloat16),
        ],
        compiler_params=pltpu.CompilerParams(vmem_limit_bytes=32 * MIB),
        name="finish",
    )(position, rows, part, other, land, gone, cross, cross_other, row_first, second, a00, low, upper_inverse, place)
    result = result.reshape(matrix.shape)
    return lax.cond(
        flag[0] > 0,
        lambda a, *rest: general_steps(*rest),
        lambda a, *rest: a,
        result,
        matrix,
        pivots,
        lower_inverse,
        upper_inverse,
    )


def solution(mesh):
    return jax.shard_map(
        per_device,
        mesh=mesh,
        in_specs=(P(None, "prow", None, "pcol"), P(), P(), P()),
        out_specs=P(None, "prow", None, "pcol"),
        check_vma=False,
    )
```

```python
import functools

import jax
import jax.numpy as jnp
from jax import lax
from jax.experimental import pallas as pl
from jax.experimental.pallas import tpu as pltpu
from jax.sharding import PartitionSpec as P

NY, NZ, NX, NC = 4, 8, 4, 2
N_HOMES = NY * NZ
PAIR_ROWS = 8
DEST_ROWS = 32
LINE_ROWS = 80
Z_ORDER = (0, 7, 1, 4, 6, 5, 2, 3)
Y_ORDER = (0, 3, 1, 2)
MIB = 1 << 20


def shift_y(step, rows=range(NY), cols=range(NZ)):
    return [(y * NZ + z, (y + step) % NY * NZ + z) for y in rows for z in cols]


def shift_z(step, cols=range(NZ)):
    return [(y * NZ + z, y * NZ + (z + step) % NZ) for y in range(NY) for z in cols]


def move_x(pairs):
    return [(a * NC + core, b * NC + core) for a, b in pairs for core in range(NC)]


SWAP = [(x * NC + core, x * NC + 1 - core) for x in range(NX) for core in range(NC)]


def broadcast(value, axis, root):
    mine = lax.axis_index(axis) == root
    return lax.psum(jnp.where(mine, value, jnp.zeros_like(value)), axis)


def locate(pivot_list, panel, prow_size, prow_here):
    block_index = pivot_list // panel
    owned_rows = block_index % prow_size == prow_here
    local_row = block_index // prow_size * panel + pivot_list % panel
    return (owned_rows, local_row)


def general_steps(matrix, pivots, lower_inverse, upper_inverse):
    row_blocks = matrix.shape[0]
    panel = matrix.shape[1]
    col_blocks = matrix.shape[2]
    prow_size = lax.axis_size("prow")
    pcol_size = lax.axis_size("pcol")
    prow_here = lax.axis_index("prow")
    pcol_here = lax.axis_index("pcol")
    local_rows = row_blocks * panel
    local_cols = col_blocks * panel
    current = matrix.reshape(local_rows, local_cols)
    row_global = jnp.repeat(jnp.arange(row_blocks, dtype=jnp.int32) * prow_size + prow_here, panel)
    col_global = jnp.repeat(jnp.arange(col_blocks, dtype=jnp.int32) * pcol_size + pcol_here, panel)
    offsets = jnp.arange(panel, dtype=jnp.int32)
    bf_zero = jnp.zeros((), jnp.bfloat16)
    def one_panel(panel_index, current):
        root_row, root_col = panel_index, panel_index
        diag_local = panel_local = 0
        pivot_list = pivots[panel_index]
        owned_rows, local_row = locate(pivot_list, panel, prow_size, prow_here)
        safe_rows = jnp.where(owned_rows, local_row, 0)
        picked = jnp.where(owned_rows[:, None], current[safe_rows], bf_zero)
        is_root = prow_here == root_row
        previous = current[diag_local : diag_local + panel]
        right_cols = col_global > panel_index
        displaced = broadcast(previous, "prow", root_row)
        gathered = lax.psum(picked, "prow").astype(jnp.float32)
        pivot_block = gathered.astype(jnp.bfloat16)
        product = jnp.dot(
            lower_inverse[panel_index], pivot_block, preferred_element_type=jnp.float32
        ).astype(jnp.bfloat16)
        new_row = jnp.where(right_cols[None, :], product, pivot_block)
        moved_rows = owned_rows & (pivot_list != panel_index * panel + offsets)
        targets = jnp.where(moved_rows, local_row, local_rows)
        current = current.at[targets].set(displaced, mode="drop")
        below_mask = row_global > panel_index
        panel_part = current[:, panel_local : panel_local + panel]
        upper_block = upper_inverse[panel_index]

        def factor(columns):
            result = jnp.dot(columns, upper_block, preferred_element_type=jnp.float32).astype(
                jnp.bfloat16
            )
            return jnp.where(below_mask[:, None], result, jnp.zeros((), jnp.bfloat16))

        def nothing(columns):
            return jnp.zeros((local_rows, panel), jnp.bfloat16)

        factors = lax.cond(pcol_here == root_col, factor, nothing, panel_part)
        factors = broadcast(factors, "pcol", root_col)
        update_rows = jnp.where(right_cols[None, :], new_row, bf_zero)
        correction = jnp.dot(factors, update_rows, preferred_element_type=jnp.float32)
        updated = (current.astype(jnp.float32) - correction).astype(jnp.bfloat16)
        owner_col = pcol_here == root_col
        new_panel = jnp.where(
            owner_col & below_mask[:, None], factors, updated[:, panel_local : panel_local + panel]
        )
        updated = updated.at[:, panel_local : panel_local + panel].set(new_panel)
        row_block = jnp.where(is_root, new_row, updated[diag_local : diag_local + panel])
        return updated.at[diag_local : diag_local + panel].set(row_block)

    current = lax.fori_loop(0, 2, one_panel, current)
    return current.reshape(matrix.shape)


def dot(a, b):
    return jnp.dot(a, b, preferred_element_type=jnp.float32)


def narrow(value):
    return value.astype(jnp.bfloat16)


def iota(shape, axis):
    return lax.broadcasted_iota(jnp.int32, shape, axis)


def total(mask_or_value, axis):
    return jnp.sum(mask_or_value, axis=axis, keepdims=True).astype(jnp.int32)


def pick(mask, value):
    return jnp.where(mask, value, 0).astype(jnp.float32)


def split_rows(row, panel):
    shift = panel.bit_length() - 1
    block = row >> shift
    return block & (N_HOMES - 1), ((block >> 5) << shift) + (row & (panel - 1))


def upright(row):
    tall = jnp.transpose(jnp.broadcast_to(row.astype(jnp.float32), (8, row.shape[1])))
    return tall[:, 0:1].astype(jnp.int32)


def place_of(step, order):
    result = jnp.zeros_like(step)
    for place, value in enumerate(order):
        result = jnp.where(step == value, place, result)
    return result


def deal_kernel(panel, pos_ref, across_ref, rows_ref, picks_ref, keep_ref, place_ref, flag_ref):
    here = pos_ref[0]
    y, z = here >> 3, here & 7
    first_r, second_r = across_ref[0:1, :], across_ref[1:2, :]
    first_c, second_c = upright(first_r), upright(second_r)
    square = (panel, panel)
    number_c, number_r = iota(square, 0), iota(square, 1)
    came_r = total(pick(first_c == second_r, number_c + 1), 0)
    came_c = total(pick(second_c == first_r, number_r + 1), 1)
    source_r = [first_r, jnp.where(came_r > 0, came_r - 1, second_r)]
    source_c = [first_c, jnp.where(came_c > 0, came_c - 1, second_c)]
    owners_r, locals_r = zip(*[split_rows(s, panel) for s in source_r])
    owners_c = [split_rows(s, panel)[0] for s in source_c]
    before = number_c < number_r
    slots, homes, entries = [], [], []
    for s in range(2):
        counts = total(
            pick((owners_c[s] == owners_r[s]) & before, 1025) + pick(owners_c[s] < owners_r[s], 1), 0
        )
        within, rank = counts >> 10, counts & 1023
        slot = within >> 5
        if s == 1:
            shared = total(pick(owners_c[0] == owners_r[1], 1), 0)
            slot = slot + ((shared + N_HOMES - 1) >> 5)
        slots.append(slot)
        homes.append(rank & (N_HOMES - 1))
        entries.append(rank >> 5)
    flag_ref[...] = jnp.maximum(slots[0], slots[1])
    deal = jnp.zeros((N_HOMES * PAIR_ROWS, 1), jnp.int32)
    position = iota((N_HOMES * PAIR_ROWS, panel), 0)
    per_home = panel // N_HOMES
    for s in range(2):
        at = jnp.where(owners_r[s] == here, homes[s] * PAIR_ROWS + slots[s], -1)
        deal = deal + total(pick(position == at, locals_r[s]), 1)
        kept_at = jnp.where(homes[s] == here, entries[s], -1)
        keep_ref[s * per_home : (s + 1) * per_home, :] = total(
            pick(iota((per_home, panel), 0) == kept_at, owners_r[s] * PAIR_ROWS + slots[s]), 1
        )
        z_place = place_of((homes[s] - z) & (NZ - 1), Z_ORDER)
        y_place = place_of(((homes[s] >> 3) - y) & (NY - 1), Y_ORDER)
        place_ref[s : s + 1, :] = (y_place * NZ + z_place) * per_home + entries[s]
    n_rows = rows_ref.shape[0]
    choose = jnp.where(iota((N_HOMES * PAIR_ROWS, n_rows), 1) == deal, 1.0, 0.0)
    picks_ref[...] = narrow(dot(narrow(choose), rows_ref[...]))


def leave_kernel(
    panel,
    pos_ref,
    across_ref,
    rows_ref,
    place_ref,
    lower_ref,
    slots_ref,
    kept_ref,
    send_ref,
    passing_ref,
    land_ref,
    flag_ref,
    low_ref,
):
    here = pos_ref[0]
    y, z = here >> 3, here & 7
    odd = (here & 1) == 1
    first_r, second_r = across_ref[0:1, :], across_ref[1:2, :]
    first_c, second_c = upright(first_r), upright(second_r)
    square = (panel, panel)
    number_c, number_r = iota(square, 0), iota(square, 1)
    big = 1 << 20
    seen_r = total(pick(second_c == first_r, big) + pick(number_c + panel == first_r, second_c), 0)
    seen_c = total(pick(first_c == second_r, big) + pick(first_c == number_r + panel, second_r), 1)
    used_r = total(pick(first_c == number_r + panel, 1), 0)
    used_c = total(pick(number_c + panel == first_r, 1), 1)

    def goals(first, second, seen, used, number):
        inner = (first >= panel) & (first < 2 * panel)
        stop = seen & (big - 1)
        goal_first = jnp.where(
            inner,
            jnp.where(stop == first, -1, stop),
            jnp.where((first == number) | (seen >= big), -1, first),
        )
        goal_second = jnp.where((used > 0) | (second == number + panel), -1, second)
        return goal_first, goal_second

    goal_r = goals(first_r, second_r, seen_r, used_r, number_r[0:1, :])
    goal_c = goals(first_c, second_c, seen_c, used_c, number_c[:, 0:1])
    before = number_c < number_r
    lines, line_ranks, dests, dest_ranks, landing = [], [], [], [], []
    worst = jnp.zeros((1, panel), jnp.int32)
    for s in range(2):
        dest_r, local_r = split_rows(goal_r[s], panel)
        dest_r = jnp.where(goal_r[s] < 0, -1, dest_r)
        dest_c = jnp.where(goal_c[s] < 0, -1, split_rows(goal_c[s], panel)[0])
        line_r = jnp.where(dest_r < 0, -1, dest_r & (NZ - 1))
        line_c = jnp.where(dest_c < 0, -1, dest_c & (NZ - 1))
        counts = total(
            pick((dest_c == dest_r) & before, 1024) + pick((line_c == line_r) & before, 1), 0
        )
        line_rank, dest_rank = counts & 1023, counts >> 10
        worst = jnp.maximum(
            worst,
            jnp.where(
                (dest_r >= 0) & ((line_rank >= LINE_ROWS) | (dest_rank >= DEST_ROWS)), 1, 0
            ),
        )
        land_at = jnp.where(dest_r == here, dest_rank, -1)
        landing.append(total(pick(iota((DEST_ROWS, panel), 0) == land_at, local_r + 1), 1) - 1)
        lines.append(line_r)
        line_ranks.append(line_rank)
        dests.append(dest_r)
        dest_ranks.append(dest_rank)
    worst = jnp.maximum(worst, jnp.where(slots_ref[...] >= PAIR_ROWS, 1, 0))
    flag_ref[0] = jnp.max(worst.astype(jnp.float32)).astype(jnp.int32)
    landing = jnp.concatenate(landing).astype(jnp.float32)
    landing = jnp.transpose(jnp.broadcast_to(landing, (2 * DEST_ROWS, 128)))
    land_ref[...] = landing[0:1, :].astype(jnp.int32)
    line = jnp.where(odd, lines[1], lines[0])
    line_rank = jnp.where(odd, line_ranks[1], line_ranks[0])
    send_at = jnp.where(line < 0, -1, ((line - z) & (NZ - 1)) * LINE_ROWS + line_rank)
    choose = jnp.where(iota((NZ * LINE_ROWS, panel), 0) == send_at, 1.0, 0.0)
    leaving = narrow(dot(narrow(choose), rows_ref[:panel, :]))
    kept_ref[...] = leaving[: NZ // 2 * LINE_ROWS]
    send_ref[...] = leaving[NZ // 2 * LINE_ROWS :]
    for s in range(2):
        pass_at = jnp.where(lines[s] == z, (dests[s] >> 3) * DEST_ROWS + dest_ranks[s], -1)
        passing_ref[s * NY * DEST_ROWS : (s + 1) * NY * DEST_ROWS, :] = total(
            pick(iota((NY * DEST_ROWS, panel), 0) == pass_at, line_ranks[s]), 1
        )
    for s in range(2):
        order = narrow(jnp.where(number_c == place_ref[s : s + 1, :], 1.0, 0.0))
        low_ref[s] = narrow(
            lax.dot_general(
                lower_ref[s], order, (((1,), (1,)), ((), ())), preferred_element_type=jnp.float32
            )
        )


def block_kernel(keep_ref, dealt_ref, block_ref):
    n = dealt_ref.shape[0]
    choose = jnp.where(keep_ref[...] == iota((keep_ref.shape[0], n), 1), 1.0, 0.0)
    block_ref[...] = narrow(dot(narrow(choose), dealt_ref[...]))


def pair_kernel(block_ref, lo_ref, hi_ref, pair_lo_ref, pair_hi_ref):
    n = block_ref.shape[0]
    pair_lo_ref[:n, :] = block_ref[...]
    pair_lo_ref[n:, :] = lo_ref[...]
    pair_hi_ref[:n, :] = block_ref[...]
    pair_hi_ref[n:, :] = hi_ref[...]


def line_kernel(block_ref, lo_ref, hi_ref, opposite_ref, two_lo_ref, two_hi_ref, line_ref):
    n = block_ref.shape[0]
    half = n // 2
    blocks = [block_ref[...], lo_ref[...], hi_ref[...], opposite_ref[...]]
    blocks += [two_lo_ref[:n, :], two_lo_ref[n:, :], two_hi_ref[:n, :], two_hi_ref[n:, :]]
    for k, value in enumerate(blocks):
        line_ref[k * half : (k + 1) * half, :] = value[:half]
        line_ref[(NZ + k) * half : (NZ + k + 1) * half, :] = value[half:]


def by_x(x, at_0, at_1, at_2, at_3):
    return jnp.where(x <= 1, jnp.where(x == 0, at_0, at_1), jnp.where(x == 2, at_2, at_3))


def choose_kernel(pos_ref, own_ref, one_ref, two_ref, three_ref, out_ref):
    x = pos_ref[1] >> 1
    for place, ref in enumerate((own_ref, one_ref, two_ref, three_ref)):

        @pl.when(x == place)
        def _(ref=ref):
            out_ref[...] = ref[...]


def fold_kernel(pos_ref, kept_ref, came_ref, *out_refs):
    for bit, source in ((0, kept_ref), (4, came_ref)):

        @pl.when((pos_ref[0] & 4) == bit)
        def _(source=source):
            for k, ref in enumerate(out_refs):
                ref[...] = source[k * LINE_ROWS : (k + 1) * LINE_ROWS, :]


def spread_kernel(pos_ref, passing_ref, r0_ref, r1_ref, r2_ref, r3_ref, *refs):
    out_refs, rows_ref = refs[:NY], refs[NY]
    landed = (r0_ref, r1_ref, r2_ref, r3_ref)
    for s in range(2):
        for k in range(4):

            @pl.when(((pos_ref[0] - s) & 3) == k)
            def _(k=k):
                rows_ref[...] = landed[k][...]

        marks = passing_ref[s * NY * DEST_ROWS : (s + 1) * NY * DEST_ROWS, :]
        choose = jnp.where(marks == iota((NY * DEST_ROWS, LINE_ROWS), 1), 1.0, 0.0)
        spread = narrow(dot(narrow(choose), rows_ref[...]))
        for k, ref in enumerate(out_refs):
            ref[s * DEST_ROWS : (s + 1) * DEST_ROWS, :] = spread[k * DEST_ROWS : (k + 1) * DEST_ROWS]


def gone_kernel(pos_ref, line_ref, y0_ref, y1_ref, y2_ref, y3_ref, gone_ref, extra_ref):
    y = pos_ref[0] >> 3
    width = extra_ref.shape[1]
    half = line_ref.shape[0] // 2
    gone_ref[...] = by_x(y, y0_ref[...], y1_ref[...], y2_ref[...], y3_ref[...])
    even = (pos_ref[1] & 1) == 0
    extra_ref[:half, :] = jnp.where(even, line_ref[half:, :width], line_ref[:half, :width])
    extra_ref[half:, :] = gone_ref[:, :width]


def settle(land_ref, begin, value, gone):
    n = value.shape[0]
    hits = (iota((n, 2 * DEST_ROWS), 0) + begin) == land_ref[...]
    marks = jnp.where(hits, 1.0, 0.0)
    hit = jnp.sum(marks, axis=1, keepdims=True) > 0.5
    return jnp.where(hit, dot(narrow(marks), gone), value.astype(jnp.float32))


def settle_kernel(rows_ref, land_ref, gone_ref, out_ref):
    begin = pl.program_id(0) * rows_ref.shape[0]
    out_ref[...] = narrow(settle(land_ref, begin, rows_ref[...], gone_ref[...]))


def factor_kernel(pos_ref, part_ref, other_ref, upper_ref, out_ref):
    even = (pos_ref[1] & 1) == 0
    out_ref[...] = narrow(
        dot(jnp.where(even, part_ref[...], other_ref[...]), upper_ref[0])
    )


def extra_kernel(pos_ref, own_ref, one_ref, two_ref, three_ref, cross_ref, gone_ref):
    x = pos_ref[1] >> 1
    value = by_x(x, own_ref[...], one_ref[...], two_ref[...], three_ref[...])
    n = cross_ref.shape[0]
    cross_ref[...] = value[:n]
    gone_ref[...] = value[n:]


def part_kernel(pos_ref, mine_ref, before_ref, after_ref, across_ref, part_ref):
    x = pos_ref[1] >> 1
    n = mine_ref.shape[0]
    for step, ref in ((0, mine_ref), (-1, before_ref), (1, after_ref), (2, across_ref)):
        begin = ((x + step) & (NX - 1)) * n
        part_ref[pl.ds(pl.multiple_of(begin, n), n), :] = ref[...]


def cross_kernel(*refs):
    begin = 0
    for ref in refs[:-1]:
        n = ref.shape[0]
        refs[-1][begin : begin + n, :] = ref[...]
        begin += n


def first_kernel(
    low_ref, y0_ref, y1_ref, y2_ref, far_first_ref, far_second_ref, row_ref, second_ref, a00_ref
):
    quarter = far_first_ref.shape[0]
    y_refs = (y0_ref, y1_ref, y2_ref)
    pivot_first = jnp.concatenate([r[:quarter, :] for r in y_refs] + [far_first_ref[...]])
    row_ref[...] = narrow(dot(low_ref[0], pivot_first))
    a00_ref[...] = pivot_first[:, : a00_ref.shape[1]]
    for k, ref in enumerate(y_refs):
        second_ref[k * quarter : (k + 1) * quarter, :] = ref[quarter:, :]
    second_ref[3 * quarter :, :] = far_second_ref[...]


def finish_kernel(
    panel,
    pos_ref,
    rows_ref,
    part_ref,
    other_ref,
    factor_ref,
    land_ref,
    cross_ref,
    cross_other_ref,
    row_first_ref,
    second_ref,
    a00_ref,
    low_ref,
    upper_ref,
    place_ref,
    out_ref,
    new_ref,
    corner_ref,
    gone_first_ref,
    gone_second_ref,
    top_ref,
):
    step = pl.program_id(0)
    here, column = pos_ref[0], pos_ref[1]
    even = (column & 1) == 0
    width = panel
    bf16 = jnp.bfloat16

    @pl.when(step == 0)
    def _():
        mine, others = cross_ref[...], cross_other_ref[...]
        from_first = jnp.where(even, mine, others)
        from_second = jnp.where(even, others, mine)
        gone_first_ref[...] = narrow(dot(from_first[panel:], upper_ref[0]))
        gone_second_ref[...] = from_second[panel:]
        row_first = row_first_ref[...]
        pivot_second = second_ref[...]
        corner_ref[...] = narrow(dot(low_ref[0], from_second[:panel]))
        lower_factor = narrow(dot(from_first[:panel], upper_ref[0]))
        reduced = narrow(pivot_second.astype(jnp.float32) - dot(lower_factor, row_first))
        row_second = narrow(dot(low_ref[1], reduced))
        new_ref[:panel, :] = row_first
        new_ref[panel:, :] = row_second

        @pl.when(here <= 1)
        def _():
            top_ref[...] = jnp.where(here == 0, row_first, row_second)

        @pl.when((here <= 1) & (column <= 1) & (here >= column))
        def _():
            raw = jnp.where(
                here == 0,
                a00_ref[...],
                jnp.where(column == 0, lower_factor, reduced[:, :width]),
            )
            place = jnp.where(here == 0, place_ref[0:1, :], place_ref[1:2, :])
            order = narrow(jnp.where(iota((panel, panel), 0) == place, 1.0, 0.0))
            top_ref[:, :width] = narrow(
                lax.dot_general(
                    order, raw, (((0,), (0,)), ((), ())), preferred_element_type=jnp.float32
                )
            )

    @pl.when(step > 0)
    def _():
        n = rows_ref.shape[0]
        begin = (step - 1) * n
        second = jnp.where(even, other_ref[...], part_ref[...])
        factor_first = narrow(settle(land_ref, begin, factor_ref[...], gone_first_ref[...]))
        panel_second = settle(land_ref, begin, second, gone_second_ref[...])
        mid = narrow(panel_second - dot(factor_first, corner_ref[...]))
        factor_second = narrow(dot(mid, upper_ref[1]))
        current = rows_ref[...].astype(jnp.float32)
        updated = narrow(
            current
            - dot(factor_first, new_ref[:panel, :])
            - dot(factor_second, new_ref[panel:, :])
        )
        out_ref[...] = updated

        @pl.when(column <= 1)
        def _():
            out_ref[:, :width] = jnp.where(column == 0, factor_first, factor_second)

        @pl.when((here <= 1) & (begin < panel))
        def _():
            out_ref[...] = top_ref[pl.ds(pl.multiple_of(begin, n), n), :]


def whole(shape):
    return pl.BlockSpec(shape, lambda *_: (0,) * len(shape))


def smem():
    return pl.BlockSpec(memory_space=pltpu.SMEM)


def shape(dims, dtype=jnp.bfloat16):
    return jax.ShapeDtypeStruct(dims, dtype)


def local_kernel(body, name, outs, scalars, *arrays, limit=12):
    return pl.pallas_call(
        body,
        grid=(1,),
        in_specs=[smem() for _ in scalars] + [whole(v.shape) for v in arrays],
        out_specs=[smem() if o.shape == (1,) else whole(o.shape) for o in outs],
        out_shape=outs,
        compiler_params=pltpu.CompilerParams(vmem_limit_bytes=limit * MIB),
        cost_estimate=pl.CostEstimate(flops=0, bytes_accessed=0, transcendentals=0),
        name=name,
    )(*scalars, *arrays)


def after(values, *others):
    return lax.optimization_barrier((values, others))[0]


def per_device(matrix, pivots, lower_inverse, upper_inverse):
    row_blocks, panel, col_blocks, width = matrix.shape
    local_rows, local_cols = row_blocks * panel, col_blocks * width
    here = lax.axis_index("prow")
    column = lax.axis_index("pcol")
    position = jnp.stack([here, column]).astype(jnp.int32)
    rows = matrix.reshape(local_rows, local_cols)
    per_home = panel // N_HOMES
    i32 = jnp.int32

    picks, keep, place, slots = local_kernel(
        functools.partial(deal_kernel, panel),
        "deal",
        [
            shape((N_HOMES * PAIR_ROWS, local_cols)),
            shape((2 * per_home, 1), i32),
            shape((2, panel), i32),
            shape((1, panel), i32),
        ],
        [position],
        pivots,
        rows,
        limit=32,
    )
    dealt = lax.all_to_all(picks, "prow", 0, 0, tiled=True)

    quarter = local_rows // NX
    own = [rows[k * quarter : (k + 1) * quarter, :width] for k in range(NX)]
    got = [lax.ppermute(own[k], "pcol", move_x([(0, k)])) for k in range(1, NX)]
    zs_shape = shape((NZ // 2 * LINE_ROWS, local_cols))
    kept, send, passing, land, flag, low = local_kernel(
        functools.partial(leave_kernel, panel),
        "leave",
        [
            zs_shape,
            pltpu.HBM(zs_shape.shape, zs_shape.dtype),
            shape((2 * NY * DEST_ROWS, 1), i32),
            shape((1, 2 * DEST_ROWS), i32),
            shape((1,), i32),
            shape((2, panel, panel)),
        ],
        [position],
        pivots,
        rows,
        place,
        lower_inverse,
        slots,
        limit=32,
    )
    came = lax.ppermute(send, "prow", shift_z(4, [0, 1]))

    (block,) = local_kernel(
        block_kernel, "block", [shape((2 * per_home, local_cols))], [], keep, after(dealt, came)
    )
    from_lo = lax.ppermute(block, "prow", shift_z(1))
    from_hi = lax.ppermute(block, "prow", shift_z(-1))
    opposite = lax.ppermute(block, "prow", shift_z(4))
    spread = local_kernel(
        fold_kernel,
        "fold",
        [shape((LINE_ROWS, local_cols))] * 4,
        [position],
        kept,
        after(came, block),
    )
    landed = [spread[0]] + [
        lax.ppermute(spread[k], "prow", shift_z(k, [0, 1, 4, 5])) for k in (1, 2, 3)
    ]

    (mine,) = local_kernel(
        choose_kernel, "choose", [shape((quarter, width))], [position], own[0], *after(got, from_lo, from_hi)
    )

    from_lo, from_hi = after((from_lo, from_hi), landed, mine)
    pair_shape = shape((4 * per_home, local_cols))
    pair_lo, pair_hi = local_kernel(
        pair_kernel, "pair", [pair_shape] * 2, [], block, from_lo, from_hi
    )
    two_lo = lax.ppermute(pair_lo, "prow", shift_z(2))
    two_hi = lax.ppermute(pair_hi, "prow", shift_z(-2))
    n_gone = 2 * DEST_ROWS
    gone_shape = shape((n_gone, local_cols))
    going = pl.pallas_call(
        spread_kernel,
        grid=(1,),
        in_specs=[smem(), whole((2 * NY * DEST_ROWS, 1))] + [whole((LINE_ROWS, local_cols))] * 4,
        out_specs=[whole((n_gone, local_cols))] * NY,
        out_shape=[gone_shape] * NY,
        scratch_shapes=[pltpu.VMEM((LINE_ROWS, local_cols), jnp.bfloat16)],
        compiler_params=pltpu.CompilerParams(vmem_limit_bytes=12 * MIB),
        cost_estimate=pl.CostEstimate(flops=0, bytes_accessed=0, transcendentals=0),
        name="spread",
    )(position, passing, *after(landed, pair_lo))
    ending = [going[0]] + [lax.ppermute(going[k], "prow", shift_y(k, [0])) for k in (1, 2, 3)]
    quarter_out = after(mine, pair_lo)
    ring = [(x, (x + 1) % NX) for x in range(NX)]
    before = lax.ppermute(quarter_out, "pcol", move_x(ring))
    behind = lax.ppermute(quarter_out, "pcol", move_x([(b, a) for a, b in ring]))

    two_lo, two_hi, opposite = after((two_lo, two_hi, opposite), before, behind, ending)
    half = panel // NY
    (z_line,) = local_kernel(
        line_kernel,
        "line",
        [shape((2 * half, local_cols))],
        [],
        block,
        from_lo,
        from_hi,
        opposite,
        two_lo,
        two_hi,
    )
    y_lo = lax.ppermute(z_line, "prow", shift_y(1))
    y_hi = lax.ppermute(z_line, "prow", shift_y(-1))
    gone, extra = local_kernel(
        gone_kernel,
        "gone",
        [gone_shape, shape((half + n_gone, width))],
        [position],
        z_line,
        *ending,
    )
    n_block = panel // 2
    steps = local_rows // n_block

    def block_of(cols, lead=0):
        return pl.BlockSpec((n_block, cols), lambda i: (jnp.maximum(i - lead, 0), 0))

    settled = pl.pallas_call(
        settle_kernel,
        grid=(steps,),
        in_specs=[block_of(local_cols), whole((1, n_gone)), whole((n_gone, local_cols))],
        out_specs=block_of(local_cols),
        out_shape=shape((local_rows, local_cols)),
        compiler_params=pltpu.CompilerParams(vmem_limit_bytes=16 * MIB),
        cost_estimate=pl.CostEstimate(flops=0, bytes_accessed=0, transcendentals=0),
        name="settle",
    )(rows, land, gone)
    sent = [lax.ppermute(extra, "pcol", move_x([(0, k)])) for k in (1, 2, 3)]
    across = lax.ppermute(
        after(mine, z_line), "pcol", move_x([(x, (x + 2) % NX) for x in range(NX)])
    )

    y_lo, y_hi = after((y_lo, y_hi), sent, across, settled)
    far_first = lax.ppermute(y_lo[:half], "prow", shift_y(1))
    far_second = lax.ppermute(y_hi[half:], "prow", shift_y(-1))
    cross, gone_panel = local_kernel(
        extra_kernel,
        "extra",
        [shape((half, width)), shape((n_gone, width))],
        [position],
        extra,
        *sent,
    )
    crossed = [lax.ppermute(cross, "prow", shift_y(s)) for s in (1, -1, 2)]
    (part,) = local_kernel(
        part_kernel,
        "part",
        [shape((local_rows, width))],
        [position],
        mine,
        before,
        behind,
        after(across, y_lo),
    )
    other = lax.ppermute(part, "pcol", SWAP)
    factor_raw = pl.pallas_call(
        factor_kernel,
        grid=(steps,),
        in_specs=[smem(), block_of(width), block_of(width), whole((2, panel, panel))],
        out_specs=block_of(width),
        out_shape=shape((local_rows, width)),
        compiler_params=pltpu.CompilerParams(vmem_limit_bytes=16 * MIB),
        cost_estimate=pl.CostEstimate(flops=0, bytes_accessed=0, transcendentals=0),
        name="factor",
    )(position, part, other, upper_inverse)

    crossed = after(crossed, far_first, far_second, factor_raw)
    (cross,) = local_kernel(
        cross_kernel,
        "cross",
        [shape((panel + n_gone, width))],
        [],
        cross,
        *crossed,
        gone_panel,
    )
    cross_other = lax.ppermute(cross, "pcol", SWAP)
    row_first, second, a00 = pl.pallas_call(
        first_kernel,
        grid=(1,),
        in_specs=[whole((2, panel, panel))]
        + [whole((2 * half, local_cols))] * 3
        + [whole((half, local_cols))] * 2,
        out_specs=[whole((panel, local_cols))] * 2 + [whole((panel, width))],
        out_shape=[shape((panel, local_cols))] * 2 + [shape((panel, width))],
        compiler_params=pltpu.CompilerParams(vmem_limit_bytes=40 * MIB),
        cost_estimate=pl.CostEstimate(
            flops=2 * panel * panel * local_cols, bytes_accessed=8 * MIB, transcendentals=0
        ),
        name="first",
    )(low, z_line, y_lo, y_hi, far_first, far_second)

    result = pl.pallas_call(
        functools.partial(finish_kernel, panel),
        grid=(steps + 1,),
        in_specs=[
            smem(),
            block_of(local_cols, 1),
            block_of(width, 1),
            block_of(width, 1),
            block_of(width, 1),
            whole((1, 2 * DEST_ROWS)),
            whole((panel + 2 * DEST_ROWS, width)),
            whole((panel + 2 * DEST_ROWS, width)),
            whole((panel, local_cols)),
            whole((panel, local_cols)),
            whole((panel, width)),
            whole((2, panel, panel)),
            whole((2, panel, panel)),
            whole((2, panel)),
        ],
        out_specs=block_of(local_cols, 1),
        out_shape=shape((local_rows, local_cols)),
        scratch_shapes=[
            pltpu.VMEM((2 * panel, local_cols), jnp.bfloat16),
            pltpu.VMEM((panel, width), jnp.bfloat16),
            pltpu.VMEM((2 * DEST_ROWS, width), jnp.bfloat16),
            pltpu.VMEM((2 * DEST_ROWS, width), jnp.bfloat16),
            pltpu.VMEM((panel, local_cols), jnp.bfloat16),
        ],
        compiler_params=pltpu.CompilerParams(vmem_limit_bytes=32 * MIB),
        name="finish",
    )(position, settled, part, other, factor_raw, land, cross, cross_other, row_first, second, a00, low, upper_inverse, place)
    result = result.reshape(matrix.shape)
    return lax.cond(
        flag[0] > 0,
        lambda a, *rest: general_steps(*rest),
        lambda a, *rest: a,
        result,
        matrix,
        pivots,
        lower_inverse,
        upper_inverse,
    )


def solution(mesh):
    return jax.shard_map(
        per_device,
        mesh=mesh,
        in_specs=(P(None, "prow", None, "pcol"), P(), P(), P()),
        out_specs=P(None, "prow", None, "pcol"),
        check_vma=False,
    )
```

```python
import functools

import jax
import jax.numpy as jnp
from jax import lax
from jax.experimental import pallas as pl
from jax.experimental.pallas import tpu as pltpu
from jax.sharding import PartitionSpec as P

NY, NZ, NX, NC = 4, 8, 4, 2
N_HOMES = NY * NZ
PAIR_ROWS = 8
DEST_ROWS = 32
LINE_ROWS = 144
Z_ORDER = (0, 7, 1, 4, 6, 5, 2, 3)
Y_ORDER = (0, 3, 1, 2)
MIB = 1 << 20


def shift_y(step, rows=range(NY), cols=range(NZ)):
    return [(y * NZ + z, (y + step) % NY * NZ + z) for y in rows for z in cols]


def shift_z(step, cols=range(NZ)):
    return [(y * NZ + z, y * NZ + (z + step) % NZ) for y in range(NY) for z in cols]


def move_x(pairs):
    return [(a * NC + core, b * NC + core) for a, b in pairs for core in range(NC)]


SWAP = [(x * NC + core, x * NC + 1 - core) for x in range(NX) for core in range(NC)]


def broadcast(value, axis, root):
    mine = lax.axis_index(axis) == root
    return lax.psum(jnp.where(mine, value, jnp.zeros_like(value)), axis)


def locate(pivot_list, panel, prow_size, prow_here):
    block_index = pivot_list // panel
    owned_rows = block_index % prow_size == prow_here
    local_row = block_index // prow_size * panel + pivot_list % panel
    return (owned_rows, local_row)


def general_steps(matrix, pivots, lower_inverse, upper_inverse):
    row_blocks = matrix.shape[0]
    panel = matrix.shape[1]
    col_blocks = matrix.shape[2]
    prow_size = lax.axis_size("prow")
    pcol_size = lax.axis_size("pcol")
    prow_here = lax.axis_index("prow")
    pcol_here = lax.axis_index("pcol")
    local_rows = row_blocks * panel
    local_cols = col_blocks * panel
    current = matrix.reshape(local_rows, local_cols)
    row_global = jnp.repeat(jnp.arange(row_blocks, dtype=jnp.int32) * prow_size + prow_here, panel)
    col_global = jnp.repeat(jnp.arange(col_blocks, dtype=jnp.int32) * pcol_size + pcol_here, panel)
    offsets = jnp.arange(panel, dtype=jnp.int32)
    bf_zero = jnp.zeros((), jnp.bfloat16)
    def one_panel(panel_index, current):
        root_row, root_col = panel_index, panel_index
        diag_local = panel_local = 0
        pivot_list = pivots[panel_index]
        owned_rows, local_row = locate(pivot_list, panel, prow_size, prow_here)
        safe_rows = jnp.where(owned_rows, local_row, 0)
        picked = jnp.where(owned_rows[:, None], current[safe_rows], bf_zero)
        is_root = prow_here == root_row
        previous = current[diag_local : diag_local + panel]
        right_cols = col_global > panel_index
        displaced = broadcast(previous, "prow", root_row)
        gathered = lax.psum(picked, "prow").astype(jnp.float32)
        pivot_block = gathered.astype(jnp.bfloat16)
        product = jnp.dot(
            lower_inverse[panel_index], pivot_block, preferred_element_type=jnp.float32
        ).astype(jnp.bfloat16)
        new_row = jnp.where(right_cols[None, :], product, pivot_block)
        moved_rows = owned_rows & (pivot_list != panel_index * panel + offsets)
        targets = jnp.where(moved_rows, local_row, local_rows)
        current = current.at[targets].set(displaced, mode="drop")
        below_mask = row_global > panel_index
        panel_part = current[:, panel_local : panel_local + panel]
        upper_block = upper_inverse[panel_index]

        def factor(columns):
            result = jnp.dot(columns, upper_block, preferred_element_type=jnp.float32).astype(
                jnp.bfloat16
            )
            return jnp.where(below_mask[:, None], result, jnp.zeros((), jnp.bfloat16))

        def nothing(columns):
            return jnp.zeros((local_rows, panel), jnp.bfloat16)

        factors = lax.cond(pcol_here == root_col, factor, nothing, panel_part)
        factors = broadcast(factors, "pcol", root_col)
        update_rows = jnp.where(right_cols[None, :], new_row, bf_zero)
        correction = jnp.dot(factors, update_rows, preferred_element_type=jnp.float32)
        updated = (current.astype(jnp.float32) - correction).astype(jnp.bfloat16)
        owner_col = pcol_here == root_col
        new_panel = jnp.where(
            owner_col & below_mask[:, None], factors, updated[:, panel_local : panel_local + panel]
        )
        updated = updated.at[:, panel_local : panel_local + panel].set(new_panel)
        row_block = jnp.where(is_root, new_row, updated[diag_local : diag_local + panel])
        return updated.at[diag_local : diag_local + panel].set(row_block)

    current = lax.fori_loop(0, 2, one_panel, current)
    return current.reshape(matrix.shape)


def dot(a, b):
    return jnp.dot(a, b, preferred_element_type=jnp.float32)


def narrow(value):
    return value.astype(jnp.bfloat16)


def iota(shape, axis):
    return lax.broadcasted_iota(jnp.int32, shape, axis)


def total(mask_or_value, axis):
    return jnp.sum(mask_or_value, axis=axis, keepdims=True).astype(jnp.int32)


def pick(mask, value):
    return jnp.where(mask, value, 0).astype(jnp.float32)


def split_rows(row, panel):
    shift = panel.bit_length() - 1
    block = row >> shift
    return block & (N_HOMES - 1), ((block >> 5) << shift) + (row & (panel - 1))


def upright(row):
    tall = jnp.transpose(jnp.broadcast_to(row.astype(jnp.float32), (8, row.shape[1])))
    return tall[:, 0:1].astype(jnp.int32)


def place_of(step, order):
    result = jnp.zeros_like(step)
    for place, value in enumerate(order):
        result = jnp.where(step == value, place, result)
    return result


def deal_kernel(panel, pos_ref, across_ref, rows_ref, picks_ref, keep_ref, place_ref, flag_ref):
    here = pos_ref[0]
    y, z = here >> 3, here & 7
    first_r, second_r = across_ref[0:1, :], across_ref[1:2, :]
    first_c, second_c = upright(first_r), upright(second_r)
    square = (panel, panel)
    number_c, number_r = iota(square, 0), iota(square, 1)
    came_r = total(pick(first_c == second_r, number_c + 1), 0)
    came_c = total(pick(second_c == first_r, number_r + 1), 1)
    source_r = [first_r, jnp.where(came_r > 0, came_r - 1, second_r)]
    source_c = [first_c, jnp.where(came_c > 0, came_c - 1, second_c)]
    owners_r, locals_r = zip(*[split_rows(s, panel) for s in source_r])
    owners_c = [split_rows(s, panel)[0] for s in source_c]
    before = number_c < number_r
    slots, homes, entries = [], [], []
    for s in range(2):
        counts = total(
            pick((owners_c[s] == owners_r[s]) & before, 1025) + pick(owners_c[s] < owners_r[s], 1), 0
        )
        within, rank = counts >> 10, counts & 1023
        slot = within >> 5
        if s == 1:
            shared = total(pick(owners_c[0] == owners_r[1], 1), 0)
            slot = slot + ((shared + N_HOMES - 1) >> 5)
        slots.append(slot)
        homes.append(rank & (N_HOMES - 1))
        entries.append(rank >> 5)
    flag_ref[...] = jnp.maximum(slots[0], slots[1])
    deal = jnp.zeros((N_HOMES * PAIR_ROWS, 1), jnp.int32)
    position = iota((N_HOMES * PAIR_ROWS, panel), 0)
    per_home = panel // N_HOMES
    for s in range(2):
        at = jnp.where(owners_r[s] == here, homes[s] * PAIR_ROWS + slots[s], -1)
        deal = deal + total(pick(position == at, locals_r[s]), 1)
        kept_at = jnp.where(homes[s] == here, entries[s], -1)
        keep_ref[s * per_home : (s + 1) * per_home, :] = total(
            pick(iota((per_home, panel), 0) == kept_at, owners_r[s] * PAIR_ROWS + slots[s]), 1
        )
        z_place = place_of((homes[s] - z) & (NZ - 1), Z_ORDER)
        y_place = place_of(((homes[s] >> 3) - y) & (NY - 1), Y_ORDER)
        place_ref[s : s + 1, :] = (y_place * NZ + z_place) * per_home + entries[s]
    n_rows = rows_ref.shape[0]
    choose = jnp.where(iota((N_HOMES * PAIR_ROWS, n_rows), 1) == deal, 1.0, 0.0)
    picks_ref[...] = narrow(dot(narrow(choose), rows_ref[...]))


def leave_kernel(
    panel,
    pos_ref,
    across_ref,
    rows_ref,
    place_ref,
    lower_ref,
    slots_ref,
    leave0_ref,
    leave1_ref,
    leave2_ref,
    leave3_ref,
    passing_ref,
    land_ref,
    flag_ref,
    low_ref,
):
    here = pos_ref[0]
    y, z = here >> 3, here & 7
    odd = (here & 1) == 1
    first_r, second_r = across_ref[0:1, :], across_ref[1:2, :]
    first_c, second_c = upright(first_r), upright(second_r)
    square = (panel, panel)
    number_c, number_r = iota(square, 0), iota(square, 1)
    big = 1 << 20
    seen_r = total(pick(second_c == first_r, big) + pick(number_c + panel == first_r, second_c), 0)
    seen_c = total(pick(first_c == second_r, big) + pick(first_c == number_r + panel, second_r), 1)
    used_r = total(pick(first_c == number_r + panel, 1), 0)
    used_c = total(pick(number_c + panel == first_r, 1), 1)

    def goals(first, second, seen, used, number):
        inner = (first >= panel) & (first < 2 * panel)
        stop = seen & (big - 1)
        goal_first = jnp.where(
            inner,
            jnp.where(stop == first, -1, stop),
            jnp.where((first == number) | (seen >= big), -1, first),
        )
        goal_second = jnp.where((used > 0) | (second == number + panel), -1, second)
        return goal_first, goal_second

    goal_r = goals(first_r, second_r, seen_r, used_r, number_r[0:1, :])
    goal_c = goals(first_c, second_c, seen_c, used_c, number_c[:, 0:1])
    before = number_c < number_r
    lines, line_ranks, dests, dest_ranks, landing = [], [], [], [], []
    worst = jnp.zeros((1, panel), jnp.int32)
    for s in range(2):
        dest_r, local_r = split_rows(goal_r[s], panel)
        dest_r = jnp.where(goal_r[s] < 0, -1, dest_r)
        dest_c = jnp.where(goal_c[s] < 0, -1, split_rows(goal_c[s], panel)[0])
        line_r, line_c = dest_r >> 3, dest_c >> 3
        counts = total(
            pick((dest_c == dest_r) & before, 1024) + pick((line_c == line_r) & before, 1), 0
        )
        line_rank, dest_rank = counts & 1023, counts >> 10
        worst = jnp.maximum(
            worst,
            jnp.where(
                (dest_r >= 0) & ((line_rank >= LINE_ROWS) | (dest_rank >= DEST_ROWS)), 1, 0
            ),
        )
        land_at = jnp.where(dest_r == here, dest_rank, -1)
        landing.append(total(pick(iota((DEST_ROWS, panel), 0) == land_at, local_r + 1), 1) - 1)
        lines.append(line_r)
        line_ranks.append(line_rank)
        dests.append(dest_r)
        dest_ranks.append(dest_rank)
    worst = jnp.maximum(worst, jnp.where(slots_ref[...] >= PAIR_ROWS, 1, 0))
    flag_ref[0] = jnp.max(worst.astype(jnp.float32)).astype(jnp.int32)
    landing = jnp.concatenate(landing).astype(jnp.float32)
    landing = jnp.transpose(jnp.broadcast_to(landing, (2 * DEST_ROWS, 128)))
    land_ref[...] = landing[0:1, :].astype(jnp.int32)
    line = jnp.where(odd, lines[1], lines[0])
    line_rank = jnp.where(odd, line_ranks[1], line_ranks[0])
    dest = jnp.where(odd, dests[1], dests[0])
    dest_rank = jnp.where(odd, dest_ranks[1], dest_ranks[0])
    send_at = jnp.where(line < 0, -1, line * LINE_ROWS + line_rank)
    choose = jnp.where(iota((NY * LINE_ROWS, panel), 0) == send_at, 1.0, 0.0)
    leaving = narrow(dot(narrow(choose), rows_ref[:panel, :]))
    for k, ref in enumerate((leave0_ref, leave1_ref, leave2_ref, leave3_ref)):
        ref[...] = leaving[k * LINE_ROWS : (k + 1) * LINE_ROWS]
    pass_at = jnp.where(line == y, ((dest - z) & (NZ - 1)) * DEST_ROWS + dest_rank, -1)
    passing_ref[...] = total(
        pick(iota((NZ * DEST_ROWS, panel), 0) == pass_at, line_rank), 1
    )
    for s in range(2):
        order = narrow(jnp.where(number_c == place_ref[s : s + 1, :], 1.0, 0.0))
        low_ref[s] = narrow(
            lax.dot_general(
                lower_ref[s], order, (((1,), (1,)), ((), ())), preferred_element_type=jnp.float32
            )
        )


def block_kernel(keep_ref, dealt_ref, block_ref):
    n = dealt_ref.shape[0]
    choose = jnp.where(keep_ref[...] == iota((keep_ref.shape[0], n), 1), 1.0, 0.0)
    block_ref[...] = narrow(dot(narrow(choose), dealt_ref[...]))


def pair_kernel(block_ref, lo_ref, hi_ref, pair_lo_ref, pair_hi_ref):
    n = block_ref.shape[0]
    pair_lo_ref[:n, :] = block_ref[...]
    pair_lo_ref[n:, :] = lo_ref[...]
    pair_hi_ref[:n, :] = block_ref[...]
    pair_hi_ref[n:, :] = hi_ref[...]


def line_kernel(
    pos_ref, block_ref, lo_ref, hi_ref, opposite_ref, two_lo_ref, two_hi_ref, line_ref, extra_ref
):
    n = block_ref.shape[0]
    half = n // 2
    blocks = [block_ref[...], lo_ref[...], hi_ref[...], opposite_ref[...]]
    blocks += [two_lo_ref[:n, :], two_lo_ref[n:, :], two_hi_ref[:n, :], two_hi_ref[n:, :]]
    for k, value in enumerate(blocks):
        line_ref[k * half : (k + 1) * half, :] = value[:half]
        line_ref[(NZ + k) * half : (NZ + k + 1) * half, :] = value[half:]
    even = (pos_ref[1] & 1) == 0
    n, width = extra_ref.shape
    extra_ref[...] = jnp.where(even, line_ref[n:, :width], line_ref[:n, :width])


def by_x(x, at_0, at_1, at_2, at_3):
    return jnp.where(x <= 1, jnp.where(x == 0, at_0, at_1), jnp.where(x == 2, at_2, at_3))


def choose_kernel(pos_ref, own_ref, one_ref, two_ref, three_ref, out_ref):
    x = pos_ref[1] >> 1
    for place, ref in enumerate((own_ref, one_ref, two_ref, three_ref)):

        @pl.when(x == place)
        def _(ref=ref):
            out_ref[...] = ref[...]


def spread_kernel(pos_ref, passing_ref, own_ref, one_ref, two_ref, three_ref, keep_ref, send_ref):
    y = pos_ref[0] >> 3
    on_line = by_x(y, own_ref[...], one_ref[...], two_ref[...], three_ref[...])
    n_rows = passing_ref.shape[0]
    choose = jnp.where(passing_ref[...] == iota((n_rows, LINE_ROWS), 1), 1.0, 0.0)
    spread = narrow(dot(narrow(choose), on_line))
    keep_ref[...] = spread[: n_rows // 2]
    send_ref[...] = spread[n_rows // 2 :]


def fold_kernel(pos_ref, kept_ref, came_ref, *out_refs):
    for bit, source in ((0, kept_ref), (4, came_ref)):

        @pl.when((pos_ref[0] & 4) == bit)
        def _(source=source):
            for k, ref in enumerate(out_refs):
                ref[...] = source[k * DEST_ROWS : (k + 1) * DEST_ROWS, :]


def gone_kernel(pos_ref, *refs):
    landed, gone_ref, gone_panel_ref = refs[:4], refs[4], refs[5]
    width = gone_panel_ref.shape[1]
    for s in range(2):
        for k in range(4):

            @pl.when(((pos_ref[0] - s) & 3) == k)
            def _(k=k, s=s):
                gone_ref[s * DEST_ROWS : (s + 1) * DEST_ROWS, :] = landed[k][...]

    gone_panel_ref[...] = gone_ref[:, :width]


def settle(land_ref, begin, value, gone):
    n = value.shape[0]
    hits = (iota((n, 2 * DEST_ROWS), 0) + begin) == land_ref[...]
    marks = jnp.where(hits, 1.0, 0.0)
    hit = jnp.sum(marks, axis=1, keepdims=True) > 0.5
    return jnp.where(hit, dot(narrow(marks), gone), value.astype(jnp.float32))


def settle_kernel(rows_ref, land_ref, gone_ref, out_ref):
    begin = pl.program_id(0) * rows_ref.shape[0]
    out_ref[...] = narrow(settle(land_ref, begin, rows_ref[...], gone_ref[...]))


def factor_kernel(pos_ref, part_ref, other_ref, upper_ref, out_ref):
    even = (pos_ref[1] & 1) == 0
    out_ref[...] = narrow(
        dot(jnp.where(even, part_ref[...], other_ref[...]), upper_ref[0])
    )


def extra_kernel(pos_ref, own_ref, one_ref, two_ref, three_ref, cross_ref):
    x = pos_ref[1] >> 1
    cross_ref[...] = by_x(x, own_ref[...], one_ref[...], two_ref[...], three_ref[...])


def part_kernel(pos_ref, mine_ref, before_ref, after_ref, across_ref, part_ref):
    x = pos_ref[1] >> 1
    n = mine_ref.shape[0]
    for step, ref in ((0, mine_ref), (-1, before_ref), (1, after_ref), (2, across_ref)):
        begin = ((x + step) & (NX - 1)) * n
        part_ref[pl.ds(pl.multiple_of(begin, n), n), :] = ref[...]


def cross_kernel(pos_ref, c0_ref, c1_ref, c2_ref, c3_ref, own_ref, one_ref, two_ref, three_ref, cross_ref):
    n = c0_ref.shape[0]
    for k, ref in enumerate((c0_ref, c1_ref, c2_ref, c3_ref)):
        cross_ref[k * n : (k + 1) * n, :] = ref[...]
    x = pos_ref[1] >> 1
    cross_ref[NY * n :, :] = by_x(x, own_ref[...], one_ref[...], two_ref[...], three_ref[...])


def first_kernel(
    low_ref, y0_ref, y1_ref, y2_ref, far_first_ref, far_second_ref, row_ref, second_ref, a00_ref
):
    quarter = far_first_ref.shape[0]
    y_refs = (y0_ref, y1_ref, y2_ref)
    pivot_first = jnp.concatenate([r[:quarter, :] for r in y_refs] + [far_first_ref[...]])
    row_ref[...] = narrow(dot(low_ref[0], pivot_first))
    a00_ref[...] = pivot_first[:, : a00_ref.shape[1]]
    for k, ref in enumerate(y_refs):
        second_ref[k * quarter : (k + 1) * quarter, :] = ref[quarter:, :]
    second_ref[3 * quarter :, :] = far_second_ref[...]


def finish_kernel(
    panel,
    pos_ref,
    rows_ref,
    part_ref,
    other_ref,
    factor_ref,
    land_ref,
    cross_ref,
    cross_other_ref,
    row_first_ref,
    second_ref,
    a00_ref,
    low_ref,
    upper_ref,
    place_ref,
    out_ref,
    new_ref,
    corner_ref,
    gone_first_ref,
    gone_second_ref,
    top_ref,
):
    step = pl.program_id(0)
    here, column = pos_ref[0], pos_ref[1]
    even = (column & 1) == 0
    width = panel
    bf16 = jnp.bfloat16

    @pl.when(step == 0)
    def _():
        mine, others = cross_ref[...], cross_other_ref[...]
        from_first = jnp.where(even, mine, others)
        from_second = jnp.where(even, others, mine)
        gone_first_ref[...] = narrow(dot(from_first[panel:], upper_ref[0]))
        gone_second_ref[...] = from_second[panel:]
        row_first = row_first_ref[...]
        pivot_second = second_ref[...]
        corner_ref[...] = narrow(dot(low_ref[0], from_second[:panel]))
        lower_factor = narrow(dot(from_first[:panel], upper_ref[0]))
        reduced = narrow(pivot_second.astype(jnp.float32) - dot(lower_factor, row_first))
        row_second = narrow(dot(low_ref[1], reduced))
        new_ref[:panel, :] = row_first
        new_ref[panel:, :] = row_second

        @pl.when(here <= 1)
        def _():
            top_ref[...] = jnp.where(here == 0, row_first, row_second)

        @pl.when((here <= 1) & (column <= 1) & (here >= column))
        def _():
            raw = jnp.where(
                here == 0,
                a00_ref[...],
                jnp.where(column == 0, lower_factor, reduced[:, :width]),
            )
            place = jnp.where(here == 0, place_ref[0:1, :], place_ref[1:2, :])
            order = narrow(jnp.where(iota((panel, panel), 0) == place, 1.0, 0.0))
            top_ref[:, :width] = narrow(
                lax.dot_general(
                    order, raw, (((0,), (0,)), ((), ())), preferred_element_type=jnp.float32
                )
            )

    @pl.when(step > 0)
    def _():
        n = rows_ref.shape[0]
        begin = (step - 1) * n
        second = jnp.where(even, other_ref[...], part_ref[...])
        factor_first = narrow(settle(land_ref, begin, factor_ref[...], gone_first_ref[...]))
        panel_second = settle(land_ref, begin, second, gone_second_ref[...])
        mid = narrow(panel_second - dot(factor_first, corner_ref[...]))
        factor_second = narrow(dot(mid, upper_ref[1]))
        current = rows_ref[...].astype(jnp.float32)
        updated = narrow(
            current
            - dot(factor_first, new_ref[:panel, :])
            - dot(factor_second, new_ref[panel:, :])
        )
        out_ref[...] = updated

        @pl.when(column <= 1)
        def _():
            out_ref[:, :width] = jnp.where(column == 0, factor_first, factor_second)

        @pl.when((here <= 1) & (begin < panel))
        def _():
            out_ref[...] = top_ref[pl.ds(pl.multiple_of(begin, n), n), :]


def whole(shape):
    return pl.BlockSpec(shape, lambda *_: (0,) * len(shape))


def smem():
    return pl.BlockSpec(memory_space=pltpu.SMEM)


def shape(dims, dtype=jnp.bfloat16):
    return jax.ShapeDtypeStruct(dims, dtype)


def local_kernel(body, name, outs, scalars, *arrays, limit=12):
    return pl.pallas_call(
        body,
        grid=(1,),
        in_specs=[smem() for _ in scalars] + [whole(v.shape) for v in arrays],
        out_specs=[smem() if o.shape == (1,) else whole(o.shape) for o in outs],
        out_shape=outs,
        compiler_params=pltpu.CompilerParams(vmem_limit_bytes=limit * MIB),
        cost_estimate=pl.CostEstimate(flops=0, bytes_accessed=0, transcendentals=0),
        name=name,
    )(*scalars, *arrays)


def after(values, *others):
    return lax.optimization_barrier((values, others))[0]


def per_device(matrix, pivots, lower_inverse, upper_inverse):
    row_blocks, panel, col_blocks, width = matrix.shape
    local_rows, local_cols = row_blocks * panel, col_blocks * width
    here = lax.axis_index("prow")
    column = lax.axis_index("pcol")
    position = jnp.stack([here, column]).astype(jnp.int32)
    rows = matrix.reshape(local_rows, local_cols)
    per_home = panel // N_HOMES
    i32 = jnp.int32

    picks, keep, place, slots = local_kernel(
        functools.partial(deal_kernel, panel),
        "deal",
        [
            shape((N_HOMES * PAIR_ROWS, local_cols)),
            shape((2 * per_home, 1), i32),
            shape((2, panel), i32),
            shape((1, panel), i32),
        ],
        [position],
        pivots,
        rows,
        limit=32,
    )
    dealt = lax.all_to_all(picks, "prow", 0, 0, tiled=True)

    quarter = local_rows // NX
    own = [rows[k * quarter : (k + 1) * quarter, :width] for k in range(NX)]
    got = [lax.ppermute(own[k], "pcol", move_x([(0, k)])) for k in range(1, NX)]
    (mine,) = local_kernel(
        choose_kernel, "choose", [shape((quarter, width))], [position], own[0], *got
    )

    line_shape = shape((LINE_ROWS, local_cols))
    *leaving, passing, land, flag, low = local_kernel(
        functools.partial(leave_kernel, panel),
        "leave",
        [line_shape]
        + [pltpu.HBM(line_shape.shape, line_shape.dtype)] * (NY - 1)
        + [
            shape((NZ * DEST_ROWS, 1), i32),
            shape((1, 2 * DEST_ROWS), i32),
            shape((1,), i32),
            shape((2, panel, panel)),
        ],
        [position],
        pivots,
        rows,
        place,
        lower_inverse,
        slots,
        limit=32,
    )
    arrived = [lax.ppermute(leaving[s], "prow", shift_y(s, [0], [0, 1])) for s in (1, 2, 3)]

    (block,) = local_kernel(
        block_kernel, "block", [shape((2 * per_home, local_cols))], [], keep, after(dealt, passing)
    )
    from_lo = lax.ppermute(block, "prow", shift_z(1))
    from_hi = lax.ppermute(block, "prow", shift_z(-1))
    opposite = lax.ppermute(block, "prow", shift_z(4))
    quarter_shape = shape((NZ // 2 * DEST_ROWS, local_cols))
    kept, send = local_kernel(
        spread_kernel,
        "spread",
        [quarter_shape] * 2,
        [position],
        after(passing, block),
        leaving[0],
        *arrived,
    )
    came = lax.ppermute(send, "prow", shift_z(4, [0, 1]))

    from_lo, from_hi = after((from_lo, from_hi), mine)
    pair_shape = shape((4 * per_home, local_cols))
    pair_lo, pair_hi = local_kernel(
        pair_kernel, "pair", [pair_shape] * 2, [], block, from_lo, from_hi
    )
    two_lo = lax.ppermute(pair_lo, "prow", shift_z(2))
    two_hi = lax.ppermute(pair_hi, "prow", shift_z(-2))
    quarter_out = after(mine, pair_lo)
    ring = [(x, (x + 1) % NX) for x in range(NX)]
    before = lax.ppermute(quarter_out, "pcol", move_x(ring))
    behind = lax.ppermute(quarter_out, "pcol", move_x([(b, a) for a, b in ring]))

    two_lo, two_hi, opposite = after((two_lo, two_hi, opposite), before, behind)
    half = panel // NY
    n_gone = 2 * DEST_ROWS
    z_line, extra = local_kernel(
        line_kernel,
        "line",
        [shape((2 * half, local_cols)), shape((half, width))],
        [position],
        block,
        from_lo,
        from_hi,
        opposite,
        two_lo,
        two_hi,
    )
    y_lo = lax.ppermute(z_line, "prow", shift_y(1))
    y_hi = lax.ppermute(z_line, "prow", shift_y(-1))
    sent = [lax.ppermute(extra, "pcol", move_x([(0, k)])) for k in (1, 2, 3)]
    one_shape = shape((DEST_ROWS, local_cols))
    spread = local_kernel(
        fold_kernel, "fold", [one_shape] * 4, [position], kept, after(came, extra)
    )
    landed = [spread[0]] + [
        lax.ppermute(spread[k], "prow", shift_z(k, [0, 1, 4, 5])) for k in (1, 2, 3)
    ]
    across = lax.ppermute(
        after(mine, extra), "pcol", move_x([(x, (x + 2) % NX) for x in range(NX)])
    )

    y_lo, y_hi = after((y_lo, y_hi), sent, across, landed)
    far_first = lax.ppermute(y_lo[:half], "prow", shift_y(1))
    far_second = lax.ppermute(y_hi[half:], "prow", shift_y(-1))
    (cross,) = local_kernel(
        extra_kernel, "extra", [shape((half, width))], [position], extra, *sent
    )
    crossed = [lax.ppermute(cross, "prow", shift_y(s)) for s in (1, -1, 2)]
    gone, gone_panel = local_kernel(
        gone_kernel,
        "gone",
        [shape((n_gone, local_cols)), shape((n_gone, width))],
        [position],
        *after(landed, y_lo),
    )
    gone_sent = [lax.ppermute(gone_panel, "pcol", move_x([(0, k)])) for k in (1, 2, 3)]
    (part,) = local_kernel(
        part_kernel,
        "part",
        [shape((local_rows, width))],
        [position],
        mine,
        before,
        behind,
        after(across, y_lo),
    )
    other = lax.ppermute(part, "pcol", SWAP)
    n_block = panel // 2
    steps = local_rows // n_block

    def block_of(cols, lead=0):
        return pl.BlockSpec((n_block, cols), lambda i: (jnp.maximum(i - lead, 0), 0))

    settled = pl.pallas_call(
        settle_kernel,
        grid=(steps,),
        in_specs=[block_of(local_cols), whole((1, n_gone)), whole((n_gone, local_cols))],
        out_specs=block_of(local_cols),
        out_shape=shape((local_rows, local_cols)),
        compiler_params=pltpu.CompilerParams(vmem_limit_bytes=16 * MIB),
        cost_estimate=pl.CostEstimate(flops=0, bytes_accessed=0, transcendentals=0),
        name="settle",
    )(rows, land, gone)
    factor_raw = pl.pallas_call(
        factor_kernel,
        grid=(steps,),
        in_specs=[smem(), block_of(width), block_of(width), whole((2, panel, panel))],
        out_specs=block_of(width),
        out_shape=shape((local_rows, width)),
        compiler_params=pltpu.CompilerParams(vmem_limit_bytes=16 * MIB),
        cost_estimate=pl.CostEstimate(flops=0, bytes_accessed=0, transcendentals=0),
        name="factor",
    )(position, part, other, upper_inverse)

    crossed = after(crossed, far_first, far_second, factor_raw, settled)
    (cross,) = local_kernel(
        cross_kernel,
        "cross",
        [shape((panel + n_gone, width))],
        [position],
        cross,
        *crossed,
        gone_panel,
        *gone_sent,
    )
    cross_other = lax.ppermute(cross, "pcol", SWAP)
    row_first, second, a00 = pl.pallas_call(
        first_kernel,
        grid=(1,),
        in_specs=[whole((2, panel, panel))]
        + [whole((2 * half, local_cols))] * 3
        + [whole((half, local_cols))] * 2,
        out_specs=[whole((panel, local_cols))] * 2 + [whole((panel, width))],
        out_shape=[shape((panel, local_cols))] * 2 + [shape((panel, width))],
        compiler_params=pltpu.CompilerParams(vmem_limit_bytes=40 * MIB),
        cost_estimate=pl.CostEstimate(
            flops=2 * panel * panel * local_cols, bytes_accessed=8 * MIB, transcendentals=0
        ),
        name="first",
    )(low, z_line, y_lo, y_hi, far_first, far_second)

    result = pl.pallas_call(
        functools.partial(finish_kernel, panel),
        grid=(steps + 1,),
        in_specs=[
            smem(),
            block_of(local_cols, 1),
            block_of(width, 1),
            block_of(width, 1),
            block_of(width, 1),
            whole((1, 2 * DEST_ROWS)),
            whole((panel + 2 * DEST_ROWS, width)),
            whole((panel + 2 * DEST_ROWS, width)),
            whole((panel, local_cols)),
            whole((panel, local_cols)),
            whole((panel, width)),
            whole((2, panel, panel)),
            whole((2, panel, panel)),
            whole((2, panel)),
        ],
        out_specs=block_of(local_cols, 1),
        out_shape=shape((local_rows, local_cols)),
        scratch_shapes=[
            pltpu.VMEM((2 * panel, local_cols), jnp.bfloat16),
            pltpu.VMEM((panel, width), jnp.bfloat16),
            pltpu.VMEM((2 * DEST_ROWS, width), jnp.bfloat16),
            pltpu.VMEM((2 * DEST_ROWS, width), jnp.bfloat16),
            pltpu.VMEM((panel, local_cols), jnp.bfloat16),
        ],
        compiler_params=pltpu.CompilerParams(vmem_limit_bytes=32 * MIB),
        name="finish",
    )(position, settled, part, other, factor_raw, land, cross, cross_other, row_first, second, a00, low, upper_inverse, place)
    result = result.reshape(matrix.shape)

    def general(state):
        return 0, general_steps(matrix, pivots, lower_inverse, upper_inverse)

    return lax.while_loop(lambda state: state[0] > 0, general, (flag[0], result))[1]


def solution(mesh):
    return jax.shard_map(
        per_device,
        mesh=mesh,
        in_specs=(P(None, "prow", None, "pcol"), P(), P(), P()),
        out_specs=P(None, "prow", None, "pcol"),
        check_vma=False,
    )
```

```python
import functools

import jax
import jax.numpy as jnp
from jax import lax
from jax.experimental import pallas as pl
from jax.experimental.pallas import tpu as pltpu
from jax.sharding import PartitionSpec as P

NY, NZ, NX, NC = 4, 8, 4, 2
N_HOMES = NY * NZ
PAIR_ROWS = 8
DEST_ROWS = 32
LINE_ROWS = 144
Z_ORDER = (0, 7, 1, 4, 6, 5, 2, 3)
Y_ORDER = (0, 3, 1, 2)
MIB = 1 << 20


def shift_y(step, rows=range(NY), cols=range(NZ)):
    return [(y * NZ + z, (y + step) % NY * NZ + z) for y in rows for z in cols]


def shift_z(step, cols=range(NZ)):
    return [(y * NZ + z, y * NZ + (z + step) % NZ) for y in range(NY) for z in cols]


def move_x(pairs):
    return [(a * NC + core, b * NC + core) for a, b in pairs for core in range(NC)]


def cross_y(bit):
    return [(y * NZ + z, (y ^ bit) * NZ + z) for y in range(NY) for z in range(NZ)]


SWAP = [(x * NC + core, x * NC + 1 - core) for x in range(NX) for core in range(NC)]


def broadcast(value, axis, root):
    mine = lax.axis_index(axis) == root
    return lax.psum(jnp.where(mine, value, jnp.zeros_like(value)), axis)


def locate(pivot_list, panel, prow_size, prow_here):
    block_index = pivot_list // panel
    owned_rows = block_index % prow_size == prow_here
    local_row = block_index // prow_size * panel + pivot_list % panel
    return (owned_rows, local_row)


def general_steps(matrix, pivots, lower_inverse, upper_inverse):
    row_blocks = matrix.shape[0]
    panel = matrix.shape[1]
    col_blocks = matrix.shape[2]
    prow_size = lax.axis_size("prow")
    pcol_size = lax.axis_size("pcol")
    prow_here = lax.axis_index("prow")
    pcol_here = lax.axis_index("pcol")
    local_rows = row_blocks * panel
    local_cols = col_blocks * panel
    current = matrix.reshape(local_rows, local_cols)
    row_global = jnp.repeat(jnp.arange(row_blocks, dtype=jnp.int32) * prow_size + prow_here, panel)
    col_global = jnp.repeat(jnp.arange(col_blocks, dtype=jnp.int32) * pcol_size + pcol_here, panel)
    offsets = jnp.arange(panel, dtype=jnp.int32)
    bf_zero = jnp.zeros((), jnp.bfloat16)
    def one_panel(panel_index, current):
        root_row, root_col = panel_index, panel_index
        diag_local = panel_local = 0
        pivot_list = pivots[panel_index]
        owned_rows, local_row = locate(pivot_list, panel, prow_size, prow_here)
        safe_rows = jnp.where(owned_rows, local_row, 0)
        picked = jnp.where(owned_rows[:, None], current[safe_rows], bf_zero)
        is_root = prow_here == root_row
        previous = current[diag_local : diag_local + panel]
        right_cols = col_global > panel_index
        displaced = broadcast(previous, "prow", root_row)
        gathered = lax.psum(picked, "prow").astype(jnp.float32)
        pivot_block = gathered.astype(jnp.bfloat16)
        product = jnp.dot(
            lower_inverse[panel_index], pivot_block, preferred_element_type=jnp.float32
        ).astype(jnp.bfloat16)
        new_row = jnp.where(right_cols[None, :], product, pivot_block)
        moved_rows = owned_rows & (pivot_list != panel_index * panel + offsets)
        targets = jnp.where(moved_rows, local_row, local_rows)
        current = current.at[targets].set(displaced, mode="drop")
        below_mask = row_global > panel_index
        panel_part = current[:, panel_local : panel_local + panel]
        upper_block = upper_inverse[panel_index]

        def factor(columns):
            result = jnp.dot(columns, upper_block, preferred_element_type=jnp.float32).astype(
                jnp.bfloat16
            )
            return jnp.where(below_mask[:, None], result, jnp.zeros((), jnp.bfloat16))

        def nothing(columns):
            return jnp.zeros((local_rows, panel), jnp.bfloat16)

        factors = lax.cond(pcol_here == root_col, factor, nothing, panel_part)
        factors = broadcast(factors, "pcol", root_col)
        update_rows = jnp.where(right_cols[None, :], new_row, bf_zero)
        correction = jnp.dot(factors, update_rows, preferred_element_type=jnp.float32)
        updated = (current.astype(jnp.float32) - correction).astype(jnp.bfloat16)
        owner_col = pcol_here == root_col
        new_panel = jnp.where(
            owner_col & below_mask[:, None], factors, updated[:, panel_local : panel_local + panel]
        )
        updated = updated.at[:, panel_local : panel_local + panel].set(new_panel)
        row_block = jnp.where(is_root, new_row, updated[diag_local : diag_local + panel])
        return updated.at[diag_local : diag_local + panel].set(row_block)

    current = lax.fori_loop(0, 2, one_panel, current)
    return current.reshape(matrix.shape)


def dot(a, b):
    return jnp.dot(a, b, preferred_element_type=jnp.float32)


def narrow(value):
    return value.astype(jnp.bfloat16)


def iota(shape, axis):
    return lax.broadcasted_iota(jnp.int32, shape, axis)


def total(mask_or_value, axis):
    return jnp.sum(mask_or_value, axis=axis, keepdims=True).astype(jnp.int32)


def pick(mask, value):
    return jnp.where(mask, value, 0).astype(jnp.float32)


def split_rows(row, panel):
    shift = panel.bit_length() - 1
    block = row >> shift
    return block & (N_HOMES - 1), ((block >> 5) << shift) + (row & (panel - 1))


def upright(row):
    tall = jnp.transpose(jnp.broadcast_to(row.astype(jnp.float32), (8, row.shape[1])))
    return tall[:, 0:1].astype(jnp.int32)


def place_of(step, order):
    result = jnp.zeros_like(step)
    for place, value in enumerate(order):
        result = jnp.where(step == value, place, result)
    return result


def deal_kernel(panel, pos_ref, across_ref, rows_ref, picks_ref, keep_ref, place_ref, flag_ref):
    here = pos_ref[0]
    y, z = here >> 3, here & 7
    first_r, second_r = across_ref[0:1, :], across_ref[1:2, :]
    first_c, second_c = upright(first_r), upright(second_r)
    square = (panel, panel)
    number_c, number_r = iota(square, 0), iota(square, 1)
    came_r = total(pick(first_c == second_r, number_c + 1), 0)
    came_c = total(pick(second_c == first_r, number_r + 1), 1)
    source_r = [first_r, jnp.where(came_r > 0, came_r - 1, second_r)]
    source_c = [first_c, jnp.where(came_c > 0, came_c - 1, second_c)]
    owners_r, locals_r = zip(*[split_rows(s, panel) for s in source_r])
    owners_c = [split_rows(s, panel)[0] for s in source_c]
    before = number_c < number_r
    slots, homes, entries = [], [], []
    for s in range(2):
        counts = total(
            pick((owners_c[s] == owners_r[s]) & before, 1025) + pick(owners_c[s] < owners_r[s], 1), 0
        )
        within, rank = counts >> 10, counts & 1023
        slot = within >> 5
        if s == 1:
            shared = total(pick(owners_c[0] == owners_r[1], 1), 0)
            slot = slot + ((shared + N_HOMES - 1) >> 5)
        slots.append(slot)
        homes.append(rank & (N_HOMES - 1))
        entries.append(rank >> 5)
    flag_ref[...] = jnp.maximum(slots[0], slots[1])
    deal = jnp.zeros((N_HOMES * PAIR_ROWS, 1), jnp.int32)
    position = iota((N_HOMES * PAIR_ROWS, panel), 0)
    per_home = panel // N_HOMES
    for s in range(2):
        at = jnp.where(owners_r[s] == here, homes[s] * PAIR_ROWS + slots[s], -1)
        deal = deal + total(pick(position == at, locals_r[s]), 1)
        kept_at = jnp.where(homes[s] == here, entries[s], -1)
        keep_ref[s * per_home : (s + 1) * per_home, :] = total(
            pick(iota((per_home, panel), 0) == kept_at, owners_r[s] * PAIR_ROWS + slots[s]), 1
        )
        z_place = place_of((homes[s] - z) & (NZ - 1), Z_ORDER)
        y_place = place_of(((homes[s] >> 3) - y) & (NY - 1), Y_ORDER)
        place_ref[s : s + 1, :] = (y_place * NZ + z_place) * per_home + entries[s]
    n_rows = rows_ref.shape[0]
    choose = jnp.where(iota((N_HOMES * PAIR_ROWS, n_rows), 1) == deal, 1.0, 0.0)
    picks_ref[...] = narrow(dot(narrow(choose), rows_ref[...]))


def leave_kernel(
    panel,
    pos_ref,
    across_ref,
    rows_ref,
    place_ref,
    lower_ref,
    slots_ref,
    leave0_ref,
    leave1_ref,
    leave2_ref,
    leave3_ref,
    passing_ref,
    land_ref,
    flag_ref,
    low_ref,
):
    here = pos_ref[0]
    y, z = here >> 3, here & 7
    odd = (here & 1) == 1
    first_r, second_r = across_ref[0:1, :], across_ref[1:2, :]
    first_c, second_c = upright(first_r), upright(second_r)
    square = (panel, panel)
    number_c, number_r = iota(square, 0), iota(square, 1)
    big = 1 << 20
    seen_r = total(pick(second_c == first_r, big) + pick(number_c + panel == first_r, second_c), 0)
    seen_c = total(pick(first_c == second_r, big) + pick(first_c == number_r + panel, second_r), 1)
    used_r = total(pick(first_c == number_r + panel, 1), 0)
    used_c = total(pick(number_c + panel == first_r, 1), 1)

    def goals(first, second, seen, used, number):
        inner = (first >= panel) & (first < 2 * panel)
        stop = seen & (big - 1)
        goal_first = jnp.where(
            inner,
            jnp.where(stop == first, -1, stop),
            jnp.where((first == number) | (seen >= big), -1, first),
        )
        goal_second = jnp.where((used > 0) | (second == number + panel), -1, second)
        return goal_first, goal_second

    goal_r = goals(first_r, second_r, seen_r, used_r, number_r[0:1, :])
    goal_c = goals(first_c, second_c, seen_c, used_c, number_c[:, 0:1])
    before = number_c < number_r
    lines, line_ranks, dests, dest_ranks, landing = [], [], [], [], []
    worst = jnp.zeros((1, panel), jnp.int32)
    for s in range(2):
        dest_r, local_r = split_rows(goal_r[s], panel)
        dest_r = jnp.where(goal_r[s] < 0, -1, dest_r)
        dest_c = jnp.where(goal_c[s] < 0, -1, split_rows(goal_c[s], panel)[0])
        line_r, line_c = dest_r >> 3, dest_c >> 3
        counts = total(
            pick((dest_c == dest_r) & before, 1024) + pick((line_c == line_r) & before, 1), 0
        )
        line_rank, dest_rank = counts & 1023, counts >> 10
        worst = jnp.maximum(
            worst,
            jnp.where(
                (dest_r >= 0) & ((line_rank >= LINE_ROWS) | (dest_rank >= DEST_ROWS)), 1, 0
            ),
        )
        land_at = jnp.where(dest_r == here, dest_rank, -1)
        landing.append(total(pick(iota((DEST_ROWS, panel), 0) == land_at, local_r + 1), 1) - 1)
        lines.append(line_r)
        line_ranks.append(line_rank)
        dests.append(dest_r)
        dest_ranks.append(dest_rank)
    worst = jnp.maximum(worst, jnp.where(slots_ref[...] >= PAIR_ROWS, 1, 0))
    flag_ref[0] = jnp.max(worst.astype(jnp.float32)).astype(jnp.int32)
    landing = jnp.concatenate(landing).astype(jnp.float32)
    landing = jnp.transpose(jnp.broadcast_to(landing, (2 * DEST_ROWS, 128)))
    land_ref[...] = landing[0:1, :].astype(jnp.int32)
    line = jnp.where(odd, lines[1], lines[0])
    line_rank = jnp.where(odd, line_ranks[1], line_ranks[0])
    dest = jnp.where(odd, dests[1], dests[0])
    dest_rank = jnp.where(odd, dest_ranks[1], dest_ranks[0])
    send_at = jnp.where(line < 0, -1, line * LINE_ROWS + line_rank)
    choose = jnp.where(iota((NY * LINE_ROWS, panel), 0) == send_at, 1.0, 0.0)
    leaving = narrow(dot(narrow(choose), rows_ref[:panel, :]))
    for k, ref in enumerate((leave0_ref, leave1_ref, leave2_ref, leave3_ref)):
        ref[...] = leaving[k * LINE_ROWS : (k + 1) * LINE_ROWS]
    pass_at = jnp.where(line == y, ((dest - z) & (NZ - 1)) * DEST_ROWS + dest_rank, -1)
    passing_ref[...] = total(
        pick(iota((NZ * DEST_ROWS, panel), 0) == pass_at, line_rank), 1
    )
    for s in range(2):
        order = narrow(jnp.where(number_c == place_ref[s : s + 1, :], 1.0, 0.0))
        low_ref[s] = narrow(
            lax.dot_general(
                lower_ref[s], order, (((1,), (1,)), ((), ())), preferred_element_type=jnp.float32
            )
        )


def block_kernel(keep_ref, dealt_ref, block_ref):
    n = dealt_ref.shape[0]
    choose = jnp.where(keep_ref[...] == iota((keep_ref.shape[0], n), 1), 1.0, 0.0)
    block_ref[...] = narrow(dot(narrow(choose), dealt_ref[...]))


def pair_kernel(block_ref, lo_ref, hi_ref, pair_lo_ref, pair_hi_ref):
    n = block_ref.shape[0]
    pair_lo_ref[:n, :] = block_ref[...]
    pair_lo_ref[n:, :] = lo_ref[...]
    pair_hi_ref[:n, :] = block_ref[...]
    pair_hi_ref[n:, :] = hi_ref[...]


def line_kernel(
    pos_ref, block_ref, lo_ref, hi_ref, opposite_ref, two_lo_ref, two_hi_ref, line_ref, extra_ref
):
    n = block_ref.shape[0]
    half = n // 2
    blocks = [block_ref[...], lo_ref[...], hi_ref[...], opposite_ref[...]]
    blocks += [two_lo_ref[:n, :], two_lo_ref[n:, :], two_hi_ref[:n, :], two_hi_ref[n:, :]]
    for k, value in enumerate(blocks):
        line_ref[k * half : (k + 1) * half, :] = value[:half]
        line_ref[(NZ + k) * half : (NZ + k + 1) * half, :] = value[half:]
    even = (pos_ref[1] & 1) == 0
    n, width = extra_ref.shape
    extra_ref[...] = jnp.where(even, line_ref[n:, :width], line_ref[:n, :width])


def by_x(x, at_0, at_1, at_2, at_3):
    return jnp.where(x <= 1, jnp.where(x == 0, at_0, at_1), jnp.where(x == 2, at_2, at_3))


def choose_kernel(pos_ref, own_ref, one_ref, two_ref, three_ref, out_ref):
    x = pos_ref[1] >> 1
    for place, ref in enumerate((own_ref, one_ref, two_ref, three_ref)):

        @pl.when(x == place)
        def _(ref=ref):
            out_ref[...] = ref[...]


def spread_kernel(pos_ref, passing_ref, own_ref, one_ref, two_ref, three_ref, keep_ref, send_ref):
    y = pos_ref[0] >> 3
    on_line = by_x(y, own_ref[...], one_ref[...], two_ref[...], three_ref[...])
    n_rows = passing_ref.shape[0]
    choose = jnp.where(passing_ref[...] == iota((n_rows, LINE_ROWS), 1), 1.0, 0.0)
    spread = narrow(dot(narrow(choose), on_line))
    keep_ref[...] = spread[: n_rows // 2]
    send_ref[...] = spread[n_rows // 2 :]


def fold_kernel(bit, pos_ref, kept_ref, came_ref, keep_ref, send_ref):
    n = keep_ref.shape[0]

    @pl.when((pos_ref[0] & bit) == 0)
    def _():
        keep_ref[...] = kept_ref[:n, :]
        send_ref[...] = kept_ref[n:, :]

    @pl.when((pos_ref[0] & bit) != 0)
    def _():
        keep_ref[...] = came_ref[:n, :]
        send_ref[...] = came_ref[n:, :]


def gone_kernel(pos_ref, kept_ref, came_ref, gone_ref, gone_panel_ref):
    n, width = kept_ref.shape[0], gone_panel_ref.shape[1]
    even = (pos_ref[0] & 1) == 0
    kept, came = kept_ref[...], came_ref[...]
    gone_ref[:n, :] = jnp.where(even, kept, came)
    gone_ref[n:, :] = jnp.where(even, came, kept)
    gone_panel_ref[...] = gone_ref[:, :width]


def settle(land_ref, begin, value, gone):
    n = value.shape[0]
    hits = (iota((n, 2 * DEST_ROWS), 0) + begin) == land_ref[...]
    marks = jnp.where(hits, 1.0, 0.0)
    hit = jnp.sum(marks, axis=1, keepdims=True) > 0.5
    return jnp.where(hit, dot(narrow(marks), gone), value.astype(jnp.float32))


def settle_kernel(rows_ref, land_ref, gone_ref, out_ref):
    begin = pl.program_id(0) * rows_ref.shape[0]
    out_ref[...] = narrow(settle(land_ref, begin, rows_ref[...], gone_ref[...]))


def factor_kernel(pos_ref, part_ref, other_ref, upper_ref, out_ref):
    even = (pos_ref[1] & 1) == 0
    out_ref[...] = narrow(
        dot(jnp.where(even, part_ref[...], other_ref[...]), upper_ref[0])
    )


def pass_kernel(pos_ref, own_ref, came_ref, out_ref):
    out_ref[...] = jnp.where((pos_ref[1] >> 1) == 2, came_ref[...], own_ref[...])


def even_odd(pos_ref, even_ref, odd_ref):
    return jnp.where(((pos_ref[1] >> 1) & 1) == 0, even_ref[...], odd_ref[...])


def extra_kernel(pos_ref, even_ref, odd_ref, cross_ref):
    cross_ref[...] = even_odd(pos_ref, even_ref, odd_ref)


def two_kernel(own_ref, came_ref, out_ref):
    n = own_ref.shape[0]
    out_ref[:n, :] = own_ref[...]
    out_ref[n:, :] = came_ref[...]


def part_kernel(pos_ref, mine_ref, before_ref, after_ref, across_ref, part_ref):
    x = pos_ref[1] >> 1
    n = mine_ref.shape[0]
    for step, ref in ((0, mine_ref), (-1, before_ref), (1, after_ref), (2, across_ref)):
        begin = ((x + step) & (NX - 1)) * n
        part_ref[pl.ds(pl.multiple_of(begin, n), n), :] = ref[...]


def cross_kernel(pos_ref, near_ref, far_ref, even_ref, odd_ref, cross_ref):
    y = pos_ref[0] >> 3
    n = near_ref.shape[0] // 2
    for k in range(NY):
        source = near_ref if k < 2 else far_ref
        place = place_of(((y ^ k) - y) & (NY - 1), Y_ORDER)
        cross_ref[pl.ds(pl.multiple_of(place * n, n), n), :] = source[
            (k & 1) * n : ((k & 1) + 1) * n, :
        ]
    cross_ref[NY * n :, :] = even_odd(pos_ref, even_ref, odd_ref)


def first_kernel(
    low_ref, y0_ref, y1_ref, y2_ref, far_first_ref, far_second_ref, row_ref, second_ref, a00_ref
):
    quarter = far_first_ref.shape[0]
    y_refs = (y0_ref, y1_ref, y2_ref)
    pivot_first = jnp.concatenate([r[:quarter, :] for r in y_refs] + [far_first_ref[...]])
    row_ref[...] = narrow(dot(low_ref[0], pivot_first))
    a00_ref[...] = pivot_first[:, : a00_ref.shape[1]]
    for k, ref in enumerate(y_refs):
        second_ref[k * quarter : (k + 1) * quarter, :] = ref[quarter:, :]
    second_ref[3 * quarter :, :] = far_second_ref[...]


def finish_kernel(
    panel,
    pos_ref,
    rows_ref,
    part_ref,
    other_ref,
    factor_ref,
    land_ref,
    cross_ref,
    cross_other_ref,
    row_first_ref,
    second_ref,
    a00_ref,
    low_ref,
    upper_ref,
    place_ref,
    out_ref,
    new_ref,
    corner_ref,
    gone_first_ref,
    gone_second_ref,
    top_ref,
):
    step = pl.program_id(0)
    here, column = pos_ref[0], pos_ref[1]
    even = (column & 1) == 0
    width = panel
    bf16 = jnp.bfloat16

    @pl.when(step == 0)
    def _():
        mine, others = cross_ref[...], cross_other_ref[...]
        from_first = jnp.where(even, mine, others)
        from_second = jnp.where(even, others, mine)
        gone_first_ref[...] = narrow(dot(from_first[panel:], upper_ref[0]))
        gone_second_ref[...] = from_second[panel:]
        row_first = row_first_ref[...]
        pivot_second = second_ref[...]
        corner_ref[...] = narrow(dot(low_ref[0], from_second[:panel]))
        lower_factor = narrow(dot(from_first[:panel], upper_ref[0]))
        reduced = narrow(pivot_second.astype(jnp.float32) - dot(lower_factor, row_first))
        row_second = narrow(dot(low_ref[1], reduced))
        new_ref[:panel, :] = row_first
        new_ref[panel:, :] = row_second

        @pl.when(here <= 1)
        def _():
            top_ref[...] = jnp.where(here == 0, row_first, row_second)

        @pl.when((here <= 1) & (column <= 1) & (here >= column))
        def _():
            raw = jnp.where(
                here == 0,
                a00_ref[...],
                jnp.where(column == 0, lower_factor, reduced[:, :width]),
            )
            place = jnp.where(here == 0, place_ref[0:1, :], place_ref[1:2, :])
            order = narrow(jnp.where(iota((panel, panel), 0) == place, 1.0, 0.0))
            top_ref[:, :width] = narrow(
                lax.dot_general(
                    order, raw, (((0,), (0,)), ((), ())), preferred_element_type=jnp.float32
                )
            )

    @pl.when(step > 0)
    def _():
        n = rows_ref.shape[0]
        begin = (step - 1) * n
        second = jnp.where(even, other_ref[...], part_ref[...])
        factor_first = narrow(settle(land_ref, begin, factor_ref[...], gone_first_ref[...]))
        panel_second = settle(land_ref, begin, second, gone_second_ref[...])
        mid = narrow(panel_second - dot(factor_first, corner_ref[...]))
        factor_second = narrow(dot(mid, upper_ref[1]))
        current = rows_ref[...].astype(jnp.float32)
        updated = narrow(
            current
            - dot(factor_first, new_ref[:panel, :])
            - dot(factor_second, new_ref[panel:, :])
        )
        out_ref[...] = updated

        @pl.when(column <= 1)
        def _():
            out_ref[:, :width] = jnp.where(column == 0, factor_first, factor_second)

        @pl.when((here <= 1) & (begin < panel))
        def _():
            out_ref[...] = top_ref[pl.ds(pl.multiple_of(begin, n), n), :]


def whole(shape):
    return pl.BlockSpec(shape, lambda *_: (0,) * len(shape))


def smem():
    return pl.BlockSpec(memory_space=pltpu.SMEM)


def shape(dims, dtype=jnp.bfloat16):
    return jax.ShapeDtypeStruct(dims, dtype)


def local_kernel(body, name, outs, scalars, *arrays, limit=12):
    return pl.pallas_call(
        body,
        grid=(1,),
        in_specs=[smem() for _ in scalars] + [whole(v.shape) for v in arrays],
        out_specs=[smem() if o.shape == (1,) else whole(o.shape) for o in outs],
        out_shape=outs,
        compiler_params=pltpu.CompilerParams(vmem_limit_bytes=limit * MIB),
        cost_estimate=pl.CostEstimate(flops=0, bytes_accessed=0, transcendentals=0),
        name=name,
    )(*scalars, *arrays)


def after(values, *others):
    return lax.optimization_barrier((values, others))[0]


def per_device(matrix, pivots, lower_inverse, upper_inverse):
    row_blocks, panel, col_blocks, width = matrix.shape
    local_rows, local_cols = row_blocks * panel, col_blocks * width
    here = lax.axis_index("prow")
    column = lax.axis_index("pcol")
    position = jnp.stack([here, column]).astype(jnp.int32)
    rows = matrix.reshape(local_rows, local_cols)
    per_home = panel // N_HOMES
    i32 = jnp.int32

    picks, keep, place, slots = local_kernel(
        functools.partial(deal_kernel, panel),
        "deal",
        [
            shape((N_HOMES * PAIR_ROWS, local_cols)),
            shape((2 * per_home, 1), i32),
            shape((2, panel), i32),
            shape((1, panel), i32),
        ],
        [position],
        pivots,
        rows,
        limit=32,
    )
    dealt = lax.all_to_all(picks, "prow", 0, 0, tiled=True)

    quarter = local_rows // NX
    own = [rows[k * quarter : (k + 1) * quarter, :width] for k in range(NX)]
    got = [lax.ppermute(own[k], "pcol", move_x([(0, k)])) for k in range(1, NX)]
    (mine,) = local_kernel(
        choose_kernel, "choose", [shape((quarter, width))], [position], own[0], *got
    )

    line_shape = shape((LINE_ROWS, local_cols))
    *leaving, passing, land, flag, low = local_kernel(
        functools.partial(leave_kernel, panel),
        "leave",
        [line_shape]
        + [pltpu.HBM(line_shape.shape, line_shape.dtype)] * (NY - 1)
        + [
            shape((NZ * DEST_ROWS, 1), i32),
            shape((1, 2 * DEST_ROWS), i32),
            shape((1,), i32),
            shape((2, panel, panel)),
        ],
        [position],
        pivots,
        rows,
        place,
        lower_inverse,
        slots,
        limit=32,
    )

    (block,) = local_kernel(
        block_kernel, "block", [shape((2 * per_home, local_cols))], [], keep, after(dealt, passing)
    )
    from_lo = lax.ppermute(block, "prow", shift_z(1))
    from_hi = lax.ppermute(block, "prow", shift_z(-1))
    opposite = lax.ppermute(block, "prow", shift_z(4))
    arrived = [lax.ppermute(leaving[s], "prow", shift_y(s, [0], [0, 1])) for s in (1, 2, 3)]
    quarter_shape = shape((NZ // 2 * DEST_ROWS, local_cols))
    kept, send = local_kernel(
        spread_kernel,
        "spread",
        [quarter_shape] * 2,
        [position],
        after(passing, from_lo),
        leaving[0],
        *arrived,
    )
    came = lax.ppermute(send, "prow", shift_z(4, [0, 1]))

    from_lo, from_hi = after((from_lo, from_hi), mine)
    pair_shape = shape((4 * per_home, local_cols))
    pair_lo, pair_hi = local_kernel(
        pair_kernel, "pair", [pair_shape] * 2, [], block, from_lo, from_hi
    )
    two_lo = lax.ppermute(pair_lo, "prow", shift_z(2))
    two_hi = lax.ppermute(pair_hi, "prow", shift_z(-2))
    quarter_out = after(mine, pair_lo)
    ring = [(x, (x + 1) % NX) for x in range(NX)]
    before = lax.ppermute(quarter_out, "pcol", move_x(ring))
    behind = lax.ppermute(quarter_out, "pcol", move_x([(b, a) for a, b in ring]))

    two_lo, two_hi, opposite = after((two_lo, two_hi, opposite), before, behind, came)
    half = panel // NY
    n_gone = 2 * DEST_ROWS
    z_line, extra = local_kernel(
        line_kernel,
        "line",
        [shape((2 * half, local_cols)), shape((half, width))],
        [position],
        block,
        from_lo,
        from_hi,
        opposite,
        two_lo,
        two_hi,
    )
    y_lo = lax.ppermute(z_line, "prow", shift_y(1))
    y_hi = lax.ppermute(z_line, "prow", shift_y(-1))
    extra_mid = lax.ppermute(extra, "pcol", move_x([(0, 2)]))
    extra_shape = shape((half, width))
    (extra,) = local_kernel(
        pass_kernel, "pass", [extra_shape], [position], extra, extra_mid
    )
    extra_odd = lax.ppermute(extra, "pcol", move_x([(0, 1), (2, 3)]))
    kept, send = local_kernel(
        functools.partial(fold_kernel, 4),
        "fold4",
        [shape((2 * DEST_ROWS, local_cols))] * 2,
        [position],
        kept,
        after(came, z_line),
    )
    came = lax.ppermute(send, "prow", shift_z(2, [0, 1, 4, 5]))
    kept, send = local_kernel(
        functools.partial(fold_kernel, 2),
        "fold2",
        [shape((DEST_ROWS, local_cols))] * 2,
        [position],
        kept,
        came,
    )
    came = lax.ppermute(send, "prow", shift_z(1))
    across = lax.ppermute(
        after(mine, z_line), "pcol", move_x([(x, (x + 2) % NX) for x in range(NX)])
    )

    y_lo, y_hi = after((y_lo, y_hi), extra_odd, across, came)
    far_first = lax.ppermute(y_lo[:half], "prow", shift_y(1))
    far_second = lax.ppermute(y_hi[half:], "prow", shift_y(-1))
    (near,) = local_kernel(
        extra_kernel, "extra", [extra_shape], [position], extra, extra_odd
    )
    near_other = lax.ppermute(near, "prow", cross_y(1))
    (near,) = local_kernel(
        two_kernel, "two", [shape((2 * half, width))], [], near, near_other
    )
    far = lax.ppermute(near, "prow", cross_y(2))
    gone_shape = shape((n_gone, width))
    gone, gone_panel = local_kernel(
        gone_kernel,
        "gone",
        [shape((n_gone, local_cols)), gone_shape],
        [position],
        *after((kept, came), y_lo),
    )
    gone_mid = lax.ppermute(gone_panel, "pcol", move_x([(0, 2)]))
    (gone_panel,) = local_kernel(
        pass_kernel, "pass2", [gone_shape], [position], gone_panel, gone_mid
    )
    gone_odd = lax.ppermute(gone_panel, "pcol", move_x([(0, 1), (2, 3)]))
    (part,) = local_kernel(
        part_kernel,
        "part",
        [shape((local_rows, width))],
        [position],
        mine,
        before,
        behind,
        after(across, y_lo),
    )
    other = lax.ppermute(part, "pcol", SWAP)
    n_block = panel // 2
    steps = local_rows // n_block

    def block_of(cols, lead=0):
        return pl.BlockSpec((n_block, cols), lambda i: (jnp.maximum(i - lead, 0), 0))

    settled = pl.pallas_call(
        settle_kernel,
        grid=(steps,),
        in_specs=[block_of(local_cols), whole((1, n_gone)), whole((n_gone, local_cols))],
        out_specs=block_of(local_cols),
        out_shape=shape((local_rows, local_cols)),
        compiler_params=pltpu.CompilerParams(vmem_limit_bytes=16 * MIB),
        cost_estimate=pl.CostEstimate(flops=0, bytes_accessed=0, transcendentals=0),
        name="settle",
    )(rows, land, gone)
    factor_raw = pl.pallas_call(
        factor_kernel,
        grid=(steps,),
        in_specs=[smem(), block_of(width), block_of(width), whole((2, panel, panel))],
        out_specs=block_of(width),
        out_shape=shape((local_rows, width)),
        compiler_params=pltpu.CompilerParams(vmem_limit_bytes=16 * MIB),
        cost_estimate=pl.CostEstimate(flops=0, bytes_accessed=0, transcendentals=0),
        name="factor",
    )(position, part, other, upper_inverse)

    far = after(far, far_first, far_second, factor_raw, settled)
    (cross,) = local_kernel(
        cross_kernel,
        "cross",
        [shape((panel + n_gone, width))],
        [position],
        near,
        far,
        gone_panel,
        gone_odd,
    )
    cross_other = lax.ppermute(cross, "pcol", SWAP)
    row_first, second, a00 = pl.pallas_call(
        first_kernel,
        grid=(1,),
        in_specs=[whole((2, panel, panel))]
        + [whole((2 * half, local_cols))] * 3
        + [whole((half, local_cols))] * 2,
        out_specs=[whole((panel, local_cols))] * 2 + [whole((panel, width))],
        out_shape=[shape((panel, local_cols))] * 2 + [shape((panel, width))],
        compiler_params=pltpu.CompilerParams(vmem_limit_bytes=40 * MIB),
        cost_estimate=pl.CostEstimate(
            flops=2 * panel * panel * local_cols, bytes_accessed=8 * MIB, transcendentals=0
        ),
        name="first",
    )(low, z_line, y_lo, y_hi, far_first, far_second)

    result = pl.pallas_call(
        functools.partial(finish_kernel, panel),
        grid=(steps + 1,),
        in_specs=[
            smem(),
            block_of(local_cols, 1),
            block_of(width, 1),
            block_of(width, 1),
            block_of(width, 1),
            whole((1, 2 * DEST_ROWS)),
            whole((panel + 2 * DEST_ROWS, width)),
            whole((panel + 2 * DEST_ROWS, width)),
            whole((panel, local_cols)),
            whole((panel, local_cols)),
            whole((panel, width)),
            whole((2, panel, panel)),
            whole((2, panel, panel)),
            whole((2, panel)),
        ],
        out_specs=block_of(local_cols, 1),
        out_shape=shape((local_rows, local_cols)),
        scratch_shapes=[
            pltpu.VMEM((2 * panel, local_cols), jnp.bfloat16),
            pltpu.VMEM((panel, width), jnp.bfloat16),
            pltpu.VMEM((2 * DEST_ROWS, width), jnp.bfloat16),
            pltpu.VMEM((2 * DEST_ROWS, width), jnp.bfloat16),
            pltpu.VMEM((panel, local_cols), jnp.bfloat16),
        ],
        compiler_params=pltpu.CompilerParams(vmem_limit_bytes=32 * MIB),
        name="finish",
    )(position, settled, part, other, factor_raw, land, cross, cross_other, row_first, second, a00, low, upper_inverse, place)
    result = result.reshape(matrix.shape)

    def general(state):
        return 0, general_steps(matrix, pivots, lower_inverse, upper_inverse)

    return lax.while_loop(lambda state: state[0] > 0, general, (flag[0], result))[1]


def solution(mesh):
    return jax.shard_map(
        per_device,
        mesh=mesh,
        in_specs=(P(None, "prow", None, "pcol"), P(), P(), P()),
        out_specs=P(None, "prow", None, "pcol"),
        check_vma=False,
    )
```

```python
import functools

import jax
import jax.numpy as jnp
from jax import lax
from jax.experimental import pallas as pl
from jax.experimental.pallas import tpu as pltpu
from jax.sharding import PartitionSpec as P

NY, NZ, NX, NC = 4, 8, 4, 2
N_HOMES = NY * NZ
PAIR_ROWS = 8
DEST_ROWS = 32
LINE_ROWS = 144
Z_ORDER = (0, 7, 1, 4, 6, 5, 2, 3)
Y_ORDER = (0, 3, 1, 2)
MIB = 1 << 20


def shift_y(step, rows=range(NY), cols=range(NZ)):
    return [(y * NZ + z, (y + step) % NY * NZ + z) for y in rows for z in cols]


def shift_z(step, cols=range(NZ)):
    return [(y * NZ + z, y * NZ + (z + step) % NZ) for y in range(NY) for z in cols]


def move_x(pairs):
    return [(a * NC + core, b * NC + core) for a, b in pairs for core in range(NC)]


def cross_y(bit):
    return [(y * NZ + z, (y ^ bit) * NZ + z) for y in range(NY) for z in range(NZ)]


SWAP = [(x * NC + core, x * NC + 1 - core) for x in range(NX) for core in range(NC)]


def broadcast(value, axis, root):
    mine = lax.axis_index(axis) == root
    return lax.psum(jnp.where(mine, value, jnp.zeros_like(value)), axis)


def locate(pivot_list, panel, prow_size, prow_here):
    block_index = pivot_list // panel
    owned_rows = block_index % prow_size == prow_here
    local_row = block_index // prow_size * panel + pivot_list % panel
    return (owned_rows, local_row)


def general_steps(matrix, pivots, lower_inverse, upper_inverse):
    row_blocks = matrix.shape[0]
    panel = matrix.shape[1]
    col_blocks = matrix.shape[2]
    prow_size = lax.axis_size("prow")
    pcol_size = lax.axis_size("pcol")
    prow_here = lax.axis_index("prow")
    pcol_here = lax.axis_index("pcol")
    local_rows = row_blocks * panel
    local_cols = col_blocks * panel
    current = matrix.reshape(local_rows, local_cols)
    row_global = jnp.repeat(jnp.arange(row_blocks, dtype=jnp.int32) * prow_size + prow_here, panel)
    col_global = jnp.repeat(jnp.arange(col_blocks, dtype=jnp.int32) * pcol_size + pcol_here, panel)
    offsets = jnp.arange(panel, dtype=jnp.int32)
    bf_zero = jnp.zeros((), jnp.bfloat16)
    def one_panel(panel_index, current):
        root_row, root_col = panel_index, panel_index
        diag_local = panel_local = 0
        pivot_list = pivots[panel_index]
        owned_rows, local_row = locate(pivot_list, panel, prow_size, prow_here)
        safe_rows = jnp.where(owned_rows, local_row, 0)
        picked = jnp.where(owned_rows[:, None], current[safe_rows], bf_zero)
        is_root = prow_here == root_row
        previous = current[diag_local : diag_local + panel]
        right_cols = col_global > panel_index
        displaced = broadcast(previous, "prow", root_row)
        gathered = lax.psum(picked, "prow").astype(jnp.float32)
        pivot_block = gathered.astype(jnp.bfloat16)
        product = jnp.dot(
            lower_inverse[panel_index], pivot_block, preferred_element_type=jnp.float32
        ).astype(jnp.bfloat16)
        new_row = jnp.where(right_cols[None, :], product, pivot_block)
        moved_rows = owned_rows & (pivot_list != panel_index * panel + offsets)
        targets = jnp.where(moved_rows, local_row, local_rows)
        current = current.at[targets].set(displaced, mode="drop")
        below_mask = row_global > panel_index
        panel_part = current[:, panel_local : panel_local + panel]
        upper_block = upper_inverse[panel_index]

        def factor(columns):
            result = jnp.dot(columns, upper_block, preferred_element_type=jnp.float32).astype(
                jnp.bfloat16
            )
            return jnp.where(below_mask[:, None], result, jnp.zeros((), jnp.bfloat16))

        def nothing(columns):
            return jnp.zeros((local_rows, panel), jnp.bfloat16)

        factors = lax.cond(pcol_here == root_col, factor, nothing, panel_part)
        factors = broadcast(factors, "pcol", root_col)
        update_rows = jnp.where(right_cols[None, :], new_row, bf_zero)
        correction = jnp.dot(factors, update_rows, preferred_element_type=jnp.float32)
        updated = (current.astype(jnp.float32) - correction).astype(jnp.bfloat16)
        owner_col = pcol_here == root_col
        new_panel = jnp.where(
            owner_col & below_mask[:, None], factors, updated[:, panel_local : panel_local + panel]
        )
        updated = updated.at[:, panel_local : panel_local + panel].set(new_panel)
        row_block = jnp.where(is_root, new_row, updated[diag_local : diag_local + panel])
        return updated.at[diag_local : diag_local + panel].set(row_block)

    current = lax.fori_loop(0, 2, one_panel, current)
    return current.reshape(matrix.shape)


def dot(a, b):
    return jnp.dot(a, b, preferred_element_type=jnp.float32)


def narrow(value):
    return value.astype(jnp.bfloat16)


def iota(shape, axis):
    return lax.broadcasted_iota(jnp.int32, shape, axis)


def total(mask_or_value, axis):
    return jnp.sum(mask_or_value, axis=axis, keepdims=True).astype(jnp.int32)


def pick(mask, value):
    return jnp.where(mask, value, 0).astype(jnp.float32)


def split_rows(row, panel):
    shift = panel.bit_length() - 1
    block = row >> shift
    return block & (N_HOMES - 1), ((block >> 5) << shift) + (row & (panel - 1))


def upright(row):
    tall = jnp.transpose(jnp.broadcast_to(row.astype(jnp.float32), (8, row.shape[1])))
    return tall[:, 0:1].astype(jnp.int32)


def place_of(step, order):
    result = jnp.zeros_like(step)
    for place, value in enumerate(order):
        result = jnp.where(step == value, place, result)
    return result


def deal_kernel(panel, pos_ref, across_ref, rows_ref, picks_ref, keep_ref, place_ref, flag_ref):
    here = pos_ref[0]
    y, z = here >> 3, here & 7
    first_r, second_r = across_ref[0:1, :], across_ref[1:2, :]
    first_c, second_c = upright(first_r), upright(second_r)
    square = (panel, panel)
    number_c, number_r = iota(square, 0), iota(square, 1)
    came_r = total(pick(first_c == second_r, number_c + 1), 0)
    came_c = total(pick(second_c == first_r, number_r + 1), 1)
    source_r = [first_r, jnp.where(came_r > 0, came_r - 1, second_r)]
    source_c = [first_c, jnp.where(came_c > 0, came_c - 1, second_c)]
    owners_r, locals_r = zip(*[split_rows(s, panel) for s in source_r])
    owners_c = [split_rows(s, panel)[0] for s in source_c]
    before = number_c < number_r
    slots, homes, entries = [], [], []
    for s in range(2):
        counts = total(
            pick((owners_c[s] == owners_r[s]) & before, 1025) + pick(owners_c[s] < owners_r[s], 1), 0
        )
        within, rank = counts >> 10, counts & 1023
        slot = within >> 5
        if s == 1:
            shared = total(pick(owners_c[0] == owners_r[1], 1), 0)
            slot = slot + ((shared + N_HOMES - 1) >> 5)
        slots.append(slot)
        homes.append(rank & (N_HOMES - 1))
        entries.append(rank >> 5)
    flag_ref[...] = jnp.maximum(slots[0], slots[1])
    deal = jnp.zeros((N_HOMES * PAIR_ROWS, 1), jnp.int32)
    position = iota((N_HOMES * PAIR_ROWS, panel), 0)
    per_home = panel // N_HOMES
    for s in range(2):
        at = jnp.where(owners_r[s] == here, homes[s] * PAIR_ROWS + slots[s], -1)
        deal = deal + total(pick(position == at, locals_r[s]), 1)
        kept_at = jnp.where(homes[s] == here, entries[s], -1)
        keep_ref[s * per_home : (s + 1) * per_home, :] = total(
            pick(iota((per_home, panel), 0) == kept_at, owners_r[s] * PAIR_ROWS + slots[s]), 1
        )
        z_place = place_of((homes[s] - z) & (NZ - 1), Z_ORDER)
        y_place = place_of(((homes[s] >> 3) - y) & (NY - 1), Y_ORDER)
        place_ref[s : s + 1, :] = (y_place * NZ + z_place) * per_home + entries[s]
    n_rows = rows_ref.shape[0]
    choose = jnp.where(iota((N_HOMES * PAIR_ROWS, n_rows), 1) == deal, 1.0, 0.0)
    picks_ref[...] = narrow(dot(narrow(choose), rows_ref[...]))


def leave_kernel(
    panel,
    pos_ref,
    across_ref,
    rows_ref,
    place_ref,
    lower_ref,
    slots_ref,
    leave0_ref,
    leave1_ref,
    leave2_ref,
    leave3_ref,
    passing_ref,
    land_ref,
    flag_ref,
    low_ref,
):
    here = pos_ref[0]
    y, z = here >> 3, here & 7
    odd = (here & 1) == 1
    first_r, second_r = across_ref[0:1, :], across_ref[1:2, :]
    first_c, second_c = upright(first_r), upright(second_r)
    square = (panel, panel)
    number_c, number_r = iota(square, 0), iota(square, 1)
    big = 1 << 20
    seen_r = total(pick(second_c == first_r, big) + pick(number_c + panel == first_r, second_c), 0)
    seen_c = total(pick(first_c == second_r, big) + pick(first_c == number_r + panel, second_r), 1)
    used_r = total(pick(first_c == number_r + panel, 1), 0)
    used_c = total(pick(number_c + panel == first_r, 1), 1)

    def goals(first, second, seen, used, number):
        inner = (first >= panel) & (first < 2 * panel)
        stop = seen & (big - 1)
        goal_first = jnp.where(
            inner,
            jnp.where(stop == first, -1, stop),
            jnp.where((first == number) | (seen >= big), -1, first),
        )
        goal_second = jnp.where((used > 0) | (second == number + panel), -1, second)
        return goal_first, goal_second

    goal_r = goals(first_r, second_r, seen_r, used_r, number_r[0:1, :])
    goal_c = goals(first_c, second_c, seen_c, used_c, number_c[:, 0:1])
    before = number_c < number_r
    lines, line_ranks, dests, dest_ranks, landing = [], [], [], [], []
    worst = jnp.zeros((1, panel), jnp.int32)
    for s in range(2):
        dest_r, local_r = split_rows(goal_r[s], panel)
        dest_r = jnp.where(goal_r[s] < 0, -1, dest_r)
        dest_c = jnp.where(goal_c[s] < 0, -1, split_rows(goal_c[s], panel)[0])
        line_r, line_c = dest_r >> 3, dest_c >> 3
        counts = total(
            pick((dest_c == dest_r) & before, 1024) + pick((line_c == line_r) & before, 1), 0
        )
        line_rank, dest_rank = counts & 1023, counts >> 10
        worst = jnp.maximum(
            worst,
            jnp.where(
                (dest_r >= 0) & ((line_rank >= LINE_ROWS) | (dest_rank >= DEST_ROWS)), 1, 0
            ),
        )
        land_at = jnp.where(dest_r == here, dest_rank, -1)
        landing.append(total(pick(iota((DEST_ROWS, panel), 0) == land_at, local_r + 1), 1) - 1)
        lines.append(line_r)
        line_ranks.append(line_rank)
        dests.append(dest_r)
        dest_ranks.append(dest_rank)
    worst = jnp.maximum(worst, jnp.where(slots_ref[...] >= PAIR_ROWS, 1, 0))
    flag_ref[0] = jnp.max(worst.astype(jnp.float32)).astype(jnp.int32)
    landing = jnp.concatenate(landing).astype(jnp.float32)
    landing = jnp.transpose(jnp.broadcast_to(landing, (2 * DEST_ROWS, 128)))
    land_ref[...] = landing[0:1, :].astype(jnp.int32)
    line = jnp.where(odd, lines[1], lines[0])
    line_rank = jnp.where(odd, line_ranks[1], line_ranks[0])
    dest = jnp.where(odd, dests[1], dests[0])
    dest_rank = jnp.where(odd, dest_ranks[1], dest_ranks[0])
    send_at = jnp.where(line < 0, -1, line * LINE_ROWS + line_rank)
    choose = jnp.where(iota((NY * LINE_ROWS, panel), 0) == send_at, 1.0, 0.0)
    leaving = narrow(dot(narrow(choose), rows_ref[:panel, :]))
    for k, ref in enumerate((leave0_ref, leave1_ref, leave2_ref, leave3_ref)):
        ref[...] = leaving[k * LINE_ROWS : (k + 1) * LINE_ROWS]
    pass_at = jnp.where(line == y, ((dest - z) & (NZ - 1)) * DEST_ROWS + dest_rank, -1)
    passing_ref[...] = total(
        pick(iota((NZ * DEST_ROWS, panel), 0) == pass_at, line_rank), 1
    )
    for s in range(2):
        order = narrow(jnp.where(number_c == place_ref[s : s + 1, :], 1.0, 0.0))
        low_ref[s] = narrow(
            lax.dot_general(
                lower_ref[s], order, (((1,), (1,)), ((), ())), preferred_element_type=jnp.float32
            )
        )


def block_kernel(keep_ref, dealt_ref, block_ref):
    n = dealt_ref.shape[0]
    choose = jnp.where(keep_ref[...] == iota((keep_ref.shape[0], n), 1), 1.0, 0.0)
    block_ref[...] = narrow(dot(narrow(choose), dealt_ref[...]))


def pair_kernel(block_ref, lo_ref, hi_ref, pair_lo_ref, pair_hi_ref):
    n = block_ref.shape[0]
    pair_lo_ref[:n, :] = block_ref[...]
    pair_lo_ref[n:, :] = lo_ref[...]
    pair_hi_ref[:n, :] = block_ref[...]
    pair_hi_ref[n:, :] = hi_ref[...]


def line_kernel(
    pos_ref, block_ref, lo_ref, hi_ref, opposite_ref, two_lo_ref, two_hi_ref, line_ref, extra_ref
):
    n = block_ref.shape[0]
    half = n // 2
    blocks = [block_ref[...], lo_ref[...], hi_ref[...], opposite_ref[...]]
    blocks += [two_lo_ref[:n, :], two_lo_ref[n:, :], two_hi_ref[:n, :], two_hi_ref[n:, :]]
    for k, value in enumerate(blocks):
        line_ref[k * half : (k + 1) * half, :] = value[:half]
        line_ref[(NZ + k) * half : (NZ + k + 1) * half, :] = value[half:]
    even = (pos_ref[1] & 1) == 0
    n, width = extra_ref.shape
    extra_ref[...] = jnp.where(even, line_ref[n:, :width], line_ref[:n, :width])


def by_x(x, at_0, at_1, at_2, at_3):
    return jnp.where(x <= 1, jnp.where(x == 0, at_0, at_1), jnp.where(x == 2, at_2, at_3))


def choose_kernel(pos_ref, own_ref, one_ref, two_ref, three_ref, out_ref):
    x = pos_ref[1] >> 1
    for place, ref in enumerate((own_ref, one_ref, two_ref, three_ref)):

        @pl.when(x == place)
        def _(ref=ref):
            out_ref[...] = ref[...]


def spread_kernel(pos_ref, passing_ref, own_ref, one_ref, two_ref, three_ref, keep_ref, send_ref):
    y = pos_ref[0] >> 3
    on_line = by_x(y, own_ref[...], one_ref[...], two_ref[...], three_ref[...])
    n_rows = passing_ref.shape[0]
    choose = jnp.where(passing_ref[...] == iota((n_rows, LINE_ROWS), 1), 1.0, 0.0)
    spread = narrow(dot(narrow(choose), on_line))
    keep_ref[...] = spread[: n_rows // 2]
    send_ref[...] = spread[n_rows // 2 :]


def fold_kernel(bit, pos_ref, kept_ref, came_ref, keep_ref, send_ref):
    n = keep_ref.shape[0]

    @pl.when((pos_ref[0] & bit) == 0)
    def _():
        keep_ref[...] = kept_ref[:n, :]
        send_ref[...] = kept_ref[n:, :]

    @pl.when((pos_ref[0] & bit) != 0)
    def _():
        keep_ref[...] = came_ref[:n, :]
        send_ref[...] = came_ref[n:, :]


def gone_kernel(pos_ref, kept_ref, came_ref, gone_ref, gone_panel_ref):
    n, width = kept_ref.shape[0], gone_panel_ref.shape[1]
    even = (pos_ref[0] & 1) == 0
    kept, came = kept_ref[...], came_ref[...]
    gone_ref[:n, :] = jnp.where(even, kept, came)
    gone_ref[n:, :] = jnp.where(even, came, kept)
    gone_panel_ref[...] = gone_ref[:, :width]


def settle(land_ref, begin, value, gone):
    n = value.shape[0]
    hits = (iota((n, 2 * DEST_ROWS), 0) + begin) == land_ref[...]
    marks = jnp.where(hits, 1.0, 0.0)
    hit = jnp.sum(marks, axis=1, keepdims=True) > 0.5
    return jnp.where(hit, dot(narrow(marks), gone), value.astype(jnp.float32))


def settle_kernel(rows_ref, land_ref, gone_ref, out_ref):
    begin = pl.program_id(0) * rows_ref.shape[0]
    out_ref[...] = narrow(settle(land_ref, begin, rows_ref[...], gone_ref[...]))


def factor_kernel(pos_ref, part_ref, other_ref, upper_ref, out_ref):
    even = (pos_ref[1] & 1) == 0
    out_ref[...] = narrow(
        dot(jnp.where(even, part_ref[...], other_ref[...]), upper_ref[0])
    )


def pass_kernel(pos_ref, own_ref, came_ref, out_ref):
    out_ref[...] = jnp.where((pos_ref[1] >> 1) == 2, came_ref[...], own_ref[...])


def even_odd(pos_ref, even_ref, odd_ref):
    return jnp.where(((pos_ref[1] >> 1) & 1) == 0, even_ref[...], odd_ref[...])


def extra_kernel(pos_ref, even_ref, odd_ref, cross_ref):
    cross_ref[...] = even_odd(pos_ref, even_ref, odd_ref)


def two_kernel(own_ref, came_ref, out_ref):
    n = own_ref.shape[0]
    out_ref[:n, :] = own_ref[...]
    out_ref[n:, :] = came_ref[...]


def part_kernel(pos_ref, mine_ref, before_ref, after_ref, across_ref, part_ref):
    x = pos_ref[1] >> 1
    n = mine_ref.shape[0]
    for step, ref in ((0, mine_ref), (-1, before_ref), (1, after_ref), (2, across_ref)):
        begin = ((x + step) & (NX - 1)) * n
        part_ref[pl.ds(pl.multiple_of(begin, n), n), :] = ref[...]


def cross_kernel(pos_ref, near_ref, far_ref, even_ref, odd_ref, cross_ref):
    y = pos_ref[0] >> 3
    n = near_ref.shape[0] // 2
    for k in range(NY):
        source = near_ref if k < 2 else far_ref
        place = place_of(((y ^ k) - y) & (NY - 1), Y_ORDER)
        cross_ref[pl.ds(pl.multiple_of(place * n, n), n), :] = source[
            (k & 1) * n : ((k & 1) + 1) * n, :
        ]
    cross_ref[NY * n :, :] = even_odd(pos_ref, even_ref, odd_ref)


def first_kernel(
    low_ref, y0_ref, y1_ref, y2_ref, far_first_ref, far_second_ref, row_ref, second_ref, a00_ref
):
    quarter = far_first_ref.shape[0]
    y_refs = (y0_ref, y1_ref, y2_ref)
    pivot_first = jnp.concatenate([r[:quarter, :] for r in y_refs] + [far_first_ref[...]])
    row_ref[...] = narrow(dot(low_ref[0], pivot_first))
    a00_ref[...] = pivot_first[:, : a00_ref.shape[1]]
    for k, ref in enumerate(y_refs):
        second_ref[k * quarter : (k + 1) * quarter, :] = ref[quarter:, :]
    second_ref[3 * quarter :, :] = far_second_ref[...]


def finish_kernel(
    panel,
    pos_ref,
    rows_ref,
    part_ref,
    other_ref,
    factor_ref,
    land_ref,
    cross_ref,
    cross_other_ref,
    row_first_ref,
    second_ref,
    a00_ref,
    low_ref,
    upper_ref,
    place_ref,
    out_ref,
    new_ref,
    corner_ref,
    gone_first_ref,
    gone_second_ref,
    top_ref,
):
    step = pl.program_id(0)
    here, column = pos_ref[0], pos_ref[1]
    even = (column & 1) == 0
    width = panel
    bf16 = jnp.bfloat16

    @pl.when(step == 0)
    def _():
        mine, others = cross_ref[...], cross_other_ref[...]
        from_first = jnp.where(even, mine, others)
        from_second = jnp.where(even, others, mine)
        gone_first_ref[...] = narrow(dot(from_first[panel:], upper_ref[0]))
        gone_second_ref[...] = from_second[panel:]
        row_first = row_first_ref[...]
        pivot_second = second_ref[...]
        corner_ref[...] = narrow(dot(low_ref[0], from_second[:panel]))
        lower_factor = narrow(dot(from_first[:panel], upper_ref[0]))
        reduced = narrow(pivot_second.astype(jnp.float32) - dot(lower_factor, row_first))
        row_second = narrow(dot(low_ref[1], reduced))
        new_ref[:panel, :] = row_first
        new_ref[panel:, :] = row_second

        @pl.when(here <= 1)
        def _():
            top_ref[...] = jnp.where(here == 0, row_first, row_second)

        @pl.when((here <= 1) & (column <= 1) & (here >= column))
        def _():
            raw = jnp.where(
                here == 0,
                a00_ref[...],
                jnp.where(column == 0, lower_factor, reduced[:, :width]),
            )
            place = jnp.where(here == 0, place_ref[0:1, :], place_ref[1:2, :])
            order = narrow(jnp.where(iota((panel, panel), 0) == place, 1.0, 0.0))
            top_ref[:, :width] = narrow(
                lax.dot_general(
                    order, raw, (((0,), (0,)), ((), ())), preferred_element_type=jnp.float32
                )
            )

    @pl.when(step > 0)
    def _():
        n = rows_ref.shape[0]
        begin = (step - 1) * n
        second = jnp.where(even, other_ref[...], part_ref[...])
        factor_first = narrow(settle(land_ref, begin, factor_ref[...], gone_first_ref[...]))
        panel_second = settle(land_ref, begin, second, gone_second_ref[...])
        mid = narrow(panel_second - dot(factor_first, corner_ref[...]))
        factor_second = narrow(dot(mid, upper_ref[1]))
        current = rows_ref[...].astype(jnp.float32)
        updated = narrow(
            current
            - dot(factor_first, new_ref[:panel, :])
            - dot(factor_second, new_ref[panel:, :])
        )
        out_ref[...] = updated

        @pl.when(column <= 1)
        def _():
            out_ref[:, :width] = jnp.where(column == 0, factor_first, factor_second)

        @pl.when((here <= 1) & (begin < panel))
        def _():
            out_ref[...] = top_ref[pl.ds(pl.multiple_of(begin, n), n), :]


def whole(shape):
    return pl.BlockSpec(shape, lambda *_: (0,) * len(shape))


def smem():
    return pl.BlockSpec(memory_space=pltpu.SMEM)


def shape(dims, dtype=jnp.bfloat16):
    return jax.ShapeDtypeStruct(dims, dtype)


def local_kernel(body, name, outs, scalars, *arrays, limit=12):
    return pl.pallas_call(
        body,
        grid=(1,),
        in_specs=[smem() for _ in scalars] + [whole(v.shape) for v in arrays],
        out_specs=[smem() if o.shape == (1,) else whole(o.shape) for o in outs],
        out_shape=outs,
        compiler_params=pltpu.CompilerParams(vmem_limit_bytes=limit * MIB),
        cost_estimate=pl.CostEstimate(flops=0, bytes_accessed=0, transcendentals=0),
        name=name,
    )(*scalars, *arrays)


def after(values, *others):
    return lax.optimization_barrier((values, others))[0]


def per_device(matrix, pivots, lower_inverse, upper_inverse):
    row_blocks, panel, col_blocks, width = matrix.shape
    local_rows, local_cols = row_blocks * panel, col_blocks * width
    here = lax.axis_index("prow")
    column = lax.axis_index("pcol")
    position = jnp.stack([here, column]).astype(jnp.int32)
    rows = matrix.reshape(local_rows, local_cols)
    per_home = panel // N_HOMES
    i32 = jnp.int32

    picks, keep, place, slots = local_kernel(
        functools.partial(deal_kernel, panel),
        "deal",
        [
            shape((N_HOMES * PAIR_ROWS, local_cols)),
            shape((2 * per_home, 1), i32),
            shape((2, panel), i32),
            shape((1, panel), i32),
        ],
        [position],
        pivots,
        rows,
        limit=32,
    )
    dealt = lax.all_to_all(picks, "prow", 0, 0, tiled=True)

    quarter = local_rows // NX
    own = [rows[k * quarter : (k + 1) * quarter, :width] for k in range(NX)]
    got = [lax.ppermute(own[k], "pcol", move_x([(0, k)])) for k in range(1, NX)]
    (mine,) = local_kernel(
        choose_kernel, "choose", [shape((quarter, width))], [position], own[0], *got
    )

    line_shape = shape((LINE_ROWS, local_cols))
    *leaving, passing, land, flag, low = local_kernel(
        functools.partial(leave_kernel, panel),
        "leave",
        [line_shape]
        + [pltpu.HBM(line_shape.shape, line_shape.dtype)] * (NY - 1)
        + [
            shape((NZ * DEST_ROWS, 1), i32),
            shape((1, 2 * DEST_ROWS), i32),
            shape((1,), i32),
            shape((2, panel, panel)),
        ],
        [position],
        pivots,
        rows,
        place,
        lower_inverse,
        slots,
        limit=32,
    )

    (block,) = local_kernel(
        block_kernel, "block", [shape((2 * per_home, local_cols))], [], keep, after(dealt, passing)
    )
    from_lo = lax.ppermute(block, "prow", shift_z(1))
    from_hi = lax.ppermute(block, "prow", shift_z(-1))
    opposite = lax.ppermute(block, "prow", shift_z(4))
    arrived = [lax.ppermute(leaving[s], "prow", shift_y(s, [0], [0, 1])) for s in (1, 2, 3)]
    quarter_shape = shape((NZ // 2 * DEST_ROWS, local_cols))
    kept, send = local_kernel(
        spread_kernel,
        "spread",
        [quarter_shape] * 2,
        [position],
        after(passing, block),
        leaving[0],
        *arrived,
    )
    came = lax.ppermute(send, "prow", shift_z(4, [0, 1]))

    from_lo, from_hi = after((from_lo, from_hi), mine)
    pair_shape = shape((4 * per_home, local_cols))
    pair_lo, pair_hi = local_kernel(
        pair_kernel, "pair", [pair_shape] * 2, [], block, from_lo, from_hi
    )
    two_lo = lax.ppermute(pair_lo, "prow", shift_z(2))
    two_hi = lax.ppermute(pair_hi, "prow", shift_z(-2))
    quarter_out = after(mine, pair_lo)
    ring = [(x, (x + 1) % NX) for x in range(NX)]
    before = lax.ppermute(quarter_out, "pcol", move_x(ring))
    behind = lax.ppermute(quarter_out, "pcol", move_x([(b, a) for a, b in ring]))

    two_lo, two_hi, opposite = after((two_lo, two_hi, opposite), before, behind, kept)
    half = panel // NY
    n_gone = 2 * DEST_ROWS
    z_line, extra = local_kernel(
        line_kernel,
        "line",
        [shape((2 * half, local_cols)), shape((half, width))],
        [position],
        block,
        from_lo,
        from_hi,
        opposite,
        two_lo,
        two_hi,
    )
    y_lo = lax.ppermute(z_line, "prow", shift_y(1))
    y_hi = lax.ppermute(z_line, "prow", shift_y(-1))
    extra_mid = lax.ppermute(extra, "pcol", move_x([(0, 2)]))
    extra_shape = shape((half, width))
    (extra,) = local_kernel(
        pass_kernel, "pass", [extra_shape], [position], extra, extra_mid
    )
    extra_odd = lax.ppermute(extra, "pcol", move_x([(0, 1), (2, 3)]))
    kept, send = local_kernel(
        functools.partial(fold_kernel, 4),
        "fold4",
        [shape((2 * DEST_ROWS, local_cols))] * 2,
        [position],
        kept,
        after(came, z_line),
    )
    came = lax.ppermute(send, "prow", shift_z(2, [0, 1, 4, 5]))
    kept, send = local_kernel(
        functools.partial(fold_kernel, 2),
        "fold2",
        [shape((DEST_ROWS, local_cols))] * 2,
        [position],
        kept,
        came,
    )
    came = lax.ppermute(send, "prow", shift_z(1))
    across = lax.ppermute(
        after(mine, z_line), "pcol", move_x([(x, (x + 2) % NX) for x in range(NX)])
    )

    y_lo, y_hi = after((y_lo, y_hi), extra_odd, across, came)
    far_first = lax.ppermute(y_lo[:half], "prow", shift_y(1))
    far_second = lax.ppermute(y_hi[half:], "prow", shift_y(-1))
    (near,) = local_kernel(
        extra_kernel, "extra", [extra_shape], [position], extra, extra_odd
    )
    near_other = lax.ppermute(near, "prow", cross_y(1))
    gone_shape = shape((n_gone, width))
    gone, gone_panel = local_kernel(
        gone_kernel,
        "gone",
        [shape((n_gone, local_cols)), gone_shape],
        [position],
        *after((kept, came), y_lo),
    )
    gone_mid = lax.ppermute(gone_panel, "pcol", move_x([(0, 2)]))
    (near,) = local_kernel(
        two_kernel,
        "two",
        [shape((2 * half, width))],
        [],
        near,
        after(near_other, far_first, far_second, gone_mid),
    )
    far = lax.ppermute(near, "prow", cross_y(2))
    (gone_panel,) = local_kernel(
        pass_kernel, "pass2", [gone_shape], [position], gone_panel, gone_mid
    )
    gone_odd = lax.ppermute(gone_panel, "pcol", move_x([(0, 1), (2, 3)]))
    (part,) = local_kernel(
        part_kernel,
        "part",
        [shape((local_rows, width))],
        [position],
        mine,
        before,
        behind,
        after(across, y_lo),
    )
    other = lax.ppermute(part, "pcol", SWAP)
    n_block = panel // 2
    steps = local_rows // n_block

    def block_of(cols, lead=0):
        return pl.BlockSpec((n_block, cols), lambda i: (jnp.maximum(i - lead, 0), 0))

    settled = pl.pallas_call(
        settle_kernel,
        grid=(steps,),
        in_specs=[block_of(local_cols), whole((1, n_gone)), whole((n_gone, local_cols))],
        out_specs=block_of(local_cols),
        out_shape=shape((local_rows, local_cols)),
        compiler_params=pltpu.CompilerParams(vmem_limit_bytes=16 * MIB),
        cost_estimate=pl.CostEstimate(flops=0, bytes_accessed=0, transcendentals=0),
        name="settle",
    )(rows, land, gone)
    factor_raw = pl.pallas_call(
        factor_kernel,
        grid=(steps,),
        in_specs=[smem(), block_of(width), block_of(width), whole((2, panel, panel))],
        out_specs=block_of(width),
        out_shape=shape((local_rows, width)),
        compiler_params=pltpu.CompilerParams(vmem_limit_bytes=16 * MIB),
        cost_estimate=pl.CostEstimate(flops=0, bytes_accessed=0, transcendentals=0),
        name="factor",
    )(position, part, other, upper_inverse)

    far = after(far, far_first, far_second, factor_raw, settled)
    (cross,) = local_kernel(
        cross_kernel,
        "cross",
        [shape((panel + n_gone, width))],
        [position],
        near,
        far,
        gone_panel,
        gone_odd,
    )
    cross_other = lax.ppermute(cross, "pcol", SWAP)
    row_first, second, a00 = pl.pallas_call(
        first_kernel,
        grid=(1,),
        in_specs=[whole((2, panel, panel))]
        + [whole((2 * half, local_cols))] * 3
        + [whole((half, local_cols))] * 2,
        out_specs=[whole((panel, local_cols))] * 2 + [whole((panel, width))],
        out_shape=[shape((panel, local_cols))] * 2 + [shape((panel, width))],
        compiler_params=pltpu.CompilerParams(vmem_limit_bytes=40 * MIB),
        cost_estimate=pl.CostEstimate(
            flops=2 * panel * panel * local_cols, bytes_accessed=8 * MIB, transcendentals=0
        ),
        name="first",
    )(low, z_line, y_lo, y_hi, far_first, far_second)

    result = pl.pallas_call(
        functools.partial(finish_kernel, panel),
        grid=(steps + 1,),
        in_specs=[
            smem(),
            block_of(local_cols, 1),
            block_of(width, 1),
            block_of(width, 1),
            block_of(width, 1),
            whole((1, 2 * DEST_ROWS)),
            whole((panel + 2 * DEST_ROWS, width)),
            whole((panel + 2 * DEST_ROWS, width)),
            whole((panel, local_cols)),
            whole((panel, local_cols)),
            whole((panel, width)),
            whole((2, panel, panel)),
            whole((2, panel, panel)),
            whole((2, panel)),
        ],
        out_specs=block_of(local_cols, 1),
        out_shape=shape((local_rows, local_cols)),
        scratch_shapes=[
            pltpu.VMEM((2 * panel, local_cols), jnp.bfloat16),
            pltpu.VMEM((panel, width), jnp.bfloat16),
            pltpu.VMEM((2 * DEST_ROWS, width), jnp.bfloat16),
            pltpu.VMEM((2 * DEST_ROWS, width), jnp.bfloat16),
            pltpu.VMEM((panel, local_cols), jnp.bfloat16),
        ],
        compiler_params=pltpu.CompilerParams(vmem_limit_bytes=32 * MIB),
        name="finish",
    )(position, settled, part, other, factor_raw, land, cross, cross_other, row_first, second, a00, low, upper_inverse, place)
    result = result.reshape(matrix.shape)

    def general(state):
        return 0, general_steps(matrix, pivots, lower_inverse, upper_inverse)

    return lax.while_loop(lambda state: state[0] > 0, general, (flag[0], result))[1]


def solution(mesh):
    return jax.shard_map(
        per_device,
        mesh=mesh,
        in_specs=(P(None, "prow", None, "pcol"), P(), P(), P()),
        out_specs=P(None, "prow", None, "pcol"),
        check_vma=False,
    )
```

```python
import functools

import jax
import jax.numpy as jnp
from jax import lax
from jax.experimental import pallas as pl
from jax.experimental.pallas import tpu as pltpu
from jax.sharding import PartitionSpec as P

NY, NZ, NX, NC = 4, 8, 4, 2
N_HOMES = NY * NZ
PAIR_ROWS = 8
DEST_ROWS = 32
LINE_ROWS = 144
Z_ORDER = (0, 7, 1, 4, 6, 5, 2, 3)
Y_ORDER = (0, 3, 1, 2)
MIB = 1 << 20


def shift_y(step, rows=range(NY), cols=range(NZ)):
    return [(y * NZ + z, (y + step) % NY * NZ + z) for y in rows for z in cols]


def shift_z(step, cols=range(NZ)):
    return [(y * NZ + z, y * NZ + (z + step) % NZ) for y in range(NY) for z in cols]


def move_x(pairs):
    return [(a * NC + core, b * NC + core) for a, b in pairs for core in range(NC)]


def cross_y(bit):
    return [(y * NZ + z, (y ^ bit) * NZ + z) for y in range(NY) for z in range(NZ)]


SWAP = [(x * NC + core, x * NC + 1 - core) for x in range(NX) for core in range(NC)]


def broadcast(value, axis, root):
    mine = lax.axis_index(axis) == root
    return lax.psum(jnp.where(mine, value, jnp.zeros_like(value)), axis)


def locate(pivot_list, panel, prow_size, prow_here):
    block_index = pivot_list // panel
    owned_rows = block_index % prow_size == prow_here
    local_row = block_index // prow_size * panel + pivot_list % panel
    return (owned_rows, local_row)


def general_steps(matrix, pivots, lower_inverse, upper_inverse):
    row_blocks = matrix.shape[0]
    panel = matrix.shape[1]
    col_blocks = matrix.shape[2]
    prow_size = lax.axis_size("prow")
    pcol_size = lax.axis_size("pcol")
    prow_here = lax.axis_index("prow")
    pcol_here = lax.axis_index("pcol")
    local_rows = row_blocks * panel
    local_cols = col_blocks * panel
    current = matrix.reshape(local_rows, local_cols)
    row_global = jnp.repeat(jnp.arange(row_blocks, dtype=jnp.int32) * prow_size + prow_here, panel)
    col_global = jnp.repeat(jnp.arange(col_blocks, dtype=jnp.int32) * pcol_size + pcol_here, panel)
    offsets = jnp.arange(panel, dtype=jnp.int32)
    bf_zero = jnp.zeros((), jnp.bfloat16)
    def one_panel(panel_index, current):
        root_row, root_col = panel_index, panel_index
        diag_local = panel_local = 0
        pivot_list = pivots[panel_index]
        owned_rows, local_row = locate(pivot_list, panel, prow_size, prow_here)
        safe_rows = jnp.where(owned_rows, local_row, 0)
        picked = jnp.where(owned_rows[:, None], current[safe_rows], bf_zero)
        is_root = prow_here == root_row
        previous = current[diag_local : diag_local + panel]
        right_cols = col_global > panel_index
        displaced = broadcast(previous, "prow", root_row)
        gathered = lax.psum(picked, "prow").astype(jnp.float32)
        pivot_block = gathered.astype(jnp.bfloat16)
        product = jnp.dot(
            lower_inverse[panel_index], pivot_block, preferred_element_type=jnp.float32
        ).astype(jnp.bfloat16)
        new_row = jnp.where(right_cols[None, :], product, pivot_block)
        moved_rows = owned_rows & (pivot_list != panel_index * panel + offsets)
        targets = jnp.where(moved_rows, local_row, local_rows)
        current = current.at[targets].set(displaced, mode="drop")
        below_mask = row_global > panel_index
        panel_part = current[:, panel_local : panel_local + panel]
        upper_block = upper_inverse[panel_index]

        def factor(columns):
            result = jnp.dot(columns, upper_block, preferred_element_type=jnp.float32).astype(
                jnp.bfloat16
            )
            return jnp.where(below_mask[:, None], result, jnp.zeros((), jnp.bfloat16))

        def nothing(columns):
            return jnp.zeros((local_rows, panel), jnp.bfloat16)

        factors = lax.cond(pcol_here == root_col, factor, nothing, panel_part)
        factors = broadcast(factors, "pcol", root_col)
        update_rows = jnp.where(right_cols[None, :], new_row, bf_zero)
        correction = jnp.dot(factors, update_rows, preferred_element_type=jnp.float32)
        updated = (current.astype(jnp.float32) - correction).astype(jnp.bfloat16)
        owner_col = pcol_here == root_col
        new_panel = jnp.where(
            owner_col & below_mask[:, None], factors, updated[:, panel_local : panel_local + panel]
        )
        updated = updated.at[:, panel_local : panel_local + panel].set(new_panel)
        row_block = jnp.where(is_root, new_row, updated[diag_local : diag_local + panel])
        return updated.at[diag_local : diag_local + panel].set(row_block)

    current = lax.fori_loop(0, 2, one_panel, current)
    return current.reshape(matrix.shape)


def dot(a, b):
    return jnp.dot(a, b, preferred_element_type=jnp.float32)


def narrow(value):
    return value.astype(jnp.bfloat16)


def iota(shape, axis):
    return lax.broadcasted_iota(jnp.int32, shape, axis)


def total(mask_or_value, axis):
    return jnp.sum(mask_or_value, axis=axis, keepdims=True).astype(jnp.int32)


def pick(mask, value):
    return jnp.where(mask, value, 0).astype(jnp.float32)


def split_rows(row, panel):
    shift = panel.bit_length() - 1
    block = row >> shift
    return block & (N_HOMES - 1), ((block >> 5) << shift) + (row & (panel - 1))


def upright(row):
    tall = jnp.transpose(jnp.broadcast_to(row.astype(jnp.float32), (8, row.shape[1])))
    return tall[:, 0:1].astype(jnp.int32)


def place_of(step, order):
    result = jnp.zeros_like(step)
    for place, value in enumerate(order):
        result = jnp.where(step == value, place, result)
    return result


def deal_kernel(panel, pos_ref, across_ref, rows_ref, picks_ref, keep_ref, place_ref, flag_ref):
    here = pos_ref[0]
    y, z = here >> 3, here & 7
    first_r, second_r = across_ref[0:1, :], across_ref[1:2, :]
    first_c, second_c = upright(first_r), upright(second_r)
    square = (panel, panel)
    number_c, number_r = iota(square, 0), iota(square, 1)
    came_r = total(pick(first_c == second_r, number_c + 1), 0)
    came_c = total(pick(second_c == first_r, number_r + 1), 1)
    source_r = [first_r, jnp.where(came_r > 0, came_r - 1, second_r)]
    source_c = [first_c, jnp.where(came_c > 0, came_c - 1, second_c)]
    owners_r, locals_r = zip(*[split_rows(s, panel) for s in source_r])
    owners_c = [split_rows(s, panel)[0] for s in source_c]
    before = number_c < number_r
    slots, homes, entries = [], [], []
    for s in range(2):
        counts = total(
            pick((owners_c[s] == owners_r[s]) & before, 1025) + pick(owners_c[s] < owners_r[s], 1), 0
        )
        within, rank = counts >> 10, counts & 1023
        slot = within >> 5
        if s == 1:
            shared = total(pick(owners_c[0] == owners_r[1], 1), 0)
            slot = slot + ((shared + N_HOMES - 1) >> 5)
        slots.append(slot)
        homes.append(rank & (N_HOMES - 1))
        entries.append(rank >> 5)
    flag_ref[...] = jnp.maximum(slots[0], slots[1])
    deal = jnp.zeros((N_HOMES * PAIR_ROWS, 1), jnp.int32)
    position = iota((N_HOMES * PAIR_ROWS, panel), 0)
    per_home = panel // N_HOMES
    for s in range(2):
        at = jnp.where(owners_r[s] == here, homes[s] * PAIR_ROWS + slots[s], -1)
        deal = deal + total(pick(position == at, locals_r[s]), 1)
        kept_at = jnp.where(homes[s] == here, entries[s], -1)
        keep_ref[s * per_home : (s + 1) * per_home, :] = total(
            pick(iota((per_home, panel), 0) == kept_at, owners_r[s] * PAIR_ROWS + slots[s]), 1
        )
        z_place = place_of((homes[s] - z) & (NZ - 1), Z_ORDER)
        y_place = place_of(((homes[s] >> 3) - y) & (NY - 1), Y_ORDER)
        place_ref[s : s + 1, :] = (y_place * NZ + z_place) * per_home + entries[s]
    n_rows = rows_ref.shape[0]
    choose = jnp.where(iota((N_HOMES * PAIR_ROWS, n_rows), 1) == deal, 1.0, 0.0)
    picks_ref[...] = narrow(dot(narrow(choose), rows_ref[...]))


def leave_kernel(
    panel,
    pos_ref,
    across_ref,
    rows_ref,
    place_ref,
    lower_ref,
    slots_ref,
    leave0_ref,
    leave1_ref,
    leave2_ref,
    leave3_ref,
    passing_ref,
    land_ref,
    flag_ref,
    low_ref,
):
    here = pos_ref[0]
    y, z = here >> 3, here & 7
    odd = (here & 1) == 1
    first_r, second_r = across_ref[0:1, :], across_ref[1:2, :]
    first_c, second_c = upright(first_r), upright(second_r)
    square = (panel, panel)
    number_c, number_r = iota(square, 0), iota(square, 1)
    big = 1 << 20
    seen_r = total(pick(second_c == first_r, big) + pick(number_c + panel == first_r, second_c), 0)
    seen_c = total(pick(first_c == second_r, big) + pick(first_c == number_r + panel, second_r), 1)
    used_r = total(pick(first_c == number_r + panel, 1), 0)
    used_c = total(pick(number_c + panel == first_r, 1), 1)

    def goals(first, second, seen, used, number):
        inner = (first >= panel) & (first < 2 * panel)
        stop = seen & (big - 1)
        goal_first = jnp.where(
            inner,
            jnp.where(stop == first, -1, stop),
            jnp.where((first == number) | (seen >= big), -1, first),
        )
        goal_second = jnp.where((used > 0) | (second == number + panel), -1, second)
        return goal_first, goal_second

    goal_r = goals(first_r, second_r, seen_r, used_r, number_r[0:1, :])
    goal_c = goals(first_c, second_c, seen_c, used_c, number_c[:, 0:1])
    before = number_c < number_r
    lines, line_ranks, dests, dest_ranks, landing = [], [], [], [], []
    worst = jnp.zeros((1, panel), jnp.int32)
    for s in range(2):
        dest_r, local_r = split_rows(goal_r[s], panel)
        dest_r = jnp.where(goal_r[s] < 0, -1, dest_r)
        dest_c = jnp.where(goal_c[s] < 0, -1, split_rows(goal_c[s], panel)[0])
        line_r, line_c = dest_r >> 3, dest_c >> 3
        counts = total(
            pick((dest_c == dest_r) & before, 1024) + pick((line_c == line_r) & before, 1), 0
        )
        line_rank, dest_rank = counts & 1023, counts >> 10
        worst = jnp.maximum(
            worst,
            jnp.where(
                (dest_r >= 0) & ((line_rank >= LINE_ROWS) | (dest_rank >= DEST_ROWS)), 1, 0
            ),
        )
        land_at = jnp.where(dest_r == here, dest_rank, -1)
        landing.append(total(pick(iota((DEST_ROWS, panel), 0) == land_at, local_r + 1), 1) - 1)
        lines.append(line_r)
        line_ranks.append(line_rank)
        dests.append(dest_r)
        dest_ranks.append(dest_rank)
    worst = jnp.maximum(worst, jnp.where(slots_ref[...] >= PAIR_ROWS, 1, 0))
    flag_ref[0] = jnp.max(worst.astype(jnp.float32)).astype(jnp.int32)
    landing = jnp.concatenate(landing).astype(jnp.float32)
    landing = jnp.transpose(jnp.broadcast_to(landing, (2 * DEST_ROWS, 128)))
    land_ref[...] = landing[0:1, :].astype(jnp.int32)
    line = jnp.where(odd, lines[1], lines[0])
    line_rank = jnp.where(odd, line_ranks[1], line_ranks[0])
    dest = jnp.where(odd, dests[1], dests[0])
    dest_rank = jnp.where(odd, dest_ranks[1], dest_ranks[0])
    send_at = jnp.where(line < 0, -1, line * LINE_ROWS + line_rank)
    choose = jnp.where(iota((NY * LINE_ROWS, panel), 0) == send_at, 1.0, 0.0)
    leaving = narrow(dot(narrow(choose), rows_ref[:panel, :]))
    for k, ref in enumerate((leave0_ref, leave1_ref, leave2_ref, leave3_ref)):
        ref[...] = leaving[k * LINE_ROWS : (k + 1) * LINE_ROWS]
    pass_at = jnp.where(line == y, ((dest - z) & (NZ - 1)) * DEST_ROWS + dest_rank, -1)
    passing_ref[...] = total(
        pick(iota((NZ * DEST_ROWS, panel), 0) == pass_at, line_rank), 1
    )
    for s in range(2):
        order = narrow(jnp.where(number_c == place_ref[s : s + 1, :], 1.0, 0.0))
        low_ref[s] = narrow(
            lax.dot_general(
                lower_ref[s], order, (((1,), (1,)), ((), ())), preferred_element_type=jnp.float32
            )
        )


def block_kernel(keep_ref, dealt_ref, block_ref):
    n = dealt_ref.shape[0]
    choose = jnp.where(keep_ref[...] == iota((keep_ref.shape[0], n), 1), 1.0, 0.0)
    block_ref[...] = narrow(dot(narrow(choose), dealt_ref[...]))


def pair_kernel(block_ref, lo_ref, hi_ref, pair_lo_ref, pair_hi_ref):
    n = block_ref.shape[0]
    pair_lo_ref[:n, :] = block_ref[...]
    pair_lo_ref[n:, :] = lo_ref[...]
    pair_hi_ref[:n, :] = block_ref[...]
    pair_hi_ref[n:, :] = hi_ref[...]


def line_kernel(
    pos_ref, block_ref, lo_ref, hi_ref, opposite_ref, two_lo_ref, two_hi_ref, line_ref, extra_ref
):
    n = block_ref.shape[0]
    half = n // 2
    blocks = [block_ref[...], lo_ref[...], hi_ref[...], opposite_ref[...]]
    blocks += [two_lo_ref[:n, :], two_lo_ref[n:, :], two_hi_ref[:n, :], two_hi_ref[n:, :]]
    for k, value in enumerate(blocks):
        line_ref[k * half : (k + 1) * half, :] = value[:half]
        line_ref[(NZ + k) * half : (NZ + k + 1) * half, :] = value[half:]
    even = (pos_ref[1] & 1) == 0
    n, width = extra_ref.shape
    extra_ref[...] = jnp.where(even, line_ref[n:, :width], line_ref[:n, :width])


def by_x(x, at_0, at_1, at_2, at_3):
    return jnp.where(x <= 1, jnp.where(x == 0, at_0, at_1), jnp.where(x == 2, at_2, at_3))


def choose_kernel(pos_ref, own_ref, one_ref, two_ref, three_ref, out_ref):
    x = pos_ref[1] >> 1
    for place, ref in enumerate((own_ref, one_ref, two_ref, three_ref)):

        @pl.when(x == place)
        def _(ref=ref):
            out_ref[...] = ref[...]


def spread_kernel(pos_ref, passing_ref, own_ref, one_ref, two_ref, three_ref, keep_ref, send_ref):
    y = pos_ref[0] >> 3
    on_line = by_x(y, own_ref[...], one_ref[...], two_ref[...], three_ref[...])
    n_rows = passing_ref.shape[0]
    choose = jnp.where(passing_ref[...] == iota((n_rows, LINE_ROWS), 1), 1.0, 0.0)
    spread = narrow(dot(narrow(choose), on_line))
    keep_ref[...] = spread[: n_rows // 2]
    send_ref[...] = spread[n_rows // 2 :]


def fold_kernel(bit, pos_ref, kept_ref, came_ref, keep_ref, send_ref):
    n = keep_ref.shape[0]

    @pl.when((pos_ref[0] & bit) == 0)
    def _():
        keep_ref[...] = kept_ref[:n, :]
        send_ref[...] = kept_ref[n:, :]

    @pl.when((pos_ref[0] & bit) != 0)
    def _():
        keep_ref[...] = came_ref[:n, :]
        send_ref[...] = came_ref[n:, :]


def gone_kernel(pos_ref, kept_ref, came_ref, gone_ref, gone_panel_ref):
    n, width = kept_ref.shape[0], gone_panel_ref.shape[1]
    even = (pos_ref[0] & 1) == 0
    kept, came = kept_ref[...], came_ref[...]
    gone_ref[:n, :] = jnp.where(even, kept, came)
    gone_ref[n:, :] = jnp.where(even, came, kept)
    gone_panel_ref[...] = gone_ref[:, :width]


def settle(land_ref, begin, value, gone):
    n = value.shape[0]
    hits = (iota((n, 2 * DEST_ROWS), 0) + begin) == land_ref[...]
    marks = jnp.where(hits, 1.0, 0.0)
    hit = jnp.sum(marks, axis=1, keepdims=True) > 0.5
    return jnp.where(hit, dot(narrow(marks), gone), value.astype(jnp.float32))


def settle_kernel(rows_ref, land_ref, gone_ref, out_ref):
    begin = pl.program_id(0) * rows_ref.shape[0]
    out_ref[...] = narrow(settle(land_ref, begin, rows_ref[...], gone_ref[...]))


def factor_kernel(pos_ref, part_ref, other_ref, upper_ref, out_ref):
    even = (pos_ref[1] & 1) == 0
    out_ref[...] = narrow(
        dot(jnp.where(even, part_ref[...], other_ref[...]), upper_ref[0])
    )


def pass_kernel(pos_ref, own_ref, came_ref, out_ref):
    out_ref[...] = jnp.where((pos_ref[1] >> 1) == 2, came_ref[...], own_ref[...])


def even_odd(pos_ref, even_ref, odd_ref):
    return jnp.where(((pos_ref[1] >> 1) & 1) == 0, even_ref[...], odd_ref[...])


def extra_kernel(pos_ref, even_ref, odd_ref, cross_ref):
    cross_ref[...] = even_odd(pos_ref, even_ref, odd_ref)


def two_kernel(own_ref, came_ref, out_ref):
    n = own_ref.shape[0]
    out_ref[:n, :] = own_ref[...]
    out_ref[n:, :] = came_ref[...]


def part_kernel(pos_ref, mine_ref, before_ref, after_ref, across_ref, part_ref):
    x = pos_ref[1] >> 1
    n = mine_ref.shape[0]
    for step, ref in ((0, mine_ref), (-1, before_ref), (1, after_ref), (2, across_ref)):
        begin = ((x + step) & (NX - 1)) * n
        part_ref[pl.ds(pl.multiple_of(begin, n), n), :] = ref[...]


def cross_kernel(pos_ref, near_ref, far_ref, even_ref, odd_ref, cross_ref):
    y = pos_ref[0] >> 3
    n = near_ref.shape[0] // 2
    for k in range(NY):
        source = near_ref if k < 2 else far_ref
        place = place_of(((y ^ k) - y) & (NY - 1), Y_ORDER)
        cross_ref[pl.ds(pl.multiple_of(place * n, n), n), :] = source[
            (k & 1) * n : ((k & 1) + 1) * n, :
        ]
    cross_ref[NY * n :, :] = even_odd(pos_ref, even_ref, odd_ref)


def first_kernel(
    low_ref, y0_ref, y1_ref, y2_ref, far_first_ref, far_second_ref, row_ref, second_ref, a00_ref
):
    quarter = far_first_ref.shape[0]
    y_refs = (y0_ref, y1_ref, y2_ref)
    pivot_first = jnp.concatenate([r[:quarter, :] for r in y_refs] + [far_first_ref[...]])
    row_ref[...] = narrow(dot(low_ref[0], pivot_first))
    a00_ref[...] = pivot_first[:, : a00_ref.shape[1]]
    for k, ref in enumerate(y_refs):
        second_ref[k * quarter : (k + 1) * quarter, :] = ref[quarter:, :]
    second_ref[3 * quarter :, :] = far_second_ref[...]


def finish_kernel(
    panel,
    pos_ref,
    rows_ref,
    part_ref,
    other_ref,
    factor_ref,
    land_ref,
    cross_ref,
    cross_other_ref,
    row_first_ref,
    second_ref,
    a00_ref,
    low_ref,
    upper_ref,
    place_ref,
    out_ref,
    new_ref,
    corner_ref,
    gone_first_ref,
    gone_second_ref,
    top_ref,
):
    step = pl.program_id(0)
    here, column = pos_ref[0], pos_ref[1]
    even = (column & 1) == 0
    width = panel
    bf16 = jnp.bfloat16

    @pl.when(step == 0)
    def _():
        mine, others = cross_ref[...], cross_other_ref[...]
        from_first = jnp.where(even, mine, others)
        from_second = jnp.where(even, others, mine)
        gone_first_ref[...] = narrow(dot(from_first[panel:], upper_ref[0]))
        gone_second_ref[...] = from_second[panel:]
        row_first = row_first_ref[...]
        pivot_second = second_ref[...]
        corner_ref[...] = narrow(dot(low_ref[0], from_second[:panel]))
        lower_factor = narrow(dot(from_first[:panel], upper_ref[0]))
        reduced = narrow(pivot_second.astype(jnp.float32) - dot(lower_factor, row_first))
        row_second = narrow(dot(low_ref[1], reduced))
        new_ref[:panel, :] = row_first
        new_ref[panel:, :] = row_second

        @pl.when(here <= 1)
        def _():
            top_ref[...] = jnp.where(here == 0, row_first, row_second)

        @pl.when((here <= 1) & (column <= 1) & (here >= column))
        def _():
            raw = jnp.where(
                here == 0,
                a00_ref[...],
                jnp.where(column == 0, lower_factor, reduced[:, :width]),
            )
            place = jnp.where(here == 0, place_ref[0:1, :], place_ref[1:2, :])
            order = narrow(jnp.where(iota((panel, panel), 0) == place, 1.0, 0.0))
            top_ref[:, :width] = narrow(
                lax.dot_general(
                    order, raw, (((0,), (0,)), ((), ())), preferred_element_type=jnp.float32
                )
            )

    @pl.when(step > 0)
    def _():
        n = rows_ref.shape[0]
        begin = (step - 1) * n
        second = jnp.where(even, other_ref[...], part_ref[...])
        factor_first = narrow(settle(land_ref, begin, factor_ref[...], gone_first_ref[...]))
        panel_second = settle(land_ref, begin, second, gone_second_ref[...])
        mid = narrow(panel_second - dot(factor_first, corner_ref[...]))
        factor_second = narrow(dot(mid, upper_ref[1]))
        current = rows_ref[...].astype(jnp.float32)
        updated = narrow(
            current
            - dot(factor_first, new_ref[:panel, :])
            - dot(factor_second, new_ref[panel:, :])
        )
        out_ref[...] = updated

        @pl.when(column <= 1)
        def _():
            out_ref[:, :width] = jnp.where(column == 0, factor_first, factor_second)

        @pl.when((here <= 1) & (begin < panel))
        def _():
            out_ref[...] = top_ref[pl.ds(pl.multiple_of(begin, n), n), :]


def whole(shape):
    return pl.BlockSpec(shape, lambda *_: (0,) * len(shape))


def smem():
    return pl.BlockSpec(memory_space=pltpu.SMEM)


def shape(dims, dtype=jnp.bfloat16):
    return jax.ShapeDtypeStruct(dims, dtype)


def local_kernel(body, name, outs, scalars, *arrays, limit=12):
    return pl.pallas_call(
        body,
        grid=(1,),
        in_specs=[smem() for _ in scalars] + [whole(v.shape) for v in arrays],
        out_specs=[smem() if o.shape == (1,) else whole(o.shape) for o in outs],
        out_shape=outs,
        compiler_params=pltpu.CompilerParams(vmem_limit_bytes=limit * MIB),
        cost_estimate=pl.CostEstimate(flops=0, bytes_accessed=0, transcendentals=0),
        name=name,
    )(*scalars, *arrays)


def after(values, *others):
    return lax.optimization_barrier((values, others))[0]


def per_device(matrix, pivots, lower_inverse, upper_inverse):
    row_blocks, panel, col_blocks, width = matrix.shape
    local_rows, local_cols = row_blocks * panel, col_blocks * width
    here = lax.axis_index("prow")
    column = lax.axis_index("pcol")
    position = jnp.stack([here, column]).astype(jnp.int32)
    rows = matrix.reshape(local_rows, local_cols)
    per_home = panel // N_HOMES
    i32 = jnp.int32

    picks, keep, place, slots = local_kernel(
        functools.partial(deal_kernel, panel),
        "deal",
        [
            shape((N_HOMES * PAIR_ROWS, local_cols)),
            shape((2 * per_home, 1), i32),
            shape((2, panel), i32),
            shape((1, panel), i32),
        ],
        [position],
        pivots,
        rows,
        limit=32,
    )
    dealt = lax.all_to_all(picks, "prow", 0, 0, tiled=True)

    quarter = local_rows // NX
    own = [rows[k * quarter : (k + 1) * quarter, :width] for k in range(NX)]

    line_shape = shape((LINE_ROWS, local_cols))
    *leaving, passing, land, flag, low = local_kernel(
        functools.partial(leave_kernel, panel),
        "leave",
        [line_shape]
        + [pltpu.HBM(line_shape.shape, line_shape.dtype)] * (NY - 1)
        + [
            shape((NZ * DEST_ROWS, 1), i32),
            shape((1, 2 * DEST_ROWS), i32),
            shape((1,), i32),
            shape((2, panel, panel)),
        ],
        [position],
        pivots,
        rows,
        place,
        lower_inverse,
        slots,
        limit=32,
    )

    (block,) = local_kernel(
        block_kernel, "block", [shape((2 * per_home, local_cols))], [], keep, after(dealt, passing)
    )
    from_lo = lax.ppermute(block, "prow", shift_z(1))
    from_hi = lax.ppermute(block, "prow", shift_z(-1))
    opposite = lax.ppermute(block, "prow", shift_z(4))
    arrived = [lax.ppermute(leaving[s], "prow", shift_y(s, [0], [0, 1])) for s in (1, 2, 3)]
    own = after(own, block)
    got = [lax.ppermute(own[k], "pcol", move_x([(0, k)])) for k in range(1, NX)]
    quarter_shape = shape((NZ // 2 * DEST_ROWS, local_cols))
    kept, send = local_kernel(
        spread_kernel,
        "spread",
        [quarter_shape] * 2,
        [position],
        after(passing, block),
        leaving[0],
        *arrived,
    )
    came = lax.ppermute(send, "prow", shift_z(4, [0, 1]))

    pair_shape = shape((4 * per_home, local_cols))
    pair_lo, pair_hi = local_kernel(
        pair_kernel, "pair", [pair_shape] * 2, [], block, from_lo, from_hi
    )
    two_lo = lax.ppermute(pair_lo, "prow", shift_z(2))
    two_hi = lax.ppermute(pair_hi, "prow", shift_z(-2))
    two_lo, two_hi, opposite = after((two_lo, two_hi, opposite), came)
    half = panel // NY
    n_gone = 2 * DEST_ROWS
    z_line, extra = local_kernel(
        line_kernel,
        "line",
        [shape((2 * half, local_cols)), shape((half, width))],
        [position],
        block,
        from_lo,
        from_hi,
        opposite,
        two_lo,
        two_hi,
    )
    y_lo = lax.ppermute(z_line, "prow", shift_y(1))
    y_hi = lax.ppermute(z_line, "prow", shift_y(-1))
    (mine,) = local_kernel(
        choose_kernel, "choose", [shape((quarter, width))], [position], own[0], *after(got, z_line)
    )
    quarter_out = mine
    ring = [(x, (x + 1) % NX) for x in range(NX)]
    before = lax.ppermute(quarter_out, "pcol", move_x(ring))
    behind = lax.ppermute(quarter_out, "pcol", move_x([(b, a) for a, b in ring]))

    extra_mid = lax.ppermute(extra, "pcol", move_x([(0, 2)]))
    extra_shape = shape((half, width))
    (extra,) = local_kernel(
        pass_kernel, "pass", [extra_shape], [position], extra, extra_mid
    )
    extra_odd = lax.ppermute(extra, "pcol", move_x([(0, 1), (2, 3)]))
    kept, send = local_kernel(
        functools.partial(fold_kernel, 4),
        "fold4",
        [shape((2 * DEST_ROWS, local_cols))] * 2,
        [position],
        kept,
        after(came, z_line),
    )
    came = lax.ppermute(send, "prow", shift_z(2, [0, 1, 4, 5]))
    kept, send = local_kernel(
        functools.partial(fold_kernel, 2),
        "fold2",
        [shape((DEST_ROWS, local_cols))] * 2,
        [position],
        kept,
        came,
    )
    came = lax.ppermute(send, "prow", shift_z(1))
    y_lo, y_hi = after((y_lo, y_hi), extra_odd, before, behind, came)
    across = lax.ppermute(
        after(mine, y_lo), "pcol", move_x([(x, (x + 2) % NX) for x in range(NX)])
    )

    far_first = lax.ppermute(y_lo[:half], "prow", shift_y(1))
    far_second = lax.ppermute(y_hi[half:], "prow", shift_y(-1))
    (near,) = local_kernel(
        extra_kernel, "extra", [extra_shape], [position], extra, extra_odd
    )
    near_other = lax.ppermute(near, "prow", cross_y(1))
    gone_shape = shape((n_gone, width))
    gone, gone_panel = local_kernel(
        gone_kernel,
        "gone",
        [shape((n_gone, local_cols)), gone_shape],
        [position],
        *after((kept, came), y_lo),
    )
    gone_mid = lax.ppermute(gone_panel, "pcol", move_x([(0, 2)]))
    (near,) = local_kernel(
        two_kernel,
        "two",
        [shape((2 * half, width))],
        [],
        near,
        after(near_other, far_first, far_second, gone_mid),
    )
    far = lax.ppermute(near, "prow", cross_y(2))
    (gone_panel,) = local_kernel(
        pass_kernel, "pass2", [gone_shape], [position], gone_panel, gone_mid
    )
    gone_odd = lax.ppermute(gone_panel, "pcol", move_x([(0, 1), (2, 3)]))
    (part,) = local_kernel(
        part_kernel,
        "part",
        [shape((local_rows, width))],
        [position],
        mine,
        before,
        behind,
        after(across, near),
    )
    other = lax.ppermute(part, "pcol", SWAP)
    n_block = panel // 2
    steps = local_rows // n_block

    def block_of(cols, lead=0):
        return pl.BlockSpec((n_block, cols), lambda i: (jnp.maximum(i - lead, 0), 0))

    settled = pl.pallas_call(
        settle_kernel,
        grid=(steps,),
        in_specs=[block_of(local_cols), whole((1, n_gone)), whole((n_gone, local_cols))],
        out_specs=block_of(local_cols),
        out_shape=shape((local_rows, local_cols)),
        compiler_params=pltpu.CompilerParams(vmem_limit_bytes=16 * MIB),
        cost_estimate=pl.CostEstimate(flops=0, bytes_accessed=0, transcendentals=0),
        name="settle",
    )(rows, land, gone)
    factor_raw = pl.pallas_call(
        factor_kernel,
        grid=(steps,),
        in_specs=[smem(), block_of(width), block_of(width), whole((2, panel, panel))],
        out_specs=block_of(width),
        out_shape=shape((local_rows, width)),
        compiler_params=pltpu.CompilerParams(vmem_limit_bytes=16 * MIB),
        cost_estimate=pl.CostEstimate(flops=0, bytes_accessed=0, transcendentals=0),
        name="factor",
    )(position, part, other, upper_inverse)

    far = after(far, far_first, far_second, settled)
    (cross,) = local_kernel(
        cross_kernel,
        "cross",
        [shape((panel + n_gone, width))],
        [position],
        near,
        far,
        gone_panel,
        gone_odd,
    )
    cross_other = lax.ppermute(cross, "pcol", SWAP)
    row_first, second, a00 = pl.pallas_call(
        first_kernel,
        grid=(1,),
        in_specs=[whole((2, panel, panel))]
        + [whole((2 * half, local_cols))] * 3
        + [whole((half, local_cols))] * 2,
        out_specs=[whole((panel, local_cols))] * 2 + [whole((panel, width))],
        out_shape=[shape((panel, local_cols))] * 2 + [shape((panel, width))],
        compiler_params=pltpu.CompilerParams(vmem_limit_bytes=40 * MIB),
        cost_estimate=pl.CostEstimate(
            flops=2 * panel * panel * local_cols, bytes_accessed=8 * MIB, transcendentals=0
        ),
        name="first",
    )(low, z_line, y_lo, y_hi, far_first, far_second)

    result = pl.pallas_call(
        functools.partial(finish_kernel, panel),
        grid=(steps + 1,),
        in_specs=[
            smem(),
            block_of(local_cols, 1),
            block_of(width, 1),
            block_of(width, 1),
            block_of(width, 1),
            whole((1, 2 * DEST_ROWS)),
            whole((panel + 2 * DEST_ROWS, width)),
            whole((panel + 2 * DEST_ROWS, width)),
            whole((panel, local_cols)),
            whole((panel, local_cols)),
            whole((panel, width)),
            whole((2, panel, panel)),
            whole((2, panel, panel)),
            whole((2, panel)),
        ],
        out_specs=block_of(local_cols, 1),
        out_shape=shape((local_rows, local_cols)),
        scratch_shapes=[
            pltpu.VMEM((2 * panel, local_cols), jnp.bfloat16),
            pltpu.VMEM((panel, width), jnp.bfloat16),
            pltpu.VMEM((2 * DEST_ROWS, width), jnp.bfloat16),
            pltpu.VMEM((2 * DEST_ROWS, width), jnp.bfloat16),
            pltpu.VMEM((panel, local_cols), jnp.bfloat16),
        ],
        compiler_params=pltpu.CompilerParams(vmem_limit_bytes=32 * MIB),
        name="finish",
    )(position, settled, part, other, factor_raw, land, cross, cross_other, row_first, second, a00, low, upper_inverse, place)
    result = result.reshape(matrix.shape)

    def general(state):
        return 0, general_steps(matrix, pivots, lower_inverse, upper_inverse)

    return lax.while_loop(lambda state: state[0] > 0, general, (flag[0], result))[1]


def solution(mesh):
    return jax.shard_map(
        per_device,
        mesh=mesh,
        in_specs=(P(None, "prow", None, "pcol"), P(), P(), P()),
        out_specs=P(None, "prow", None, "pcol"),
        check_vma=False,
    )
```

```python
import functools

import jax
import jax.numpy as jnp
from jax import lax
from jax.experimental import pallas as pl
from jax.experimental.pallas import tpu as pltpu
from jax.sharding import PartitionSpec as P

NY, NZ, NX, NC = 4, 8, 4, 2
N_HOMES = NY * NZ
PAIR_ROWS = 8
DEST_ROWS = 32
LINE_ROWS = 144
Z_ORDER = (0, 7, 1, 4, 6, 5, 2, 3)
Y_ORDER = (0, 3, 1, 2)
MIB = 1 << 20


def shift_y(step, rows=range(NY), cols=range(NZ)):
    return [(y * NZ + z, (y + step) % NY * NZ + z) for y in rows for z in cols]


def shift_z(step, cols=range(NZ)):
    return [(y * NZ + z, y * NZ + (z + step) % NZ) for y in range(NY) for z in cols]


def move_x(pairs):
    return [(a * NC + core, b * NC + core) for a, b in pairs for core in range(NC)]


def cross_y(bit):
    return [(y * NZ + z, (y ^ bit) * NZ + z) for y in range(NY) for z in range(NZ)]


SWAP = [(x * NC + core, x * NC + 1 - core) for x in range(NX) for core in range(NC)]


def broadcast(value, axis, root):
    mine = lax.axis_index(axis) == root
    return lax.psum(jnp.where(mine, value, jnp.zeros_like(value)), axis)


def locate(pivot_list, panel, prow_size, prow_here):
    block_index = pivot_list // panel
    owned_rows = block_index % prow_size == prow_here
    local_row = block_index // prow_size * panel + pivot_list % panel
    return (owned_rows, local_row)


def general_steps(matrix, pivots, lower_inverse, upper_inverse):
    row_blocks = matrix.shape[0]
    panel = matrix.shape[1]
    col_blocks = matrix.shape[2]
    prow_size = lax.axis_size("prow")
    pcol_size = lax.axis_size("pcol")
    prow_here = lax.axis_index("prow")
    pcol_here = lax.axis_index("pcol")
    local_rows = row_blocks * panel
    local_cols = col_blocks * panel
    current = matrix.reshape(local_rows, local_cols)
    row_global = jnp.repeat(jnp.arange(row_blocks, dtype=jnp.int32) * prow_size + prow_here, panel)
    col_global = jnp.repeat(jnp.arange(col_blocks, dtype=jnp.int32) * pcol_size + pcol_here, panel)
    offsets = jnp.arange(panel, dtype=jnp.int32)
    bf_zero = jnp.zeros((), jnp.bfloat16)
    def one_panel(panel_index, current):
        root_row, root_col = panel_index, panel_index
        diag_local = panel_local = 0
        pivot_list = pivots[panel_index]
        owned_rows, local_row = locate(pivot_list, panel, prow_size, prow_here)
        safe_rows = jnp.where(owned_rows, local_row, 0)
        picked = jnp.where(owned_rows[:, None], current[safe_rows], bf_zero)
        is_root = prow_here == root_row
        previous = current[diag_local : diag_local + panel]
        right_cols = col_global > panel_index
        displaced = broadcast(previous, "prow", root_row)
        gathered = lax.psum(picked, "prow").astype(jnp.float32)
        pivot_block = gathered.astype(jnp.bfloat16)
        product = jnp.dot(
            lower_inverse[panel_index], pivot_block, preferred_element_type=jnp.float32
        ).astype(jnp.bfloat16)
        new_row = jnp.where(right_cols[None, :], product, pivot_block)
        moved_rows = owned_rows & (pivot_list != panel_index * panel + offsets)
        targets = jnp.where(moved_rows, local_row, local_rows)
        current = current.at[targets].set(displaced, mode="drop")
        below_mask = row_global > panel_index
        panel_part = current[:, panel_local : panel_local + panel]
        upper_block = upper_inverse[panel_index]

        def factor(columns):
            result = jnp.dot(columns, upper_block, preferred_element_type=jnp.float32).astype(
                jnp.bfloat16
            )
            return jnp.where(below_mask[:, None], result, jnp.zeros((), jnp.bfloat16))

        def nothing(columns):
            return jnp.zeros((local_rows, panel), jnp.bfloat16)

        factors = lax.cond(pcol_here == root_col, factor, nothing, panel_part)
        factors = broadcast(factors, "pcol", root_col)
        update_rows = jnp.where(right_cols[None, :], new_row, bf_zero)
        correction = jnp.dot(factors, update_rows, preferred_element_type=jnp.float32)
        updated = (current.astype(jnp.float32) - correction).astype(jnp.bfloat16)
        owner_col = pcol_here == root_col
        new_panel = jnp.where(
            owner_col & below_mask[:, None], factors, updated[:, panel_local : panel_local + panel]
        )
        updated = updated.at[:, panel_local : panel_local + panel].set(new_panel)
        row_block = jnp.where(is_root, new_row, updated[diag_local : diag_local + panel])
        return updated.at[diag_local : diag_local + panel].set(row_block)

    current = lax.fori_loop(0, 2, one_panel, current)
    return current.reshape(matrix.shape)


def dot(a, b):
    return jnp.dot(a, b, preferred_element_type=jnp.float32)


def narrow(value):
    return value.astype(jnp.bfloat16)


def iota(shape, axis):
    return lax.broadcasted_iota(jnp.int32, shape, axis)


def total(mask_or_value, axis):
    return jnp.sum(mask_or_value, axis=axis, keepdims=True).astype(jnp.int32)


def pick(mask, value):
    return jnp.where(mask, value, 0).astype(jnp.float32)


def split_rows(row, panel):
    shift = panel.bit_length() - 1
    block = row >> shift
    return block & (N_HOMES - 1), ((block >> 5) << shift) + (row & (panel - 1))


def upright(row):
    tall = jnp.transpose(jnp.broadcast_to(row.astype(jnp.float32), (8, row.shape[1])))
    return tall[:, 0:1].astype(jnp.int32)


def place_of(step, order):
    result = jnp.zeros_like(step)
    for place, value in enumerate(order):
        result = jnp.where(step == value, place, result)
    return result


def deal_kernel(panel, pos_ref, across_ref, rows_ref, picks_ref, keep_ref, place_ref, flag_ref):
    here = pos_ref[0]
    y, z = here >> 3, here & 7
    first_r, second_r = across_ref[0:1, :], across_ref[1:2, :]
    first_c, second_c = upright(first_r), upright(second_r)
    square = (panel, panel)
    number_c, number_r = iota(square, 0), iota(square, 1)
    came_r = total(pick(first_c == second_r, number_c + 1), 0)
    came_c = total(pick(second_c == first_r, number_r + 1), 1)
    source_r = [first_r, jnp.where(came_r > 0, came_r - 1, second_r)]
    source_c = [first_c, jnp.where(came_c > 0, came_c - 1, second_c)]
    owners_r, locals_r = zip(*[split_rows(s, panel) for s in source_r])
    owners_c = [split_rows(s, panel)[0] for s in source_c]
    before = number_c < number_r
    slots, homes, entries = [], [], []
    for s in range(2):
        counts = total(
            pick((owners_c[s] == owners_r[s]) & before, 1025) + pick(owners_c[s] < owners_r[s], 1), 0
        )
        within, rank = counts >> 10, counts & 1023
        slot = within >> 5
        if s == 1:
            shared = total(pick(owners_c[0] == owners_r[1], 1), 0)
            slot = slot + ((shared + N_HOMES - 1) >> 5)
        slots.append(slot)
        homes.append(rank & (N_HOMES - 1))
        entries.append(rank >> 5)
    flag_ref[...] = jnp.maximum(slots[0], slots[1])
    deal = jnp.zeros((N_HOMES * PAIR_ROWS, 1), jnp.int32)
    position = iota((N_HOMES * PAIR_ROWS, panel), 0)
    per_home = panel // N_HOMES
    for s in range(2):
        at = jnp.where(owners_r[s] == here, homes[s] * PAIR_ROWS + slots[s], -1)
        deal = deal + total(pick(position == at, locals_r[s]), 1)
        kept_at = jnp.where(homes[s] == here, entries[s], -1)
        keep_ref[s * per_home : (s + 1) * per_home, :] = total(
            pick(iota((per_home, panel), 0) == kept_at, owners_r[s] * PAIR_ROWS + slots[s]), 1
        )
        z_place = place_of((homes[s] - z) & (NZ - 1), Z_ORDER)
        y_place = place_of(((homes[s] >> 3) - y) & (NY - 1), Y_ORDER)
        place_ref[s : s + 1, :] = (y_place * NZ + z_place) * per_home + entries[s]
    n_rows = rows_ref.shape[0]
    choose = jnp.where(iota((N_HOMES * PAIR_ROWS, n_rows), 1) == deal, 1.0, 0.0)
    picks_ref[...] = narrow(dot(narrow(choose), rows_ref[...]))


def leave_kernel(
    panel,
    pos_ref,
    across_ref,
    rows_ref,
    place_ref,
    lower_ref,
    slots_ref,
    leave0_ref,
    leave1_ref,
    leave2_ref,
    leave3_ref,
    passing_ref,
    land_ref,
    flag_ref,
    low_ref,
):
    here = pos_ref[0]
    y, z = here >> 3, here & 7
    odd = (here & 1) == 1
    first_r, second_r = across_ref[0:1, :], across_ref[1:2, :]
    first_c, second_c = upright(first_r), upright(second_r)
    square = (panel, panel)
    number_c, number_r = iota(square, 0), iota(square, 1)
    big = 1 << 20
    seen_r = total(pick(second_c == first_r, big) + pick(number_c + panel == first_r, second_c), 0)
    seen_c = total(pick(first_c == second_r, big) + pick(first_c == number_r + panel, second_r), 1)
    used_r = total(pick(first_c == number_r + panel, 1), 0)
    used_c = total(pick(number_c + panel == first_r, 1), 1)

    def goals(first, second, seen, used, number):
        inner = (first >= panel) & (first < 2 * panel)
        stop = seen & (big - 1)
        goal_first = jnp.where(
            inner,
            jnp.where(stop == first, -1, stop),
            jnp.where((first == number) | (seen >= big), -1, first),
        )
        goal_second = jnp.where((used > 0) | (second == number + panel), -1, second)
        return goal_first, goal_second

    goal_r = goals(first_r, second_r, seen_r, used_r, number_r[0:1, :])
    goal_c = goals(first_c, second_c, seen_c, used_c, number_c[:, 0:1])
    before = number_c < number_r
    lines, line_ranks, dests, dest_ranks, landing = [], [], [], [], []
    worst = jnp.zeros((1, panel), jnp.int32)
    for s in range(2):
        dest_r, local_r = split_rows(goal_r[s], panel)
        dest_r = jnp.where(goal_r[s] < 0, -1, dest_r)
        dest_c = jnp.where(goal_c[s] < 0, -1, split_rows(goal_c[s], panel)[0])
        line_r, line_c = dest_r >> 3, dest_c >> 3
        counts = total(
            pick((dest_c == dest_r) & before, 1024) + pick((line_c == line_r) & before, 1), 0
        )
        line_rank, dest_rank = counts & 1023, counts >> 10
        worst = jnp.maximum(
            worst,
            jnp.where(
                (dest_r >= 0) & ((line_rank >= LINE_ROWS) | (dest_rank >= DEST_ROWS)), 1, 0
            ),
        )
        land_at = jnp.where(dest_r == here, dest_rank, -1)
        landing.append(total(pick(iota((DEST_ROWS, panel), 0) == land_at, local_r + 1), 1) - 1)
        lines.append(line_r)
        line_ranks.append(line_rank)
        dests.append(dest_r)
        dest_ranks.append(dest_rank)
    worst = jnp.maximum(worst, jnp.where(slots_ref[...] >= PAIR_ROWS, 1, 0))
    flag_ref[0] = jnp.max(worst.astype(jnp.float32)).astype(jnp.int32)
    landing = jnp.concatenate(landing).astype(jnp.float32)
    landing = jnp.transpose(jnp.broadcast_to(landing, (2 * DEST_ROWS, 128)))
    land_ref[...] = landing[0:1, :].astype(jnp.int32)
    line = jnp.where(odd, lines[1], lines[0])
    line_rank = jnp.where(odd, line_ranks[1], line_ranks[0])
    dest = jnp.where(odd, dests[1], dests[0])
    dest_rank = jnp.where(odd, dest_ranks[1], dest_ranks[0])
    send_at = jnp.where(line < 0, -1, line * LINE_ROWS + line_rank)
    choose = jnp.where(iota((NY * LINE_ROWS, panel), 0) == send_at, 1.0, 0.0)
    leaving = narrow(dot(narrow(choose), rows_ref[:panel, :]))
    for k, ref in enumerate((leave0_ref, leave1_ref, leave2_ref, leave3_ref)):
        ref[...] = leaving[k * LINE_ROWS : (k + 1) * LINE_ROWS]
    pass_at = jnp.where(line == y, ((dest - z) & (NZ - 1)) * DEST_ROWS + dest_rank, -1)
    passing_ref[...] = total(
        pick(iota((NZ * DEST_ROWS, panel), 0) == pass_at, line_rank), 1
    )
    for s in range(2):
        order = narrow(jnp.where(number_c == place_ref[s : s + 1, :], 1.0, 0.0))
        low_ref[s] = narrow(
            lax.dot_general(
                lower_ref[s], order, (((1,), (1,)), ((), ())), preferred_element_type=jnp.float32
            )
        )


def block_kernel(keep_ref, dealt_ref, block_ref):
    n = dealt_ref.shape[0]
    choose = jnp.where(keep_ref[...] == iota((keep_ref.shape[0], n), 1), 1.0, 0.0)
    block_ref[...] = narrow(dot(narrow(choose), dealt_ref[...]))


def pair_kernel(block_ref, lo_ref, hi_ref, pair_lo_ref, pair_hi_ref):
    n = block_ref.shape[0]
    pair_lo_ref[:n, :] = block_ref[...]
    pair_lo_ref[n:, :] = lo_ref[...]
    pair_hi_ref[:n, :] = block_ref[...]
    pair_hi_ref[n:, :] = hi_ref[...]


def line_kernel(
    pos_ref, block_ref, lo_ref, hi_ref, opposite_ref, two_lo_ref, two_hi_ref, line_ref, extra_ref
):
    n = block_ref.shape[0]
    half = n // 2
    blocks = [block_ref[...], lo_ref[...], hi_ref[...], opposite_ref[...]]
    blocks += [two_lo_ref[:n, :], two_lo_ref[n:, :], two_hi_ref[:n, :], two_hi_ref[n:, :]]
    for k, value in enumerate(blocks):
        line_ref[k * half : (k + 1) * half, :] = value[:half]
        line_ref[(NZ + k) * half : (NZ + k + 1) * half, :] = value[half:]
    even = (pos_ref[1] & 1) == 0
    n, width = extra_ref.shape
    extra_ref[...] = jnp.where(even, line_ref[n:, :width], line_ref[:n, :width])


def by_x(x, at_0, at_1, at_2, at_3):
    return jnp.where(x <= 1, jnp.where(x == 0, at_0, at_1), jnp.where(x == 2, at_2, at_3))


def choose_kernel(pos_ref, own_ref, one_ref, two_ref, three_ref, out_ref):
    x = pos_ref[1] >> 1
    for place, ref in enumerate((own_ref, one_ref, two_ref, three_ref)):

        @pl.when(x == place)
        def _(ref=ref):
            out_ref[...] = ref[...]


def spread_kernel(pos_ref, passing_ref, own_ref, one_ref, two_ref, three_ref, keep_ref, send_ref):
    y = pos_ref[0] >> 3
    on_line = by_x(y, own_ref[...], one_ref[...], two_ref[...], three_ref[...])
    n_rows = passing_ref.shape[0]
    choose = jnp.where(passing_ref[...] == iota((n_rows, LINE_ROWS), 1), 1.0, 0.0)
    spread = narrow(dot(narrow(choose), on_line))
    keep_ref[...] = spread[: n_rows // 2]
    send_ref[...] = spread[n_rows // 2 :]


def fold_kernel(bit, pos_ref, kept_ref, came_ref, keep_ref, send_ref):
    n = keep_ref.shape[0]

    @pl.when((pos_ref[0] & bit) == 0)
    def _():
        keep_ref[...] = kept_ref[:n, :]
        send_ref[...] = kept_ref[n:, :]

    @pl.when((pos_ref[0] & bit) != 0)
    def _():
        keep_ref[...] = came_ref[:n, :]
        send_ref[...] = came_ref[n:, :]


def gone_kernel(pos_ref, kept_ref, came_ref, gone_ref, gone_panel_ref):
    n, width = kept_ref.shape[0], gone_panel_ref.shape[1]
    even = (pos_ref[0] & 1) == 0
    kept, came = kept_ref[...], came_ref[...]
    gone_ref[:n, :] = jnp.where(even, kept, came)
    gone_ref[n:, :] = jnp.where(even, came, kept)
    gone_panel_ref[...] = gone_ref[:, :width]


def settle(land_ref, begin, value, gone):
    n = value.shape[0]
    hits = (iota((n, 2 * DEST_ROWS), 0) + begin) == land_ref[...]
    marks = jnp.where(hits, 1.0, 0.0)
    hit = jnp.sum(marks, axis=1, keepdims=True) > 0.5
    return jnp.where(hit, dot(narrow(marks), gone), value.astype(jnp.float32))


def settle_kernel(rows_ref, land_ref, gone_ref, out_ref):
    begin = pl.program_id(0) * rows_ref.shape[0]
    out_ref[...] = narrow(settle(land_ref, begin, rows_ref[...], gone_ref[...]))


def factor_kernel(pos_ref, part_ref, other_ref, upper_ref, out_ref):
    even = (pos_ref[1] & 1) == 0
    out_ref[...] = narrow(
        dot(jnp.where(even, part_ref[...], other_ref[...]), upper_ref[0])
    )


def pass_kernel(pos_ref, own_ref, came_ref, out_ref):
    out_ref[...] = jnp.where((pos_ref[1] >> 1) == 2, came_ref[...], own_ref[...])


def even_odd(pos_ref, even_ref, odd_ref):
    return jnp.where(((pos_ref[1] >> 1) & 1) == 0, even_ref[...], odd_ref[...])


def extra_kernel(pos_ref, even_ref, odd_ref, cross_ref):
    cross_ref[...] = even_odd(pos_ref, even_ref, odd_ref)


def two_kernel(own_ref, came_ref, out_ref):
    n = own_ref.shape[0]
    out_ref[:n, :] = own_ref[...]
    out_ref[n:, :] = came_ref[...]


def part_kernel(pos_ref, mine_ref, before_ref, after_ref, across_ref, part_ref):
    x = pos_ref[1] >> 1
    n = mine_ref.shape[0]
    for step, ref in ((0, mine_ref), (-1, before_ref), (1, after_ref), (2, across_ref)):
        begin = ((x + step) & (NX - 1)) * n
        part_ref[pl.ds(pl.multiple_of(begin, n), n), :] = ref[...]


def cross_kernel(pos_ref, near_ref, far_ref, even_ref, odd_ref, cross_ref):
    y = pos_ref[0] >> 3
    n = near_ref.shape[0] // 2
    for k in range(NY):
        source = near_ref if k < 2 else far_ref
        place = place_of(((y ^ k) - y) & (NY - 1), Y_ORDER)
        cross_ref[pl.ds(pl.multiple_of(place * n, n), n), :] = source[
            (k & 1) * n : ((k & 1) + 1) * n, :
        ]
    cross_ref[NY * n :, :] = even_odd(pos_ref, even_ref, odd_ref)


def first_kernel(
    low_ref, y0_ref, y1_ref, y2_ref, far_first_ref, far_second_ref, row_ref, second_ref, a00_ref
):
    quarter = far_first_ref.shape[0]
    y_refs = (y0_ref, y1_ref, y2_ref)
    pivot_first = jnp.concatenate([r[:quarter, :] for r in y_refs] + [far_first_ref[...]])
    row_ref[...] = narrow(dot(low_ref[0], pivot_first))
    a00_ref[...] = pivot_first[:, : a00_ref.shape[1]]
    for k, ref in enumerate(y_refs):
        second_ref[k * quarter : (k + 1) * quarter, :] = ref[quarter:, :]
    second_ref[3 * quarter :, :] = far_second_ref[...]


def finish_kernel(
    panel,
    pos_ref,
    rows_ref,
    part_ref,
    other_ref,
    factor_ref,
    land_ref,
    cross_ref,
    cross_other_ref,
    row_first_ref,
    second_ref,
    a00_ref,
    low_ref,
    upper_ref,
    place_ref,
    out_ref,
    new_ref,
    corner_ref,
    gone_first_ref,
    gone_second_ref,
    top_ref,
):
    step = pl.program_id(0)
    here, column = pos_ref[0], pos_ref[1]
    even = (column & 1) == 0
    width = panel
    bf16 = jnp.bfloat16

    @pl.when(step == 0)
    def _():
        mine, others = cross_ref[...], cross_other_ref[...]
        from_first = jnp.where(even, mine, others)
        from_second = jnp.where(even, others, mine)
        gone_first_ref[...] = narrow(dot(from_first[panel:], upper_ref[0]))
        gone_second_ref[...] = from_second[panel:]
        row_first = row_first_ref[...]
        pivot_second = second_ref[...]
        corner_ref[...] = narrow(dot(low_ref[0], from_second[:panel]))
        lower_factor = narrow(dot(from_first[:panel], upper_ref[0]))
        reduced = narrow(pivot_second.astype(jnp.float32) - dot(lower_factor, row_first))
        row_second = narrow(dot(low_ref[1], reduced))
        new_ref[:panel, :] = row_first
        new_ref[panel:, :] = row_second

        @pl.when(here <= 1)
        def _():
            top_ref[...] = jnp.where(here == 0, row_first, row_second)

        @pl.when((here <= 1) & (column <= 1) & (here >= column))
        def _():
            raw = jnp.where(
                here == 0,
                a00_ref[...],
                jnp.where(column == 0, lower_factor, reduced[:, :width]),
            )
            place = jnp.where(here == 0, place_ref[0:1, :], place_ref[1:2, :])
            order = narrow(jnp.where(iota((panel, panel), 0) == place, 1.0, 0.0))
            top_ref[:, :width] = narrow(
                lax.dot_general(
                    order, raw, (((0,), (0,)), ((), ())), preferred_element_type=jnp.float32
                )
            )

    @pl.when(step > 0)
    def _():
        n = rows_ref.shape[0]
        begin = (step - 1) * n
        second = jnp.where(even, other_ref[...], part_ref[...])
        factor_first = narrow(settle(land_ref, begin, factor_ref[...], gone_first_ref[...]))
        panel_second = settle(land_ref, begin, second, gone_second_ref[...])
        mid = narrow(panel_second - dot(factor_first, corner_ref[...]))
        factor_second = narrow(dot(mid, upper_ref[1]))
        current = rows_ref[...].astype(jnp.float32)
        updated = narrow(
            current
            - dot(factor_first, new_ref[:panel, :])
            - dot(factor_second, new_ref[panel:, :])
        )
        out_ref[...] = updated

        @pl.when(column <= 1)
        def _():
            out_ref[:, :width] = jnp.where(column == 0, factor_first, factor_second)

        @pl.when((here <= 1) & (begin < panel))
        def _():
            out_ref[...] = top_ref[pl.ds(pl.multiple_of(begin, n), n), :]


def whole(shape):
    return pl.BlockSpec(shape, lambda *_: (0,) * len(shape))


def smem():
    return pl.BlockSpec(memory_space=pltpu.SMEM)


def shape(dims, dtype=jnp.bfloat16):
    return jax.ShapeDtypeStruct(dims, dtype)


def local_kernel(body, name, outs, scalars, *arrays, limit=12):
    return pl.pallas_call(
        body,
        grid=(1,),
        in_specs=[smem() for _ in scalars] + [whole(v.shape) for v in arrays],
        out_specs=[smem() if o.shape == (1,) else whole(o.shape) for o in outs],
        out_shape=outs,
        compiler_params=pltpu.CompilerParams(vmem_limit_bytes=limit * MIB),
        cost_estimate=pl.CostEstimate(flops=0, bytes_accessed=0, transcendentals=0),
        name=name,
    )(*scalars, *arrays)


def after(values, *others):
    return lax.optimization_barrier((values, others))[0]


def per_device(matrix, pivots, lower_inverse, upper_inverse):
    row_blocks, panel, col_blocks, width = matrix.shape
    local_rows, local_cols = row_blocks * panel, col_blocks * width
    here = lax.axis_index("prow")
    column = lax.axis_index("pcol")
    position = jnp.stack([here, column]).astype(jnp.int32)
    rows = matrix.reshape(local_rows, local_cols)
    per_home = panel // N_HOMES
    i32 = jnp.int32

    picks, keep, place, slots = local_kernel(
        functools.partial(deal_kernel, panel),
        "deal",
        [
            pltpu.HBM((N_HOMES * PAIR_ROWS, local_cols), jnp.bfloat16),
            pltpu.HBM((2 * per_home, 1), i32),
            shape((2, panel), i32),
            shape((1, panel), i32),
        ],
        [position],
        pivots,
        rows,
        limit=32,
    )
    dealt = lax.all_to_all(picks, "prow", 0, 0, tiled=True)

    quarter = local_rows // NX
    own = [rows[k * quarter : (k + 1) * quarter, :width] for k in range(NX)]
    got = [lax.ppermute(own[k], "pcol", move_x([(0, k)])) for k in range(1, NX)]
    (mine,) = local_kernel(
        choose_kernel, "choose", [shape((quarter, width))], [position], own[0], *got
    )

    line_shape = shape((LINE_ROWS, local_cols))
    *leaving, passing, land, flag, low = local_kernel(
        functools.partial(leave_kernel, panel),
        "leave",
        [line_shape]
        + [pltpu.HBM(line_shape.shape, line_shape.dtype)] * (NY - 1)
        + [
            shape((NZ * DEST_ROWS, 1), i32),
            shape((1, 2 * DEST_ROWS), i32),
            shape((1,), i32),
            shape((2, panel, panel)),
        ],
        [position],
        pivots,
        rows,
        place,
        lower_inverse,
        slots,
        limit=32,
    )

    (block,) = local_kernel(
        block_kernel, "block", [shape((2 * per_home, local_cols))], [], keep, after(dealt, passing)
    )
    from_lo = lax.ppermute(block, "prow", shift_z(1))
    from_hi = lax.ppermute(block, "prow", shift_z(-1))
    opposite = lax.ppermute(block, "prow", shift_z(4))
    arrived = [lax.ppermute(leaving[s], "prow", shift_y(s, [0], [0, 1])) for s in (1, 2, 3)]
    quarter_shape = shape((NZ // 2 * DEST_ROWS, local_cols))
    kept, send = local_kernel(
        spread_kernel,
        "spread",
        [quarter_shape] * 2,
        [position],
        after(passing, block),
        leaving[0],
        *arrived,
    )
    came = lax.ppermute(send, "prow", shift_z(4, [0, 1]))

    from_lo, from_hi = after((from_lo, from_hi), mine)
    pair_shape = shape((4 * per_home, local_cols))
    pair_lo, pair_hi = local_kernel(
        pair_kernel, "pair", [pair_shape] * 2, [], block, from_lo, from_hi
    )
    two_lo = lax.ppermute(pair_lo, "prow", shift_z(2))
    two_hi = lax.ppermute(pair_hi, "prow", shift_z(-2))
    quarter_out = after(mine, pair_lo)
    ring = [(x, (x + 1) % NX) for x in range(NX)]
    before = lax.ppermute(quarter_out, "pcol", move_x(ring))
    behind = lax.ppermute(quarter_out, "pcol", move_x([(b, a) for a, b in ring]))

    two_lo, two_hi, opposite = after((two_lo, two_hi, opposite), before, behind, kept)
    half = panel // NY
    n_gone = 2 * DEST_ROWS
    z_line, extra = local_kernel(
        line_kernel,
        "line",
        [shape((2 * half, local_cols)), shape((half, width))],
        [position],
        block,
        from_lo,
        from_hi,
        opposite,
        two_lo,
        two_hi,
    )
    y_lo = lax.ppermute(z_line, "prow", shift_y(1))
    y_hi = lax.ppermute(z_line, "prow", shift_y(-1))
    extra_mid = lax.ppermute(extra, "pcol", move_x([(0, 2)]))
    extra_shape = shape((half, width))
    (extra,) = local_kernel(
        pass_kernel, "pass", [extra_shape], [position], extra, extra_mid
    )
    extra_odd = lax.ppermute(extra, "pcol", move_x([(0, 1), (2, 3)]))
    kept, send = local_kernel(
        functools.partial(fold_kernel, 4),
        "fold4",
        [shape((2 * DEST_ROWS, local_cols))] * 2,
        [position],
        kept,
        after(came, z_line),
    )
    came = lax.ppermute(send, "prow", shift_z(2, [0, 1, 4, 5]))
    kept, send = local_kernel(
        functools.partial(fold_kernel, 2),
        "fold2",
        [shape((DEST_ROWS, local_cols))] * 2,
        [position],
        kept,
        came,
    )
    came = lax.ppermute(send, "prow", shift_z(1))
    across = lax.ppermute(
        after(mine, z_line), "pcol", move_x([(x, (x + 2) % NX) for x in range(NX)])
    )

    y_lo, y_hi = after((y_lo, y_hi), extra_odd, across, came)
    far_first = lax.ppermute(y_lo[:half], "prow", shift_y(1))
    far_second = lax.ppermute(y_hi[half:], "prow", shift_y(-1))
    (near,) = local_kernel(
        extra_kernel, "extra", [extra_shape], [position], extra, extra_odd
    )
    near_other = lax.ppermute(near, "prow", cross_y(1))
    gone_shape = shape((n_gone, width))
    gone, gone_panel = local_kernel(
        gone_kernel,
        "gone",
        [shape((n_gone, local_cols)), gone_shape],
        [position],
        *after((kept, came), y_lo),
    )
    gone_mid = lax.ppermute(gone_panel, "pcol", move_x([(0, 2)]))
    (near,) = local_kernel(
        two_kernel,
        "two",
        [shape((2 * half, width))],
        [],
        near,
        after(near_other, far_first, far_second, gone_mid),
    )
    far = lax.ppermute(near, "prow", cross_y(2))
    (gone_panel,) = local_kernel(
        pass_kernel, "pass2", [gone_shape], [position], gone_panel, gone_mid
    )
    gone_odd = lax.ppermute(gone_panel, "pcol", move_x([(0, 1), (2, 3)]))
    (part,) = local_kernel(
        part_kernel,
        "part",
        [shape((local_rows, width))],
        [position],
        mine,
        before,
        behind,
        after(across, y_lo),
    )
    other = lax.ppermute(part, "pcol", SWAP)
    n_block = panel // 2
    steps = local_rows // n_block

    def block_of(cols, lead=0):
        return pl.BlockSpec((n_block, cols), lambda i: (jnp.maximum(i - lead, 0), 0))

    settled = pl.pallas_call(
        settle_kernel,
        grid=(steps,),
        in_specs=[block_of(local_cols), whole((1, n_gone)), whole((n_gone, local_cols))],
        out_specs=block_of(local_cols),
        out_shape=shape((local_rows, local_cols)),
        compiler_params=pltpu.CompilerParams(vmem_limit_bytes=16 * MIB),
        cost_estimate=pl.CostEstimate(flops=0, bytes_accessed=0, transcendentals=0),
        name="settle",
    )(rows, land, gone)
    factor_raw = pl.pallas_call(
        factor_kernel,
        grid=(steps,),
        in_specs=[smem(), block_of(width), block_of(width), whole((2, panel, panel))],
        out_specs=block_of(width),
        out_shape=shape((local_rows, width)),
        compiler_params=pltpu.CompilerParams(vmem_limit_bytes=16 * MIB),
        cost_estimate=pl.CostEstimate(flops=0, bytes_accessed=0, transcendentals=0),
        name="factor",
    )(position, part, other, upper_inverse)

    far = after(far, far_first, far_second, factor_raw, settled)
    (cross,) = local_kernel(
        cross_kernel,
        "cross",
        [shape((panel + n_gone, width))],
        [position],
        near,
        far,
        gone_panel,
        gone_odd,
    )
    cross_other = lax.ppermute(cross, "pcol", SWAP)
    row_first, second, a00 = pl.pallas_call(
        first_kernel,
        grid=(1,),
        in_specs=[whole((2, panel, panel))]
        + [whole((2 * half, local_cols))] * 3
        + [whole((half, local_cols))] * 2,
        out_specs=[whole((panel, local_cols))] * 2 + [whole((panel, width))],
        out_shape=[shape((panel, local_cols))] * 2 + [shape((panel, width))],
        compiler_params=pltpu.CompilerParams(vmem_limit_bytes=40 * MIB),
        cost_estimate=pl.CostEstimate(
            flops=2 * panel * panel * local_cols, bytes_accessed=8 * MIB, transcendentals=0
        ),
        name="first",
    )(low, z_line, y_lo, y_hi, far_first, far_second)

    result = pl.pallas_call(
        functools.partial(finish_kernel, panel),
        grid=(steps + 1,),
        in_specs=[
            smem(),
            block_of(local_cols, 1),
            block_of(width, 1),
            block_of(width, 1),
            block_of(width, 1),
            whole((1, 2 * DEST_ROWS)),
            whole((panel + 2 * DEST_ROWS, width)),
            whole((panel + 2 * DEST_ROWS, width)),
            whole((panel, local_cols)),
            whole((panel, local_cols)),
            whole((panel, width)),
            whole((2, panel, panel)),
            whole((2, panel, panel)),
            whole((2, panel)),
        ],
        out_specs=block_of(local_cols, 1),
        out_shape=shape((local_rows, local_cols)),
        scratch_shapes=[
            pltpu.VMEM((2 * panel, local_cols), jnp.bfloat16),
            pltpu.VMEM((panel, width), jnp.bfloat16),
            pltpu.VMEM((2 * DEST_ROWS, width), jnp.bfloat16),
            pltpu.VMEM((2 * DEST_ROWS, width), jnp.bfloat16),
            pltpu.VMEM((panel, local_cols), jnp.bfloat16),
        ],
        compiler_params=pltpu.CompilerParams(vmem_limit_bytes=32 * MIB),
        name="finish",
    )(position, settled, part, other, factor_raw, land, cross, cross_other, row_first, second, a00, low, upper_inverse, place)
    result = result.reshape(matrix.shape)

    def general(state):
        return 0, general_steps(matrix, pivots, lower_inverse, upper_inverse)

    return lax.while_loop(lambda state: state[0] > 0, general, (flag[0], result))[1]


def solution(mesh):
    return jax.shard_map(
        per_device,
        mesh=mesh,
        in_specs=(P(None, "prow", None, "pcol"), P(), P(), P()),
        out_specs=P(None, "prow", None, "pcol"),
        check_vma=False,
    )
```
